32 devices in a mesh: section: 2 (over core), ctx: 4 (over z), dp: 4 (over y, x).
Axes of the slice: x: 2, y: 2, z: 4, core: 2. Of those that a mesh axis runs over, the one named last changes fastest.
Arguments:
- tokens: bfloat16 [8, 1024, 768], P('dp', 'ctx'), may hold values from -6 to 6
- seg_ids: int32 [8, 1024], P('dp'), may hold values from 0 to 15, as said below
- query_key_value_weight: bfloat16 [2, 768, 2304], P('section', 'dp'), may hold values from -0.21875 to 0.21875
- output_weight: bfloat16 [2, 768, 768], P('section', 'dp'), may hold values from -1.75 to 1.75
- gate_weight: bfloat16 [2, 768, 3072], P('section', 'dp'), may hold values from -0.21875 to 0.21875
- up_weight: bfloat16 [2, 768, 3072], P('section', 'dp'), may hold values from -0.21875 to 0.21875
- down_weight: bfloat16 [2, 3072, 768], P('section', 'dp'), may hold values from -0.109375 to 0.109375
- norm1_gain: bfloat16 [2, 768], P('section', 'dp'), may hold values from 0.5 to 1.5
- norm1_bias: bfloat16 [2, 768], P('section', 'dp'), may hold values from -1.5 to 1.5
- norm2_gain: bfloat16 [2, 768], P('section', 'dp'), may hold values from 0.5 to 1.5
- norm2_bias: bfloat16 [2, 768], P('section', 'dp'), may hold values from -1.5 to 1.5
- cotangent: bfloat16 [8, 1024, 768], P('dp', 'ctx'), may hold values from -6 to 6
Outputs:
- section_outputs: bfloat16 [2, 8, 1024, 768], P('section', 'dp', 'ctx')
- input_grads: float32 [2, 8, 1024, 768], P('section', 'dp', 'ctx')
- grad_qkv: float32 [2, 768, 2304], P('section', 'dp')
- grad_out: float32 [2, 768, 768], P('section', 'dp')
- grad_gate: float32 [2, 768, 3072], P('section', 'dp')
- grad_up: float32 [2, 768, 3072], P('section', 'dp')
- grad_down: float32 [2, 3072, 768], P('section', 'dp')
- grad_norm1_gain: float32 [2, 768], P('section', 'dp')
- grad_norm1_bias: float32 [2, 768], P('section', 'dp')
- grad_norm2_gain: float32 [2, 768], P('section', 'dp')
- grad_norm2_bias: float32 [2, 768], P('section', 'dp')
The draws below stay inside these ranges and needn't reach their ends.
Inputs may be any that keep to these rules, and one draw needn't show every extreme that they name: `seg_ids`: in each sequence the ids start at 0 and rise by one where a document starts; documents hold 64 to 512 tokens, the last one cut by the sequence's end; of the 2 sequences of each index of dp, one is a single document, and in every draw one sequence is cut into 16 documents of 64 tokens.
All inputs are finite; a program needn't handle non-finite values.
Results may differ from the reference program's by a relative error of at most 0.022.
Values may be sent and summed in bfloat16 or wider, within the bound.
No kernel may reach another device: no remote copies, remote signals or barrier semaphores. Data moves between devices by JAX's collectives and lax.ppermute only.
A program may use at most 320 MiB of HBM per device.

```python
import jax
import jax.numpy as jnp
from jax import lax

D = 768
HEADS = 12
HEAD = 64
FF = 3072
SEQ_DP = 2
SEQ = 1024
SEQS = 8
BLOCK = 512
N_DP = 4


def draw_seg_ids(key, part):
    key = jax.random.fold_in(key, 7)
    key_len = jax.random.fold_in(key, 1)
    key_whole = jax.random.fold_in(key, 2)
    key_even = jax.random.fold_in(key, 3)
    shortest = max(SEQ // 16, 1)
    longest = SEQ // 2 + 1
    doc_count = SEQ // shortest + 2
    lengths = jax.random.randint(key_len, (SEQS, doc_count), shortest, longest)
    whole = jax.random.randint(key_whole, (N_DP,), 0, SEQ_DP)
    offset = jax.random.randint(key_even, (), 1, SEQ_DP)
    even_row = (whole[0] + offset) % SEQ_DP
    rows = jnp.arange(SEQS, dtype=jnp.int32)
    lengths = jnp.where((rows == even_row)[:, None], shortest, lengths)
    ends = jnp.cumsum(lengths, axis=1)
    places = jnp.arange(SEQ, dtype=jnp.int32)
    ids = jnp.sum((ends[:, None, :] <= places[None, :, None]).astype(jnp.int32), axis=2)
    single = rows % SEQ_DP == whole[rows // SEQ_DP]
    return jnp.where(single[:, None], 0, ids).astype(jnp.int32)


def shard_levels(stream_key, extent, pieces, least, largest):
    factor_of = 1.0
    for dim, shards_of in pieces:
        steps = jax.random.uniform(jax.random.fold_in(jax.random.fold_in(stream_key, 6), dim), (shards_of,), jnp.float32, least / len(pieces), largest / len(pieces))
        factor_of = factor_of * jnp.repeat(jnp.exp(steps), extent[dim] // shards_of).reshape((-1,) + (1,) * (len(extent) - 1 - dim))
    return factor_of


def scatter_about(own_key, dims, scale, most, cuts=(), kind=jnp.bfloat16):
    values = jax.random.normal(own_key, dims, jnp.float32) * scale
    if len(cuts) > 0:
        values = shard_levels(own_key, dims, cuts, -0.22, 0.18) * values
    return jnp.clip(values, min=-most, max=most).astype(kind)


def setup_inputs(seed: int = 0) -> dict:
    seeds = jax.random.split(jax.random.key(seed), 13)
    tokens = scatter_about(seeds[0], (SEQS, SEQ, D), 1.0, 6.0, ((0, 4), (1, 4)))
    seg_ids = draw_seg_ids(jax.random.fold_in(seeds[12], 71), 0)
    query_key_value_weight = scatter_about(seeds[2], (2, D, 3 * D), D ** -0.5, 0.21875, ((0, 2), (1, 4)))
    output_weight = scatter_about(seeds[3], (2, D, D), (max(1, D * 16 // SEQ)) ** -0.5, 1.75, ((0, 2), (1, 4)))
    gate_weight = scatter_about(seeds[4], (2, D, FF), D ** -0.5, 0.21875, ((0, 2), (1, 4)))
    up_weight = scatter_about(seeds[5], (2, D, FF), D ** -0.5, 0.21875, ((0, 2), (1, 4)))
    down_weight = scatter_about(seeds[6], (2, FF, D), FF ** -0.5, 0.109375, ((0, 2), (1, 4)))
    norm1_gain = jnp.clip(1.0 + 0.1 * jax.random.normal(seeds[7], (2, D), jnp.float32), 0.5, 1.5).astype(jnp.bfloat16)
    norm1_bias = scatter_about(seeds[8], (2, D), 0.3, 1.5, ((0, 2), (1, 4)))
    norm2_gain = jnp.clip(1.0 + 0.1 * jax.random.normal(seeds[9], (2, D), jnp.float32), 0.5, 1.5).astype(jnp.bfloat16)
    norm2_bias = scatter_about(seeds[10], (2, D), 0.3, 1.5, ((0, 2), (1, 4)))
    cotangent = scatter_about(seeds[11], (SEQS, SEQ, D), 1.0, 6.0, ((0, 4), (1, 4)))
    return dict(tokens=tokens, seg_ids=seg_ids, query_key_value_weight=query_key_value_weight, output_weight=output_weight, gate_weight=gate_weight, up_weight=up_weight, down_weight=down_weight, norm1_gain=norm1_gain, norm1_bias=norm1_bias, norm2_gain=norm2_gain, norm2_bias=norm2_bias, cotangent=cotangent)


EPS = 1e-05
HIGHEST_PRECISE = lax.Precision.HIGHEST
NEG = -1e+30

@jax.custom_vjp
def low(v):
    return lax.optimization_barrier(v.astype(jnp.bfloat16)).astype(jnp.float32)

@jax.custom_vjp
def lowered_backward(v):
    return v

def low_keep(v):
    return (low(v), None)

def low_pass(kept, grad):
    return (grad,)

def back_keep(v):
    return (v, None)

def back_low(kept, grad):
    return (low(grad),)
low.defvjp(low_keep, low_pass)
lowered_backward.defvjp(back_keep, back_low)

def positions(seg_ids):
    places = lax.broadcasted_iota(jnp.int32, seg_ids.shape, 1)
    begins = jnp.concatenate([jnp.ones_like(seg_ids[:, :1]), (seg_ids[:, 1:] != seg_ids[:, :-1]).astype(jnp.int32)], axis=1)
    return places - lax.cummax(places * begins, axis=1)

def rope_tables(places, half_dim):
    spread = 1000.0 ** (-2.0 * jnp.arange(half_dim, dtype=jnp.float32) / (2 * half_dim))
    angles = places.astype(jnp.float32)[..., None] * spread
    return (jnp.cos(angles), jnp.sin(angles))

def rotate(values, cosine, sine_table):
    half_dim = values.shape[-1] // 2
    former, latter = (values[..., :half_dim], values[..., half_dim:])
    cosine, sine_table = (cosine[..., None, :], sine_table[..., None, :])
    return jnp.concatenate([former * cosine - latter * sine_table, latter * cosine + former * sine_table], axis=-1)

def layer_norm(resid, gain, bias):
    centred = resid - lax.optimization_barrier(jnp.mean(resid, axis=-1, keepdims=True))
    spread = lax.optimization_barrier(jnp.mean(centred * centred, axis=-1, keepdims=True))
    return centred * lax.rsqrt(spread + EPS) * gain + bias

def attention(queries, key_rows, value_rows, seg_ids):

    def one_sequence(operands):
        seq_queries, seq_keys, seq_values, segment = operands

        def one_block(block):
            row_block, row_seg = block
            scores = lowered_backward(jnp.einsum('qhd,khd->hqk', row_block, seq_keys, precision=HIGHEST_PRECISE) * HEAD ** (-0.5))
            scores = jnp.where((row_seg[:, None] == segment[None, :])[None], scores, NEG)
            row_max = lax.optimization_barrier(jnp.max(scores, axis=-1, keepdims=True))
            exponent = jnp.exp(scores - row_max)
            probs = low(exponent / lax.optimization_barrier(jnp.sum(exponent, axis=-1, keepdims=True)))
            return jnp.einsum('hqk,khd->qhd', probs, seq_values, precision=HIGHEST_PRECISE)
        blocks = lax.map(jax.checkpoint(one_block), (seq_queries.reshape((SEQ // BLOCK, BLOCK) + seq_queries.shape[1:]), segment.reshape(SEQ // BLOCK, BLOCK)))
        return blocks.reshape(seq_queries.shape)
    return lax.map(one_sequence, (queries, key_rows, value_rows, seg_ids))

def layer(hidden_state, params, seg_ids, cosine, sine_table):
    query_key_value_weight, output_weight, gate_weight, up_weight, down_weight, gain_one, bias_one, gain_two, bias_two = params
    shaped = hidden_state.shape[:2] + (HEADS, HEAD)
    mixed_query_key_value = lowered_backward(jnp.einsum('yrp,po->yro', hidden_state, query_key_value_weight, precision=HIGHEST_PRECISE))
    queries = low(rotate(mixed_query_key_value[..., :D].reshape(shaped), cosine, sine_table))
    key_rows = low(rotate(mixed_query_key_value[..., D:2 * D].reshape(shaped), cosine, sine_table))
    value_rows = low(mixed_query_key_value[..., 2 * D:].reshape(shaped))
    attention_output = lowered_backward(low(attention(queries, key_rows, value_rows, seg_ids).reshape(hidden_state.shape)))
    residual_first = hidden_state + lowered_backward(jnp.einsum('yrp,po->yro', attention_output, output_weight, precision=HIGHEST_PRECISE))
    normalized_rows = layer_norm(residual_first, gain_one, bias_one)
    normalized_lowered = low(normalized_rows)
    gate_projected = lowered_backward(jnp.einsum('hqx,xt->hqt', normalized_lowered, gate_weight, precision=HIGHEST_PRECISE))
    up_projected = lowered_backward(jnp.einsum('hqx,xt->hqt', normalized_lowered, up_weight, precision=HIGHEST_PRECISE))
    middle_state = low(jax.nn.silu(gate_projected) * up_projected)
    residual_second = normalized_rows + lowered_backward(jnp.einsum('cqy,yt->cqt', middle_state, down_weight, precision=HIGHEST_PRECISE))
    return layer_norm(residual_second, gain_two, bias_two)

def reference(tokens, seg_ids, query_key_value_weight, output_weight, gate_weight, up_weight, down_weight, norm1_gain, norm1_bias, norm2_gain, norm2_bias, cotangent):
    weights = tuple((array.astype(jnp.float32) for array in (query_key_value_weight, output_weight, gate_weight, up_weight, down_weight, norm1_gain, norm1_bias, norm2_gain, norm2_bias)))
    cosine, sine_table = rope_tables(positions(seg_ids), HEAD // 2)

    def forward(inputs, probe_add, params):
        layer_zero = layer(inputs, [param[0] for param in params], seg_ids, cosine, sine_table)
        between = lowered_backward(low(layer_zero)) + probe_add
        layer_one = layer(between, [param[1] for param in params], seg_ids, cosine, sine_table)
        return (layer_one, layer_zero)
    inputs = tokens.astype(jnp.float32)
    layer_one, pullback, layer_zero = jax.vjp(forward, inputs, jnp.zeros_like(inputs), weights, has_aux=True)
    dinputs, dprobe, dweights = pullback(cotangent.astype(jnp.float32))
    section_outputs = jnp.stack([layer_zero, layer_one]).astype(jnp.bfloat16)
    input_grads = jnp.stack([dinputs, dprobe])
    return (section_outputs, input_grads, dweights[0], dweights[1], dweights[2], dweights[3], dweights[4], dweights[5], dweights[6], dweights[7], dweights[8])
```

```python
import jax
import jax.numpy as jnp
from jax import lax
from jax.sharding import PartitionSpec as P

HEAD = 64
MICRO = 2


EPS = 1e-05
NEG = -1e30


def passed_along(value, axis, steps):
    count = lax.axis_size(axis)
    first, last = (max(0, -steps), min(count, count - steps))
    return lax.ppermute(value, axis, [(source, source + steps) for source in range(first, last)])


def for_sending(array):
    return jax.tree.map(lambda a: a.astype(jnp.bfloat16) if a.dtype == jnp.float32 else a, array)


def positions(seg_ids):
    places = lax.broadcasted_iota(jnp.int32, seg_ids.shape, 1)
    begins = jnp.concatenate(
        [jnp.ones_like(seg_ids[:, :1]), (seg_ids[:, 1:] != seg_ids[:, :-1]).astype(jnp.int32)],
        axis=1,
    )
    return places - lax.cummax(places * begins, axis=1)


def rope_tables(places, half_dim):
    spread = 1000.0 ** (-2.0 * jnp.arange(half_dim, dtype=jnp.float32) / (2 * half_dim))
    angles = places.astype(jnp.float32)[..., None] * spread
    return (jnp.cos(angles), jnp.sin(angles))


def rotate(values, cosine, sine_table):
    half_dim = values.shape[-1] // 2
    former, latter = (values[..., :half_dim], values[..., half_dim:])
    cosine, sine_table = (cosine[..., None, :], sine_table[..., None, :])
    return jnp.concatenate(
        [former * cosine - latter * sine_table, latter * cosine + former * sine_table], axis=-1
    )


def unrotate(values, cosine, sine_table):
    half_dim = values.shape[-1] // 2
    former, latter = (values[..., :half_dim], values[..., half_dim:])
    cosine, sine_table = (cosine[..., None, :], sine_table[..., None, :])
    return jnp.concatenate(
        [former * cosine + latter * sine_table, latter * cosine - former * sine_table], axis=-1
    )


def norm_parts(resid, gain, bias):
    centred = resid - jnp.mean(resid, axis=-1, keepdims=True)
    scaling = lax.rsqrt(jnp.mean(centred * centred, axis=-1, keepdims=True) + EPS)
    unit_rows = centred * scaling
    return (unit_rows * gain + bias, unit_rows, scaling)


def norm_back(incoming, unit_rows, scaling, gain):
    scaled = incoming * gain
    inner = (
        scaled
        - jnp.mean(scaled, axis=-1, keepdims=True)
        - unit_rows * jnp.mean(scaled * unit_rows, axis=-1, keepdims=True)
    )
    return (
        scaling * inner,
        jnp.sum(incoming * unit_rows, axis=(0, 1)),
        jnp.sum(incoming, axis=(0, 1)),
    )


def masked_scores(queries, all_keys, seg_rows, seg_keys):
    row_count, model_width = queries.shape
    head_count = model_width // HEAD
    scores = jnp.einsum(
        "qhd,khd->hqk",
        queries.reshape(row_count, head_count, HEAD),
        all_keys.reshape(all_keys.shape[0], head_count, HEAD),
        preferred_element_type=jnp.float32,
    ) * HEAD ** (-0.5)
    return jnp.where((seg_rows[:, None] == seg_keys[None, :])[None], scores, NEG)


def attend(operands):
    queries, all_keys, all_values, seg_rows, seg_keys = operands
    row_count, model_width = queries.shape
    head_count = model_width // HEAD
    scores = masked_scores(queries, all_keys, seg_rows, seg_keys)
    row_max = jnp.max(scores, axis=-1, keepdims=True)
    exponent = jnp.exp(scores - row_max)
    row_sum = jnp.sum(exponent, axis=-1, keepdims=True)
    probs_low = (exponent / row_sum).astype(jnp.bfloat16)
    result = jnp.einsum(
        "hqk,khd->qhd",
        probs_low,
        all_values.reshape(all_values.shape[0], head_count, HEAD),
        preferred_element_type=jnp.float32,
    )
    return (result.reshape(row_count, model_width), (row_max + jnp.log(row_sum))[..., 0])


def attend_back(operands):
    queries, all_keys, all_values, seg_rows, seg_keys, log_sum, incoming = operands
    row_count, model_width = queries.shape
    head_count = model_width // HEAD
    key_count = all_keys.shape[0]
    probs = jnp.exp(masked_scores(queries, all_keys, seg_rows, seg_keys) - log_sum[..., None])
    heads_in = incoming.reshape(row_count, head_count, HEAD)
    dprobs = jnp.einsum(
        "qhd,khd->hqk",
        heads_in,
        all_values.reshape(key_count, head_count, HEAD),
        preferred_element_type=jnp.float32,
    )
    dscores = (probs * (dprobs - jnp.sum(probs * dprobs, axis=-1, keepdims=True))).astype(
        jnp.bfloat16
    )
    dquery = jnp.einsum(
        "hqk,khd->qhd",
        dscores,
        all_keys.reshape(key_count, head_count, HEAD),
        preferred_element_type=jnp.float32,
    ) * HEAD ** (-0.5)
    dkeys_part = jnp.einsum(
        "hqk,qhd->khd",
        dscores,
        queries.reshape(row_count, head_count, HEAD),
        preferred_element_type=jnp.float32,
    ) * HEAD ** (-0.5)
    dvalue = jnp.einsum(
        "hqk,qhd->khd", probs.astype(jnp.bfloat16), heads_in, preferred_element_type=jnp.float32
    )
    return (
        dquery.reshape(row_count, model_width),
        dkeys_part.reshape(key_count, model_width),
        dvalue.reshape(key_count, model_width),
    )


def layer_forward(hidden_state, weights_full, seg_rows, seg_keys, cosine, sine_table):
    query_key_value_weight, output_weight, gate_weight, up_weight, down_weight, norm_params = (
        weights_full
    )
    model_width = hidden_state.shape[-1]
    shaped = hidden_state.shape[:2] + (model_width // HEAD, HEAD)
    mixed_query_key_value = jnp.einsum(
        "bld,de->ble", hidden_state, query_key_value_weight, preferred_element_type=jnp.float32
    )
    queries = (
        rotate(mixed_query_key_value[..., :model_width].reshape(shaped), cosine, sine_table)
        .reshape(hidden_state.shape)
        .astype(jnp.bfloat16)
    )
    key_rows = (
        rotate(
            mixed_query_key_value[..., model_width : 2 * model_width].reshape(shaped),
            cosine,
            sine_table,
        )
        .reshape(hidden_state.shape)
        .astype(jnp.bfloat16)
    )
    value_rows = mixed_query_key_value[..., 2 * model_width :].astype(jnp.bfloat16)
    all_keys, all_values = (
        lax.all_gather(key_rows, "ctx", axis=1, tiled=True),
        lax.all_gather(value_rows, "ctx", axis=1, tiled=True),
    )
    attention_output, log_sum = lax.map(attend, (queries, all_keys, all_values, seg_rows, seg_keys))
    attention_output = attention_output.astype(jnp.bfloat16)
    residual_first = hidden_state.astype(jnp.float32) + jnp.einsum(
        "bld,de->ble", attention_output, output_weight, preferred_element_type=jnp.float32
    )
    normalized_rows, unit_one, scale_one = norm_parts(
        residual_first, norm_params[0], norm_params[1]
    )
    normalized_lowered = normalized_rows.astype(jnp.bfloat16)
    gate_projected = jnp.einsum(
        "bld,df->blf", normalized_lowered, gate_weight, preferred_element_type=jnp.float32
    )
    up_projected = jnp.einsum(
        "bld,df->blf", normalized_lowered, up_weight, preferred_element_type=jnp.float32
    )
    middle_state = (gate_projected * jax.nn.sigmoid(gate_projected) * up_projected).astype(
        jnp.bfloat16
    )
    residual_second = normalized_rows + jnp.einsum(
        "blf,fd->bld", middle_state, down_weight, preferred_element_type=jnp.float32
    )
    output, unit_two, scale_two = norm_parts(residual_second, norm_params[2], norm_params[3])
    extra = (all_keys, all_values)
    kept = (
        hidden_state,
        queries,
        key_rows,
        value_rows,
        log_sum,
        attention_output,
        unit_one,
        scale_one,
        gate_projected,
        up_projected,
        unit_two,
        scale_two,
    ) + extra
    return (output, kept)


def layer_backward(incoming, kept, weights_full, seg_rows, seg_keys, cosine, sine_table):
    query_key_value_weight, output_weight, gate_weight, up_weight, down_weight, norm_params = (
        weights_full
    )
    (
        hidden_state,
        queries,
        key_rows,
        value_rows,
        log_sum,
        attention_output,
        unit_one,
        scale_one,
        gate_projected,
        up_projected,
        unit_two,
        scale_two,
    ) = kept[:12]
    all_keys, all_values = (kept[12], kept[13])
    dresid_two, dgain_two, dbias_two = norm_back(incoming, unit_two, scale_two, norm_params[2])
    normalized_lowered = (unit_one * norm_params[0] + norm_params[1]).astype(jnp.bfloat16)
    sigmoid_gate = jax.nn.sigmoid(gate_projected)
    swish_gate = gate_projected * sigmoid_gate
    middle_state = (swish_gate * up_projected).astype(jnp.bfloat16)
    dout_two = dresid_two.astype(jnp.bfloat16)
    grad_down = jnp.einsum(
        "blf,bld->fd", middle_state, dout_two, preferred_element_type=jnp.float32
    )
    dmiddle = jnp.einsum("bld,fd->blf", dout_two, down_weight, preferred_element_type=jnp.float32)
    dgate_proj = (
        dmiddle * up_projected * sigmoid_gate * (1.0 + gate_projected * (1.0 - sigmoid_gate))
    ).astype(jnp.bfloat16)
    dup_proj = (dmiddle * swish_gate).astype(jnp.bfloat16)
    grad_gate = jnp.einsum(
        "bld,blf->df", normalized_lowered, dgate_proj, preferred_element_type=jnp.float32
    )
    grad_up = jnp.einsum(
        "bld,blf->df", normalized_lowered, dup_proj, preferred_element_type=jnp.float32
    )
    dnormed = (
        dresid_two
        + jnp.einsum("blf,df->bld", dgate_proj, gate_weight, preferred_element_type=jnp.float32)
        + jnp.einsum("blf,df->bld", dup_proj, up_weight, preferred_element_type=jnp.float32)
    )
    dresid_one, dgain_one, dbias_one = norm_back(dnormed, unit_one, scale_one, norm_params[0])
    dattn_out = dresid_one.astype(jnp.bfloat16)
    grad_out = jnp.einsum(
        "ble,bld->ed", attention_output, dattn_out, preferred_element_type=jnp.float32
    )
    dattended = jnp.einsum(
        "bld,ed->ble", dattn_out, output_weight, preferred_element_type=jnp.float32
    ).astype(jnp.bfloat16)
    dqueries, dkeys_all, dvalues_all = lax.map(
        attend_back, (queries, all_keys, all_values, seg_rows, seg_keys, log_sum, dattended)
    )
    dkey_rows, dvalue_rows = (
        lax.psum_scatter(
            dkeys_all.astype(jnp.bfloat16), "ctx", scatter_dimension=1, tiled=True
        ).astype(jnp.float32),
        lax.psum_scatter(
            dvalues_all.astype(jnp.bfloat16), "ctx", scatter_dimension=1, tiled=True
        ).astype(jnp.float32),
    )
    shaped = dqueries.shape[:2] + (dqueries.shape[2] // HEAD, HEAD)
    dmixed = jnp.concatenate(
        [
            unrotate(dqueries.reshape(shaped), cosine, sine_table).reshape(dqueries.shape),
            unrotate(dkey_rows.reshape(shaped), cosine, sine_table).reshape(dqueries.shape),
            dvalue_rows,
        ],
        axis=-1,
    ).astype(jnp.bfloat16)
    grad_qkv = jnp.einsum("bld,ble->de", hidden_state, dmixed, preferred_element_type=jnp.float32)
    dhidden = dresid_one + jnp.einsum(
        "ble,de->bld", dmixed, query_key_value_weight, preferred_element_type=jnp.float32
    )
    return (
        dhidden,
        (
            grad_qkv,
            grad_out,
            grad_gate,
            grad_up,
            grad_down,
            jnp.stack([dgain_one, dbias_one, dgain_two, dbias_two]),
        ),
    )


def relay_on_device(
    tokens,
    seg_ids,
    query_key_value_weight,
    output_weight,
    gate_weight,
    up_weight,
    down_weight,
    norm1_gain,
    norm1_bias,
    norm2_gain,
    norm2_bias,
    cotangent,
):
    leading = lax.axis_index("section") == 0
    ctx_rank = lax.axis_index("ctx")
    span_len = tokens.shape[1]
    per_micro = tokens.shape[0] // MICRO
    seg_near = lax.dynamic_slice_in_dim(seg_ids, ctx_rank * span_len, span_len, 1)
    cosine_rows, sine_rows = rope_tables(
        lax.dynamic_slice_in_dim(positions(seg_ids), ctx_rank * span_len, span_len, 1), HEAD // 2
    )
    shards = (
        query_key_value_weight[0],
        output_weight[0],
        gate_weight[0],
        up_weight[0],
        down_weight[0],
        jnp.stack([norm1_gain[0], norm1_bias[0], norm2_gain[0], norm2_bias[0]]),
    )
    gathered = (
        lax.all_gather(shards[0], "dp", axis=0, tiled=True),
        lax.all_gather(shards[1], "dp", axis=0, tiled=True),
        lax.all_gather(shards[2], "dp", axis=0, tiled=True),
        lax.all_gather(shards[3], "dp", axis=0, tiled=True),
        lax.all_gather(shards[4], "dp", axis=0, tiled=True),
        lax.all_gather(shards[5], "dp", axis=1, tiled=True),
    )
    weights_full = gathered[:5] + (gathered[5].astype(jnp.float32),)

    def select(array, micro_idx):
        return lax.dynamic_slice_in_dim(array, micro_idx * per_micro, per_micro, 0)

    delay_fwd = jnp.where(leading, 0, 1)
    received = jnp.zeros((per_micro,) + tokens.shape[1:], jnp.bfloat16)
    outputs = []
    stored = []
    for tick_no in range(MICRO + 1):
        micro_idx = jnp.clip(tick_no - delay_fwd, 0, MICRO - 1)
        hidden_state = jnp.where(leading, select(tokens, micro_idx), received)
        output, kept = layer_forward(
            hidden_state,
            weights_full,
            select(seg_near, micro_idx),
            select(seg_ids, micro_idx),
            select(cosine_rows, micro_idx),
            select(sine_rows, micro_idx),
        )
        sent_rows = output.astype(jnp.bfloat16)
        outputs.append(sent_rows)
        stored.append(kept)
        if tick_no < MICRO:
            received = passed_along(sent_rows, "section", 1)
    gathered = (
        lax.all_gather(shards[0], "dp", axis=0, tiled=True),
        lax.all_gather(shards[1], "dp", axis=0, tiled=True),
        lax.all_gather(shards[2], "dp", axis=0, tiled=True),
        lax.all_gather(shards[3], "dp", axis=0, tiled=True),
        lax.all_gather(shards[4], "dp", axis=0, tiled=True),
        lax.all_gather(shards[5], "dp", axis=1, tiled=True),
    )
    weights_full = gathered[:5] + (gathered[5].astype(jnp.float32),)
    returned = jnp.zeros_like(received)
    totals = None
    input_parts = []
    for tick_no in range(MICRO + 1):
        micro_idx = jnp.clip(tick_no - 1 + delay_fwd, 0, MICRO - 1)
        active = jnp.where(leading, tick_no >= 1, tick_no < MICRO)
        incoming = jnp.where(
            leading, returned.astype(jnp.float32), select(cotangent, micro_idx).astype(jnp.float32)
        )
        incoming = jnp.where(active, incoming, 0.0)
        kept = jax.tree.map(
            lambda early, later: jnp.where(leading, early, later),
            stored[max(tick_no - 1, 0)],
            stored[min(tick_no + 1, MICRO)],
        )
        dhidden, grad_terms = layer_backward(
            incoming,
            kept,
            weights_full,
            select(seg_near, micro_idx),
            select(seg_ids, micro_idx),
            select(cosine_rows, micro_idx),
            select(sine_rows, micro_idx),
        )
        totals = (
            grad_terms
            if totals is None
            else tuple((early + later for early, later in zip(totals, grad_terms)))
        )
        input_parts.append(dhidden)
        if tick_no < MICRO:
            returned = passed_along(dhidden.astype(jnp.bfloat16), "section", -1)
    summed = (
        lax.psum_scatter(
            totals[0].astype(jnp.bfloat16), "dp", scatter_dimension=0, tiled=True
        ).astype(jnp.float32),
        lax.psum_scatter(
            totals[1].astype(jnp.bfloat16), "dp", scatter_dimension=0, tiled=True
        ).astype(jnp.float32),
        lax.psum_scatter(
            totals[2].astype(jnp.bfloat16), "dp", scatter_dimension=0, tiled=True
        ).astype(jnp.float32),
        lax.psum_scatter(
            totals[3].astype(jnp.bfloat16), "dp", scatter_dimension=0, tiled=True
        ).astype(jnp.float32),
        lax.psum_scatter(
            totals[4].astype(jnp.bfloat16), "dp", scatter_dimension=0, tiled=True
        ).astype(jnp.float32),
        lax.psum_scatter(
            totals[5].astype(jnp.bfloat16), "dp", scatter_dimension=1, tiled=True
        ).astype(jnp.float32),
    )
    summed = jax.tree.map(
        lambda part: part.astype(jnp.float32), lax.psum(for_sending(summed), "ctx")
    )
    last_rows = jnp.concatenate(
        [jnp.where(leading, outputs[micro_no], outputs[micro_no + 1]) for micro_no in range(MICRO)],
        axis=0,
    )
    input_grads = jnp.concatenate(
        [
            jnp.where(leading, input_parts[micro_no + 1], input_parts[micro_no])
            for micro_no in range(MICRO)
        ],
        axis=0,
    )
    norm_grads = summed[5]
    return (
        last_rows[None],
        input_grads[None],
        summed[0][None],
        summed[1][None],
        summed[2][None],
        summed[3][None],
        summed[4][None],
        norm_grads[0][None],
        norm_grads[1][None],
        norm_grads[2][None],
        norm_grads[3][None],
    )


def other_core(value, pairs=((0, 1), (1, 0))):
    return lax.ppermute(value, "section", list(pairs))


def along_x(value):
    return lax.ppermute(value, "dp", [(i, i ^ 1) for i in range(4)])


def along_y(value):
    return lax.ppermute(value, "dp", [(i, i ^ 2) for i in range(4)])


def along_z(value):
    return lax.ppermute(value, "ctx", [(i, i ^ 1) for i in range(4)])


def z_swap(value):
    pairs = [(4 + i, 4 + (i ^ 2)) for i in range(4)]
    return lax.ppermute(value, ("section", "ctx"), pairs)


def lowered(value):
    return value.astype(jnp.bfloat16)


def by_core(core, mine, theirs, axis):
    return jnp.where(
        core == 0,
        jnp.concatenate([mine, theirs], axis=axis),
        jnp.concatenate([theirs, mine], axis=axis),
    )


def half_of(array, which):
    width = array.shape[-1] // 2
    return lax.dynamic_slice_in_dim(array, which * width, width, array.ndim - 1)


def gather_half(piece, dp_rank):
    rows = piece.shape[0] // 2
    from_x, from_y = along_x(piece), along_y(piece)
    diag = jnp.concatenate([along_x(from_y[:rows]), along_y(from_x[rows:])], axis=0)
    odd, high = (dp_rank & 1) == 1, (dp_rank & 2) == 2
    near = jnp.where(odd, jnp.concatenate([from_x, piece]), jnp.concatenate([piece, from_x]))
    far = jnp.where(odd, jnp.concatenate([diag, from_y]), jnp.concatenate([from_y, diag]))
    return jnp.where(high, jnp.concatenate([far, near]), jnp.concatenate([near, far]))


def reduce_half(partial, dp_rank, ctx_rank):
    count = partial.shape[0] // 4
    rows = count // 2

    def part(flip, begin, size):
        return lax.dynamic_slice_in_dim(partial, (dp_rank ^ flip) * count + begin, size, 0)

    to_x, to_y = along_x(part(3, 0, rows)), along_y(part(3, rows, rows))
    x_first, y_last = along_x(part(1, 0, rows)), along_y(part(2, rows, rows))
    x_last = along_x(lowered(part(1, rows, rows).astype(jnp.float32) + to_y.astype(jnp.float32)))
    y_first = along_y(lowered(part(2, 0, rows).astype(jnp.float32) + to_x.astype(jnp.float32)))
    own = part(0, 0, count).astype(jnp.float32)
    summed = lowered(
        own
        + jnp.concatenate([x_first, x_last]).astype(jnp.float32)
        + jnp.concatenate([y_first, y_last]).astype(jnp.float32)
    )
    inner = lax.ppermute(summed, "ctx", [(0, 1), (3, 2)])
    pair = lowered(summed.astype(jnp.float32) + inner.astype(jnp.float32))
    across = lax.ppermute(pair, "ctx", [(1, 2), (2, 1)])
    total = lowered(pair.astype(jnp.float32) + across.astype(jnp.float32))
    outer = lax.ppermute(total, "ctx", [(1, 0), (2, 3)])
    return jnp.where((ctx_rank == 0) | (ctx_rank == 3), outer, total)


def forward_rows(hidden, weights, seg_rows, seg_keys, cosine, sine):
    qkv_weight, output_weight, gate_weight, up_weight, down_weight, norm_params = weights
    rows, width = hidden.shape
    shaped = (rows, width // HEAD, HEAD)
    dot = lambda a, b: jnp.dot(a, b, preferred_element_type=jnp.float32)
    mixed = dot(hidden, qkv_weight)
    queries = lowered(rotate(mixed[:, :width].reshape(shaped), cosine, sine).reshape(rows, width))
    keys = lowered(
        rotate(mixed[:, width : 2 * width].reshape(shaped), cosine, sine).reshape(rows, width)
    )
    own = jnp.concatenate([keys, lowered(mixed[:, 2 * width :])], axis=1)
    from_z = along_z(own)
    blocks = jnp.concatenate([own, other_core(own), from_z, other_core(from_z)], axis=0)
    all_keys, all_values = blocks[:, :width], blocks[:, width:]
    attended, log_sum = attend((queries, all_keys, all_values, seg_rows, seg_keys))
    attended = lowered(attended)
    resid_one = hidden.astype(jnp.float32) + dot(attended, output_weight)
    normed, unit_one, scale_one = norm_parts(resid_one, norm_params[0], norm_params[1])
    normed_low = lowered(normed)
    gate_proj, up_proj = dot(normed_low, gate_weight), dot(normed_low, up_weight)
    middle = lowered(gate_proj * jax.nn.sigmoid(gate_proj) * up_proj)
    resid_two = normed + dot(middle, down_weight)
    output, unit_two, scale_two = norm_parts(resid_two, norm_params[2], norm_params[3])
    kept = (
        hidden, queries, all_keys, all_values, log_sum, attended, unit_one, scale_one,
        normed_low, gate_proj, up_proj, middle, unit_two, scale_two,
    )
    return output, kept


def backward_rows(incoming, kept, weights, seg_rows, seg_keys, cosine, sine, core):
    qkv_weight, output_weight, gate_weight, up_weight, down_weight, norm_params = weights
    (
        hidden, queries, all_keys, all_values, log_sum, attended, unit_one, scale_one,
        normed_low, gate_proj, up_proj, middle, unit_two, scale_two,
    ) = kept
    rows, width = hidden.shape
    shaped = (rows, width // HEAD, HEAD)
    dot_t = lambda a, b: lax.dot_general(
        a, b, (((1,), (1,)), ((), ())), preferred_element_type=jnp.float32
    )

    def weight_grad(left, right):
        left_all = jnp.concatenate([left, other_core(left)], axis=0)
        right_all = jnp.concatenate(
            [half_of(right, core), other_core(half_of(right, 1 - core))], axis=0
        )
        return lowered(
            lax.dot_general(
                left_all, right_all, (((0,), (0,)), ((), ())), preferred_element_type=jnp.float32
            )
        )

    def norm_back_rows(grad, unit, scale, gain):
        result, dgain, dbias = norm_back(grad[None], unit[None], scale[None], gain)
        return result[0], dgain, dbias

    dresid_two, dgain_two, dbias_two = norm_back_rows(incoming, unit_two, scale_two, norm_params[2])
    dout_two = lowered(dresid_two)
    grad_down = weight_grad(middle, dout_two)
    dmiddle = dot_t(dout_two, down_weight)
    sig = jax.nn.sigmoid(gate_proj)
    dgate = lowered(dmiddle * up_proj * sig * (1.0 + gate_proj * (1.0 - sig)))
    dup = lowered(dmiddle * (gate_proj * sig))
    grad_gate, grad_up = weight_grad(normed_low, dgate), weight_grad(normed_low, dup)
    dnormed = dresid_two + dot_t(dgate, gate_weight) + dot_t(dup, up_weight)
    dresid_one, dgain_one, dbias_one = norm_back_rows(dnormed, unit_one, scale_one, norm_params[0])
    dattn_out = lowered(dresid_one)
    grad_out = weight_grad(attended, dattn_out)
    dattended = lowered(dot_t(dattn_out, output_weight))
    dqueries, dkeys, dvalues = attend_back(
        (queries, all_keys, all_values, seg_rows, seg_keys, log_sum, dattended)
    )
    parts = lowered(jnp.concatenate([dkeys, dvalues], axis=1)).reshape(4, rows, 2 * width)
    from_core = other_core(jnp.stack([parts[1], parts[3]])).astype(jnp.float32)
    from_z = along_z(lowered(parts[2].astype(jnp.float32) + from_core[1])).astype(jnp.float32)
    dkv = parts[0].astype(jnp.float32) + from_core[0] + from_z
    dmixed = lowered(
        jnp.concatenate(
            [
                unrotate(dqueries.reshape(shaped), cosine, sine).reshape(rows, width),
                unrotate(dkv[:, :width].reshape(shaped), cosine, sine).reshape(rows, width),
                dkv[:, width:],
            ],
            axis=1,
        )
    )
    grad_qkv = weight_grad(hidden, dmixed)
    dhidden = dresid_one + dot_t(dmixed, qkv_weight)
    return (
        dhidden,
        (grad_qkv, grad_out, grad_gate, grad_up, grad_down),
        jnp.stack([dgain_one, dbias_one, dgain_two, dbias_two]),
    )


def paired_on_device(
    tokens,
    seg_ids,
    query_key_value_weight,
    output_weight,
    gate_weight,
    up_weight,
    down_weight,
    norm1_gain,
    norm1_bias,
    norm2_gain,
    norm2_bias,
    cotangent,
):
    core, ctx_rank, dp_rank = (lax.axis_index(a) for a in ("section", "ctx", "dp"))
    span = tokens.shape[1]
    sequence = ctx_rank // 2
    block = ctx_rank ^ (2 * core)
    pick = lambda array, index: lax.dynamic_index_in_dim(array, index, 0, keepdims=False)

    def rows_of(array):
        return jnp.where(core == 0, pick(array, sequence), z_swap(pick(array, 1 - sequence)))

    seg = pick(seg_ids, sequence)
    places = pick(positions(seg_ids), sequence)
    seg_rows = lax.dynamic_slice_in_dim(seg, block * span, span, 0)
    seg_keys = jnp.concatenate(
        [lax.dynamic_slice_in_dim(seg, (block ^ flip) * span, span, 0) for flip in (0, 2, 1, 3)]
    )
    cosine, sine = rope_tables(lax.dynamic_slice_in_dim(places, block * span, span, 0), HEAD // 2)

    shards = (query_key_value_weight, output_weight, gate_weight, up_weight, down_weight)
    norm_shard = jnp.concatenate([norm1_gain, norm1_bias, norm2_gain, norm2_bias], axis=0)
    norms = lax.all_gather(norm_shard, "section", axis=0)
    norms = lax.all_gather(norms, "dp", axis=2, tiled=True).astype(jnp.float32)

    weights = [[], []]
    own_half = [half_of(shard[0], core) for shard in shards]
    sent_half = [other_core(half_of(shard[0], 1 - core)) for shard in shards]
    for layer in range(2):
        for own, received in zip(own_half, sent_half):
            piece = jnp.where(core == layer, own, received)
            mine = gather_half(piece, dp_rank)
            weights[layer].append(by_core(core, mine, other_core(mine), 1))
        weights[layer].append(norms[layer])

    hidden = rows_of(tokens)
    incoming = rows_of(cotangent).astype(jnp.float32)
    kept, outputs = [], []
    for layer in range(2):
        output, keep = forward_rows(hidden, weights[layer], seg_rows, seg_keys, cosine, sine)
        hidden = lowered(output)
        kept.append(keep)
        outputs.append(hidden)
    totals, norm_sums, input_rows = [None, None], [None, None], [None, None]
    for layer in (1, 0):
        dhidden, grads, norm_sums[layer] = backward_rows(
            incoming, kept[layer], weights[layer], seg_rows, seg_keys, cosine, sine, core
        )
        totals[layer] = [reduce_half(grad, dp_rank, ctx_rank) for grad in grads]
        input_rows[layer] = dhidden
        incoming = lowered(dhidden).astype(jnp.float32)

    def whole(first, second):
        from_first = other_core(first, ((1, 0),))
        from_second = other_core(second, ((0, 1),))
        mine = jnp.where(core == 0, first, second)
        theirs = jnp.where(core == 0, from_first, from_second)
        return by_core(core, mine, theirs, 1).astype(jnp.float32)[None]

    grads = [whole(first, second) for first, second in zip(*totals)]
    norm_sums = lax.psum(jnp.stack(norm_sums), ("section", "dp", "ctx"))
    norm_grads = lax.dynamic_slice_in_dim(
        pick(norm_sums, core), dp_rank * norm1_gain.shape[1], norm1_gain.shape[1], 1
    )

    def placed_rows(first, second):
        first, second = lowered(first), lowered(second)
        near = jnp.where(
            core == 0, first, other_core(second, ((0, 1),))
        )
        swapped = z_swap(jnp.stack([first, second]))
        far = jnp.where(core == 0, other_core(swapped[0], ((1, 0),)), swapped[1])
        return jnp.where(sequence == 0, jnp.stack([near, far]), jnp.stack([far, near]))[None]

    return (
        placed_rows(*outputs),
        placed_rows(*input_rows).astype(jnp.float32),
        *grads,
        *(norm_grads[i][None] for i in range(4)),
    )


def solution(mesh):
    placed = (
        P("dp", "ctx", None),
        P("dp", None),
        P("section", "dp", None),
        P("section", "dp", None),
        P("section", "dp", None),
        P("section", "dp", None),
        P("section", "dp", None),
        P("section", "dp"),
        P("section", "dp"),
        P("section", "dp"),
        P("section", "dp"),
        P("dp", "ctx", None),
    )
    paired = mesh.shape["section"] == 2 and mesh.shape["ctx"] == 4 and mesh.shape["dp"] == 4
    return jax.shard_map(
        paired_on_device if paired else relay_on_device,
        mesh=mesh,
        in_specs=placed,
        out_specs=(
            P("section", "dp", "ctx", None),
            P("section", "dp", "ctx", None),
            P("section", "dp", None),
            P("section", "dp", None),
            P("section", "dp", None),
            P("section", "dp", None),
            P("section", "dp", None),
            P("section", "dp"),
            P("section", "dp"),
            P("section", "dp"),
            P("section", "dp"),
        ),
        check_vma=False,
    )
```

```python
import jax
import jax.numpy as jnp
from jax import lax
from jax.experimental import pallas as pl
from jax.experimental.pallas import tpu as pltpu
from jax.sharding import PartitionSpec as P

HEAD = 64
MICRO = 2


EPS = 1e-05
NEG = -1e30


def passed_along(value, axis, steps):
    count = lax.axis_size(axis)
    first, last = (max(0, -steps), min(count, count - steps))
    return lax.ppermute(value, axis, [(source, source + steps) for source in range(first, last)])


def for_sending(array):
    return jax.tree.map(lambda a: a.astype(jnp.bfloat16) if a.dtype == jnp.float32 else a, array)


def positions(seg_ids):
    places = lax.broadcasted_iota(jnp.int32, seg_ids.shape, 1)
    begins = jnp.concatenate(
        [jnp.ones_like(seg_ids[:, :1]), (seg_ids[:, 1:] != seg_ids[:, :-1]).astype(jnp.int32)],
        axis=1,
    )
    return places - lax.cummax(places * begins, axis=1)


def rope_tables(places, half_dim):
    spread = 1000.0 ** (-2.0 * jnp.arange(half_dim, dtype=jnp.float32) / (2 * half_dim))
    angles = places.astype(jnp.float32)[..., None] * spread
    return (jnp.cos(angles), jnp.sin(angles))


def rotate(values, cosine, sine_table):
    half_dim = values.shape[-1] // 2
    former, latter = (values[..., :half_dim], values[..., half_dim:])
    cosine, sine_table = (cosine[..., None, :], sine_table[..., None, :])
    return jnp.concatenate(
        [former * cosine - latter * sine_table, latter * cosine + former * sine_table], axis=-1
    )


def unrotate(values, cosine, sine_table):
    half_dim = values.shape[-1] // 2
    former, latter = (values[..., :half_dim], values[..., half_dim:])
    cosine, sine_table = (cosine[..., None, :], sine_table[..., None, :])
    return jnp.concatenate(
        [former * cosine + latter * sine_table, latter * cosine - former * sine_table], axis=-1
    )


def norm_parts(resid, gain, bias):
    centred = resid - jnp.mean(resid, axis=-1, keepdims=True)
    scaling = lax.rsqrt(jnp.mean(centred * centred, axis=-1, keepdims=True) + EPS)
    unit_rows = centred * scaling
    return (unit_rows * gain + bias, unit_rows, scaling)


def norm_back(incoming, unit_rows, scaling, gain):
    scaled = incoming * gain
    inner = (
        scaled
        - jnp.mean(scaled, axis=-1, keepdims=True)
        - unit_rows * jnp.mean(scaled * unit_rows, axis=-1, keepdims=True)
    )
    return (
        scaling * inner,
        jnp.sum(incoming * unit_rows, axis=(0, 1)),
        jnp.sum(incoming, axis=(0, 1)),
    )


def masked_scores(queries, all_keys, seg_rows, seg_keys):
    row_count, model_width = queries.shape
    head_count = model_width // HEAD
    scores = jnp.einsum(
        "qhd,khd->hqk",
        queries.reshape(row_count, head_count, HEAD),
        all_keys.reshape(all_keys.shape[0], head_count, HEAD),
        preferred_element_type=jnp.float32,
    ) * HEAD ** (-0.5)
    return jnp.where((seg_rows[:, None] == seg_keys[None, :])[None], scores, NEG)


def attend(operands):
    queries, all_keys, all_values, seg_rows, seg_keys = operands
    row_count, model_width = queries.shape
    head_count = model_width // HEAD
    scores = masked_scores(queries, all_keys, seg_rows, seg_keys)
    row_max = jnp.max(scores, axis=-1, keepdims=True)
    exponent = jnp.exp(scores - row_max)
    row_sum = jnp.sum(exponent, axis=-1, keepdims=True)
    probs_low = (exponent / row_sum).astype(jnp.bfloat16)
    result = jnp.einsum(
        "hqk,khd->qhd",
        probs_low,
        all_values.reshape(all_values.shape[0], head_count, HEAD),
        preferred_element_type=jnp.float32,
    )
    return (result.reshape(row_count, model_width), (row_max + jnp.log(row_sum))[..., 0])


def attend_back(operands):
    queries, all_keys, all_values, seg_rows, seg_keys, log_sum, incoming = operands
    row_count, model_width = queries.shape
    head_count = model_width // HEAD
    key_count = all_keys.shape[0]
    probs = jnp.exp(masked_scores(queries, all_keys, seg_rows, seg_keys) - log_sum[..., None])
    heads_in = incoming.reshape(row_count, head_count, HEAD)
    dprobs = jnp.einsum(
        "qhd,khd->hqk",
        heads_in,
        all_values.reshape(key_count, head_count, HEAD),
        preferred_element_type=jnp.float32,
    )
    dscores = (probs * (dprobs - jnp.sum(probs * dprobs, axis=-1, keepdims=True))).astype(
        jnp.bfloat16
    )
    dquery = jnp.einsum(
        "hqk,khd->qhd",
        dscores,
        all_keys.reshape(key_count, head_count, HEAD),
        preferred_element_type=jnp.float32,
    ) * HEAD ** (-0.5)
    dkeys_part = jnp.einsum(
        "hqk,qhd->khd",
        dscores,
        queries.reshape(row_count, head_count, HEAD),
        preferred_element_type=jnp.float32,
    ) * HEAD ** (-0.5)
    dvalue = jnp.einsum(
        "hqk,qhd->khd", probs.astype(jnp.bfloat16), heads_in, preferred_element_type=jnp.float32
    )
    return (
        dquery.reshape(row_count, model_width),
        dkeys_part.reshape(key_count, model_width),
        dvalue.reshape(key_count, model_width),
    )


def layer_forward(hidden_state, weights_full, seg_rows, seg_keys, cosine, sine_table):
    query_key_value_weight, output_weight, gate_weight, up_weight, down_weight, norm_params = (
        weights_full
    )
    model_width = hidden_state.shape[-1]
    shaped = hidden_state.shape[:2] + (model_width // HEAD, HEAD)
    mixed_query_key_value = jnp.einsum(
        "bld,de->ble", hidden_state, query_key_value_weight, preferred_element_type=jnp.float32
    )
    queries = (
        rotate(mixed_query_key_value[..., :model_width].reshape(shaped), cosine, sine_table)
        .reshape(hidden_state.shape)
        .astype(jnp.bfloat16)
    )
    key_rows = (
        rotate(
            mixed_query_key_value[..., model_width : 2 * model_width].reshape(shaped),
            cosine,
            sine_table,
        )
        .reshape(hidden_state.shape)
        .astype(jnp.bfloat16)
    )
    value_rows = mixed_query_key_value[..., 2 * model_width :].astype(jnp.bfloat16)
    all_keys, all_values = (
        lax.all_gather(key_rows, "ctx", axis=1, tiled=True),
        lax.all_gather(value_rows, "ctx", axis=1, tiled=True),
    )
    attention_output, log_sum = lax.map(attend, (queries, all_keys, all_values, seg_rows, seg_keys))
    attention_output = attention_output.astype(jnp.bfloat16)
    residual_first = hidden_state.astype(jnp.float32) + jnp.einsum(
        "bld,de->ble", attention_output, output_weight, preferred_element_type=jnp.float32
    )
    normalized_rows, unit_one, scale_one = norm_parts(
        residual_first, norm_params[0], norm_params[1]
    )
    normalized_lowered = normalized_rows.astype(jnp.bfloat16)
    gate_projected = jnp.einsum(
        "bld,df->blf", normalized_lowered, gate_weight, preferred_element_type=jnp.float32
    )
    up_projected = jnp.einsum(
        "bld,df->blf", normalized_lowered, up_weight, preferred_element_type=jnp.float32
    )
    middle_state = (gate_projected * jax.nn.sigmoid(gate_projected) * up_projected).astype(
        jnp.bfloat16
    )
    residual_second = normalized_rows + jnp.einsum(
        "blf,fd->bld", middle_state, down_weight, preferred_element_type=jnp.float32
    )
    output, unit_two, scale_two = norm_parts(residual_second, norm_params[2], norm_params[3])
    extra = (all_keys, all_values)
    kept = (
        hidden_state,
        queries,
        key_rows,
        value_rows,
        log_sum,
        attention_output,
        unit_one,
        scale_one,
        gate_projected,
        up_projected,
        unit_two,
        scale_two,
    ) + extra
    return (output, kept)


def layer_backward(incoming, kept, weights_full, seg_rows, seg_keys, cosine, sine_table):
    query_key_value_weight, output_weight, gate_weight, up_weight, down_weight, norm_params = (
        weights_full
    )
    (
        hidden_state,
        queries,
        key_rows,
        value_rows,
        log_sum,
        attention_output,
        unit_one,
        scale_one,
        gate_projected,
        up_projected,
        unit_two,
        scale_two,
    ) = kept[:12]
    all_keys, all_values = (kept[12], kept[13])
    dresid_two, dgain_two, dbias_two = norm_back(incoming, unit_two, scale_two, norm_params[2])
    normalized_lowered = (unit_one * norm_params[0] + norm_params[1]).astype(jnp.bfloat16)
    sigmoid_gate = jax.nn.sigmoid(gate_projected)
    swish_gate = gate_projected * sigmoid_gate
    middle_state = (swish_gate * up_projected).astype(jnp.bfloat16)
    dout_two = dresid_two.astype(jnp.bfloat16)
    grad_down = jnp.einsum(
        "blf,bld->fd", middle_state, dout_two, preferred_element_type=jnp.float32
    )
    dmiddle = jnp.einsum("bld,fd->blf", dout_two, down_weight, preferred_element_type=jnp.float32)
    dgate_proj = (
        dmiddle * up_projected * sigmoid_gate * (1.0 + gate_projected * (1.0 - sigmoid_gate))
    ).astype(jnp.bfloat16)
    dup_proj = (dmiddle * swish_gate).astype(jnp.bfloat16)
    grad_gate = jnp.einsum(
        "bld,blf->df", normalized_lowered, dgate_proj, preferred_element_type=jnp.float32
    )
    grad_up = jnp.einsum(
        "bld,blf->df", normalized_lowered, dup_proj, preferred_element_type=jnp.float32
    )
    dnormed = (
        dresid_two
        + jnp.einsum("blf,df->bld", dgate_proj, gate_weight, preferred_element_type=jnp.float32)
        + jnp.einsum("blf,df->bld", dup_proj, up_weight, preferred_element_type=jnp.float32)
    )
    dresid_one, dgain_one, dbias_one = norm_back(dnormed, unit_one, scale_one, norm_params[0])
    dattn_out = dresid_one.astype(jnp.bfloat16)
    grad_out = jnp.einsum(
        "ble,bld->ed", attention_output, dattn_out, preferred_element_type=jnp.float32
    )
    dattended = jnp.einsum(
        "bld,ed->ble", dattn_out, output_weight, preferred_element_type=jnp.float32
    ).astype(jnp.bfloat16)
    dqueries, dkeys_all, dvalues_all = lax.map(
        attend_back, (queries, all_keys, all_values, seg_rows, seg_keys, log_sum, dattended)
    )
    dkey_rows, dvalue_rows = (
        lax.psum_scatter(
            dkeys_all.astype(jnp.bfloat16), "ctx", scatter_dimension=1, tiled=True
        ).astype(jnp.float32),
        lax.psum_scatter(
            dvalues_all.astype(jnp.bfloat16), "ctx", scatter_dimension=1, tiled=True
        ).astype(jnp.float32),
    )
    shaped = dqueries.shape[:2] + (dqueries.shape[2] // HEAD, HEAD)
    dmixed = jnp.concatenate(
        [
            unrotate(dqueries.reshape(shaped), cosine, sine_table).reshape(dqueries.shape),
            unrotate(dkey_rows.reshape(shaped), cosine, sine_table).reshape(dqueries.shape),
            dvalue_rows,
        ],
        axis=-1,
    ).astype(jnp.bfloat16)
    grad_qkv = jnp.einsum("bld,ble->de", hidden_state, dmixed, preferred_element_type=jnp.float32)
    dhidden = dresid_one + jnp.einsum(
        "ble,de->bld", dmixed, query_key_value_weight, preferred_element_type=jnp.float32
    )
    return (
        dhidden,
        (
            grad_qkv,
            grad_out,
            grad_gate,
            grad_up,
            grad_down,
            jnp.stack([dgain_one, dbias_one, dgain_two, dbias_two]),
        ),
    )


def relay_on_device(
    tokens,
    seg_ids,
    query_key_value_weight,
    output_weight,
    gate_weight,
    up_weight,
    down_weight,
    norm1_gain,
    norm1_bias,
    norm2_gain,
    norm2_bias,
    cotangent,
):
    leading = lax.axis_index("section") == 0
    ctx_rank = lax.axis_index("ctx")
    span_len = tokens.shape[1]
    per_micro = tokens.shape[0] // MICRO
    seg_near = lax.dynamic_slice_in_dim(seg_ids, ctx_rank * span_len, span_len, 1)
    cosine_rows, sine_rows = rope_tables(
        lax.dynamic_slice_in_dim(positions(seg_ids), ctx_rank * span_len, span_len, 1), HEAD // 2
    )
    shards = (
        query_key_value_weight[0],
        output_weight[0],
        gate_weight[0],
        up_weight[0],
        down_weight[0],
        jnp.stack([norm1_gain[0], norm1_bias[0], norm2_gain[0], norm2_bias[0]]),
    )
    gathered = (
        lax.all_gather(shards[0], "dp", axis=0, tiled=True),
        lax.all_gather(shards[1], "dp", axis=0, tiled=True),
        lax.all_gather(shards[2], "dp", axis=0, tiled=True),
        lax.all_gather(shards[3], "dp", axis=0, tiled=True),
        lax.all_gather(shards[4], "dp", axis=0, tiled=True),
        lax.all_gather(shards[5], "dp", axis=1, tiled=True),
    )
    weights_full = gathered[:5] + (gathered[5].astype(jnp.float32),)

    def select(array, micro_idx):
        return lax.dynamic_slice_in_dim(array, micro_idx * per_micro, per_micro, 0)

    delay_fwd = jnp.where(leading, 0, 1)
    received = jnp.zeros((per_micro,) + tokens.shape[1:], jnp.bfloat16)
    outputs = []
    stored = []
    for tick_no in range(MICRO + 1):
        micro_idx = jnp.clip(tick_no - delay_fwd, 0, MICRO - 1)
        hidden_state = jnp.where(leading, select(tokens, micro_idx), received)
        output, kept = layer_forward(
            hidden_state,
            weights_full,
            select(seg_near, micro_idx),
            select(seg_ids, micro_idx),
            select(cosine_rows, micro_idx),
            select(sine_rows, micro_idx),
        )
        sent_rows = output.astype(jnp.bfloat16)
        outputs.append(sent_rows)
        stored.append(kept)
        if tick_no < MICRO:
            received = passed_along(sent_rows, "section", 1)
    gathered = (
        lax.all_gather(shards[0], "dp", axis=0, tiled=True),
        lax.all_gather(shards[1], "dp", axis=0, tiled=True),
        lax.all_gather(shards[2], "dp", axis=0, tiled=True),
        lax.all_gather(shards[3], "dp", axis=0, tiled=True),
        lax.all_gather(shards[4], "dp", axis=0, tiled=True),
        lax.all_gather(shards[5], "dp", axis=1, tiled=True),
    )
    weights_full = gathered[:5] + (gathered[5].astype(jnp.float32),)
    returned = jnp.zeros_like(received)
    totals = None
    input_parts = []
    for tick_no in range(MICRO + 1):
        micro_idx = jnp.clip(tick_no - 1 + delay_fwd, 0, MICRO - 1)
        active = jnp.where(leading, tick_no >= 1, tick_no < MICRO)
        incoming = jnp.where(
            leading, returned.astype(jnp.float32), select(cotangent, micro_idx).astype(jnp.float32)
        )
        incoming = jnp.where(active, incoming, 0.0)
        kept = jax.tree.map(
            lambda early, later: jnp.where(leading, early, later),
            stored[max(tick_no - 1, 0)],
            stored[min(tick_no + 1, MICRO)],
        )
        dhidden, grad_terms = layer_backward(
            incoming,
            kept,
            weights_full,
            select(seg_near, micro_idx),
            select(seg_ids, micro_idx),
            select(cosine_rows, micro_idx),
            select(sine_rows, micro_idx),
        )
        totals = (
            grad_terms
            if totals is None
            else tuple((early + later for early, later in zip(totals, grad_terms)))
        )
        input_parts.append(dhidden)
        if tick_no < MICRO:
            returned = passed_along(dhidden.astype(jnp.bfloat16), "section", -1)
    summed = (
        lax.psum_scatter(
            totals[0].astype(jnp.bfloat16), "dp", scatter_dimension=0, tiled=True
        ).astype(jnp.float32),
        lax.psum_scatter(
            totals[1].astype(jnp.bfloat16), "dp", scatter_dimension=0, tiled=True
        ).astype(jnp.float32),
        lax.psum_scatter(
            totals[2].astype(jnp.bfloat16), "dp", scatter_dimension=0, tiled=True
        ).astype(jnp.float32),
        lax.psum_scatter(
            totals[3].astype(jnp.bfloat16), "dp", scatter_dimension=0, tiled=True
        ).astype(jnp.float32),
        lax.psum_scatter(
            totals[4].astype(jnp.bfloat16), "dp", scatter_dimension=0, tiled=True
        ).astype(jnp.float32),
        lax.psum_scatter(
            totals[5].astype(jnp.bfloat16), "dp", scatter_dimension=1, tiled=True
        ).astype(jnp.float32),
    )
    summed = jax.tree.map(
        lambda part: part.astype(jnp.float32), lax.psum(for_sending(summed), "ctx")
    )
    last_rows = jnp.concatenate(
        [jnp.where(leading, outputs[micro_no], outputs[micro_no + 1]) for micro_no in range(MICRO)],
        axis=0,
    )
    input_grads = jnp.concatenate(
        [
            jnp.where(leading, input_parts[micro_no + 1], input_parts[micro_no])
            for micro_no in range(MICRO)
        ],
        axis=0,
    )
    norm_grads = summed[5]
    return (
        last_rows[None],
        input_grads[None],
        summed[0][None],
        summed[1][None],
        summed[2][None],
        summed[3][None],
        summed[4][None],
        norm_grads[0][None],
        norm_grads[1][None],
        norm_grads[2][None],
        norm_grads[3][None],
    )


NT = (((1,), (1,)), ((), ()))
TN = (((0,), (0,)), ((), ()))


def mm(left, right, dims=(((1,), (0,)), ((), ()))):
    return lax.dot_general(left, right, dims, preferred_element_type=jnp.float32)


def in_vmem():
    return pl.BlockSpec(memory_space=pltpu.VMEM)


def anywhere():
    return pl.BlockSpec(memory_space=pl.ANY)


def in_smem():
    return pl.BlockSpec(memory_space=pltpu.SMEM)


def kernel_call(body, out_shapes, in_specs, scratch, mbytes, cost, name, out_specs=None, grid=None):
    return pl.pallas_call(
        body,
        out_shape=out_shapes,
        in_specs=in_specs,
        out_specs=[in_vmem()] * len(out_shapes) if out_specs is None else out_specs,
        scratch_shapes=scratch,
        **({} if grid is None else {"grid": grid}),
        compiler_params=pltpu.CompilerParams(vmem_limit_bytes=mbytes * 2**20),
        cost_estimate=pl.CostEstimate(flops=cost[0], bytes_accessed=cost[1], transcendentals=0),
        name=name,
    )


def shape_of(shape, dtype):
    return jax.ShapeDtypeStruct(shape, dtype)


def start_loads(place, pieces, first, width, scratch, sems, begin, rows=None):
    dp_rank, core = place[0], place[1]
    count = pieces[0].shape[0]
    copies = []
    for index, piece in enumerate(pieces):
        kind = index % 5
        flip = min(kind, 3)
        half = core if index < 5 else 1 - core
        row = (dp_rank ^ flip) * count + (count // 2 if kind == 4 else 0)
        copies.append(
            pltpu.make_async_copy(
                piece.at[:, pl.ds(first, width)],
                scratch.at[
                    pl.ds(pl.multiple_of(row, count // 2), piece.shape[0]),
                    pl.ds(pl.multiple_of(half * width, 128), width),
                ],
                sems.at[begin + index],
            )
        )
    for copy in copies:
        copy.start()
    return copies


def wait_all(copies):
    for copy in copies:
        copy.wait()


def turn(values, cosine, sine):
    lane = lax.broadcasted_iota(jnp.int32, values.shape, 1)
    swapped = jnp.where(
        lane % 64 < 32, pltpu.roll(values, 96, 1), pltpu.roll(values, 32, 1)
    )
    return values * cosine + swapped * sine


def project_rows(place, hidden, cosine, sine, pieces):
    rows, width = hidden.shape
    half = 3 * width // 2

    def body(place_ref, hidden_ref, cos_ref, sin_ref, *refs):
        parts, (q_ref, kv_ref, weight, sems) = refs[:10], refs[10:]
        wait_all(start_loads(place_ref, parts, 0, half, weight, sems, 0))
        for step in range(3 * width // 256):
            mixed = mm(hidden_ref[...], weight[:, step * 256 : step * 256 + 256])
            for pair in range(2):
                column = step * 256 + pair * 128
                part = mixed[:, pair * 128 : pair * 128 + 128]
                which, lane = column // width, column % width
                if which < 2:
                    part = turn(part, cos_ref[...], sin_ref[...])
                if which == 0:
                    q_ref[:, lane : lane + 128] = (
                        part.astype(jnp.bfloat16).astype(jnp.float32) * HEAD**-0.5
                    ).astype(jnp.bfloat16)
                else:
                    kv_ref[which - 1, :, lane : lane + 128] = part.astype(jnp.bfloat16)

    return kernel_call(
        body,
        [shape_of((rows, width), jnp.bfloat16), shape_of((2, rows, width), jnp.bfloat16)],
        [in_smem()] + [in_vmem()] * 3 + [anywhere()] * 10,
        [pltpu.VMEM((width, 3 * width), jnp.bfloat16), pltpu.SemaphoreType.DMA((10,))],
        32,
        (6 * rows * width * width, 6 * width * width + 8 * rows * width),
        "project_rows",
    )(place, hidden, cosine, sine, *pieces)


def attend_rows(queries, blocks, seg_column, seg_row):
    rows, width = queries.shape
    keys = 4 * rows

    def body(col_ref, row_ref, q_ref, b0, b1, b2, b3, out_ref, bias):
        @pl.when(pl.program_id(0) == 0)
        def _():
            bias[...] = jnp.where(col_ref[...] == row_ref[...], 0.0, NEG)

        lane = lax.broadcasted_iota(jnp.int32, (rows, 128), 1)
        query = q_ref[...]
        key = jnp.concatenate([b[0] for b in (b0, b1, b2, b3)], axis=0)
        value = jnp.concatenate([b[1] for b in (b0, b1, b2, b3)], axis=0)
        results = []
        for head in range(2):
            own = (lane < 64) if head == 0 else (lane >= 64)
            scores = mm(jnp.where(own, query, jnp.zeros_like(query)), key, NT) + bias[...]
            top = jnp.max(scores, axis=1, keepdims=True)
            exponent = jnp.exp(scores - top)
            total = jnp.sum(exponent, axis=1, keepdims=True)
            results.append(mm(exponent.astype(jnp.bfloat16), value) / total)
        out_ref[...] = jnp.where(lane < 64, results[0], results[1]).astype(jnp.bfloat16)

    block = pl.BlockSpec((2, rows, 128), lambda j: (0, 0, j))
    return kernel_call(
        body,
        [shape_of((rows, width), jnp.bfloat16)],
        [
            pl.BlockSpec((rows, 1), lambda j: (0, 0)),
            pl.BlockSpec((1, keys), lambda j: (0, 0)),
            pl.BlockSpec((rows, 128), lambda j: (0, j)),
            block, block, block, block,
        ],
        [pltpu.VMEM((rows, keys), jnp.float32)],
        48,
        (16 * rows * keys * width, 24 * rows * width),
        "attend_rows",
        [pl.BlockSpec((rows, 128), lambda j: (0, j))],
        (width // 128,),
    )(seg_column, seg_row, queries, *blocks)[0]


def attend_rows_back(queries, blocks, seg_row, seg_column, incoming):
    rows, width = queries.shape
    keys = 4 * rows

    def body(row_ref, col_ref, q_ref, in_ref, b0, b1, b2, b3, dq_ref, own_ref, z_ref, core_ref, bias):
        @pl.when(pl.program_id(0) == 0)
        def _():
            bias[...] = jnp.where(col_ref[...] == row_ref[...], 0.0, NEG)

        lane = lax.broadcasted_iota(jnp.int32, (rows, 128), 1)
        query, given = q_ref[...], in_ref[...]
        key = jnp.concatenate([b[0] for b in (b0, b1, b2, b3)], axis=0)
        value = jnp.concatenate([b[1] for b in (b0, b1, b2, b3)], axis=0)
        key_t = key.T
        dkeys, dvalues, dqueries = [], [], []
        for head in range(2):
            own = (lane < 64) if head == 0 else (lane >= 64)
            scores = mm(key, jnp.where(own, query, jnp.zeros_like(query)), NT) + bias[...]
            exponent = jnp.exp(scores - jnp.max(scores, axis=0, keepdims=True))
            probs = exponent * (1.0 / jnp.sum(exponent, axis=0, keepdims=True))
            dvalues.append(mm(probs.astype(jnp.bfloat16), given))
            dprobs = probs * mm(value, jnp.where(own, given, jnp.zeros_like(given)), NT)
            dscores = dprobs - probs * jnp.sum(dprobs, axis=0, keepdims=True)
            dscores = dscores.astype(jnp.bfloat16)
            dkeys.append(mm(dscores, query))
            dqueries.append(mm(key_t[64 * head : 64 * head + 64], dscores))
        dq_ref[...] = jnp.concatenate(dqueries, axis=0).T * HEAD**-0.5
        wide = lax.broadcasted_iota(jnp.int32, (keys, 128), 1) < 64
        for which, pair in enumerate((dkeys, dvalues)):
            both = jnp.where(wide, pair[0], pair[1]).astype(jnp.bfloat16)
            own_ref[which] = both[:rows]
            core_ref[0, which] = both[rows : 2 * rows]
            z_ref[which] = both[2 * rows : 3 * rows]
            core_ref[1, which] = both[3 * rows :]

    block = pl.BlockSpec((2, rows, 128), lambda j: (0, 0, j))
    columns = pl.BlockSpec((rows, 128), lambda j: (0, j))
    pair_shape = shape_of((2, rows, width), jnp.bfloat16)
    return kernel_call(
        body,
        [
            shape_of((rows, width), jnp.float32),
            pair_shape,
            pair_shape,
            shape_of((2, 2, rows, width), jnp.bfloat16),
        ],
        [
            pl.BlockSpec((1, rows), lambda j: (0, 0)),
            pl.BlockSpec((keys, 1), lambda j: (0, 0)),
            columns, columns, block, block, block, block,
        ],
        [pltpu.VMEM((keys, rows), jnp.float32)],
        56,
        (40 * rows * keys * width, 48 * rows * width),
        "attend_rows_back",
        [columns, block, block, pl.BlockSpec((2, 2, rows, 128), lambda j: (0, 0, 0, j))],
        (width // 128,),
    )(seg_row, seg_column, queries, incoming, *blocks)


def unit_of(resid):
    centred = resid - jnp.mean(resid, axis=1, keepdims=True)
    scaling = lax.rsqrt(jnp.mean(centred * centred, axis=1, keepdims=True) + EPS)
    return centred * scaling, scaling


def norm_rows_back(incoming, unit, scaling, gain):
    scaled = incoming * gain
    return scaling * (
        scaled
        - jnp.mean(scaled, axis=1, keepdims=True)
        - unit * jnp.mean(scaled * unit, axis=1, keepdims=True)
    )


FF_STEP = 512


def mlp_scratch(width, hidden_width):
    return [
        pltpu.VMEM((width, width), jnp.bfloat16),
        pltpu.VMEM((width, hidden_width), jnp.bfloat16),
        pltpu.VMEM((width, hidden_width), jnp.bfloat16),
        pltpu.VMEM((hidden_width, width), jnp.bfloat16),
        pltpu.VMEM((width, 256), jnp.bfloat16),
        pltpu.VMEM((128, width), jnp.float32),
        pltpu.SemaphoreType.DMA((50,)),
    ]


def mlp_rows(place, hidden, attended, first_parts, gate_up_parts, down_parts):
    rows, width = hidden.shape
    ff_half = gate_up_parts[0].shape[1] // 2
    ff = 2 * ff_half

    def body(place_ref, hidden_ref, att_ref, *refs):
        parts, rest = refs[:30], refs[30:]
        out_ref, one_ref, two_ref, acts_ref, gate_ref, up_ref = rest[:6]
        w_out, w_gate, w_up, w_down, w_norm, norm_ref, sems = rest[6:]
        normed_ref = acts_ref.at[:, :width]
        norm_loads = start_loads(place_ref, parts[:10], 2 * width, 128, w_norm, sems, 40)
        loads = [
            start_loads(place_ref, parts[:10], 3 * width // 2, width // 2, w_out, sems, 0),
            start_loads(place_ref, parts[10:20], 0, ff_half, w_gate, sems, 10),
            start_loads(place_ref, parts[10:20], ff_half, ff_half, w_up, sems, 20),
            start_loads(place_ref, parts[20:30], 0, width // 2, w_down, sems, 30),
        ]
        wait_all(norm_loads)
        norm_ref[...] = w_norm[:, :128].astype(jnp.float32).T
        wait_all(loads[0])
        resid = hidden_ref[...].astype(jnp.float32) + mm(att_ref[...], w_out[...])
        one_ref[...] = resid
        normed = unit_of(resid)[0] * norm_ref[0:1] + norm_ref[1:2]
        normed_ref[...] = normed.astype(jnp.bfloat16)
        two_ref[...] = normed
        wait_all(loads[1])
        wait_all(loads[2])
        wait_all(loads[3])

        @pl.loop(0, ff // FF_STEP)
        def _(step):
            span = pl.ds(pl.multiple_of(step * FF_STEP, FF_STEP), FF_STEP)
            gate = mm(normed_ref[...], w_gate[:, span])
            up = mm(normed_ref[...], w_up[:, span])
            gate_ref[:, span] = gate
            up_ref[:, span] = up
            middle = (gate * jax.nn.sigmoid(gate) * up).astype(jnp.bfloat16)
            acts_ref[:, pl.ds(pl.multiple_of(width + step * FF_STEP, 128), FF_STEP)] = middle
            two_ref[...] += mm(middle, w_down[span, :])

        out_ref[...] = (unit_of(two_ref[...])[0] * norm_ref[2:3] + norm_ref[3:4]).astype(jnp.bfloat16)

    return kernel_call(
        body,
        [
            shape_of((rows, width), jnp.bfloat16),
            shape_of((rows, width), jnp.float32),
            shape_of((rows, width), jnp.float32),
            shape_of((rows, width + ff), jnp.bfloat16),
            shape_of((rows, ff), jnp.float32),
            shape_of((rows, ff), jnp.float32),
        ],
        [in_smem()] + [in_vmem()] * 2 + [anywhere()] * 30,
        mlp_scratch(width, ff),
        56,
        (2 * rows * width * (width + 3 * ff), 2 * width * (width + 3 * ff)),
        "mlp_rows",
    )(place, hidden, attended, *first_parts, *gate_up_parts, *down_parts)


def mlp_rows_back(place, incoming, one, two, gate, up, first_parts, gate_up_parts, down_parts):
    rows, width = incoming.shape
    ff_half = gate_up_parts[0].shape[1] // 2
    ff = 2 * ff_half

    def body(place_ref, in_ref, one_ref, two_ref, gate_ref, up_ref, *refs):
        parts, rest = refs[:30], refs[30:]
        keep_ref, send_ref, dresid_ref, datt_ref, sums_ref = rest[:5]
        w_out, w_gate, w_up, w_down, w_norm, norm_ref, sems, low_ref = rest[5:]
        core = place_ref[1]
        norm_loads = start_loads(place_ref, parts[:10], 2 * width, 128, w_norm, sems, 40)

        def share(half, columns, value):
            @pl.when(half == core)
            def _():
                keep_ref[:, columns] = value

            @pl.when(half != core)
            def _():
                send_ref[:, columns] = value

        loads = [
            start_loads(place_ref, parts[20:30], 0, width // 2, w_down, sems, 30),
            start_loads(place_ref, parts[10:20], 0, ff_half, w_gate, sems, 10),
            start_loads(place_ref, parts[10:20], ff_half, ff_half, w_up, sems, 20),
            start_loads(place_ref, parts[:10], 3 * width // 2, width // 2, w_out, sems, 0),
        ]
        wait_all(norm_loads)
        norm_ref[...] = w_norm[:, :128].astype(jnp.float32).T
        sums_ref[...] = jnp.zeros_like(sums_ref)
        given = in_ref[...].astype(jnp.float32)
        unit, scaling = unit_of(two_ref[...])
        sums_ref[2:3] = jnp.sum(given * unit, axis=0, keepdims=True)
        sums_ref[3:4] = jnp.sum(given, axis=0, keepdims=True)
        dresid_two = norm_rows_back(given, unit, scaling, norm_ref[2:3])
        dresid_ref[...] = dresid_two
        low_ref[...] = dresid_two.astype(jnp.bfloat16)
        for half in range(2):
            span = slice(half * width // 2, (half + 1) * width // 2)
            share(half, slice(ff, ff + width // 2), low_ref[:, span])
        for copies in loads:
            wait_all(copies)

        @pl.loop(0, ff // FF_STEP)
        def _(step):
            span = pl.ds(pl.multiple_of(step * FF_STEP, FF_STEP), FF_STEP)
            dmiddle = mm(low_ref[...], w_down[span, :], NT)
            gate_block = gate_ref[:, span]
            sig = jax.nn.sigmoid(gate_block)
            dgate = (dmiddle * up_ref[:, span] * sig * (1.0 + gate_block * (1.0 - sig))).astype(jnp.bfloat16)
            dup = (dmiddle * (gate_block * sig)).astype(jnp.bfloat16)
            half, column = step // (ff_half // FF_STEP), step % (ff_half // FF_STEP) * FF_STEP
            share(half, pl.ds(pl.multiple_of(column, 128), FF_STEP), dgate)
            share(half, pl.ds(pl.multiple_of(column + ff_half, 128), FF_STEP), dup)
            dresid_ref[...] += mm(dgate, w_gate[:, span], NT) + mm(dup, w_up[:, span], NT)

        dnormed = dresid_ref[...]
        unit, scaling = unit_of(one_ref[...])
        sums_ref[0:1] = jnp.sum(dnormed * unit, axis=0, keepdims=True)
        sums_ref[1:2] = jnp.sum(dnormed, axis=0, keepdims=True)
        dresid_one = norm_rows_back(dnormed, unit, scaling, norm_ref[0:1])
        dresid_ref[...] = dresid_one
        low_ref[...] = dresid_one.astype(jnp.bfloat16)
        for half in range(2):
            span = slice(half * width // 2, (half + 1) * width // 2)
            share(half, slice(ff + width // 2, ff + width), low_ref[:, span])
        datt_ref[...] = mm(low_ref[...], w_out[...], NT).astype(jnp.bfloat16)

    return kernel_call(
        body,
        [
            shape_of((rows, ff + width), jnp.bfloat16),
            shape_of((rows, ff + width), jnp.bfloat16),
            shape_of((rows, width), jnp.float32),
            shape_of((rows, width), jnp.bfloat16),
            shape_of((8, width), jnp.float32),
        ],
        [in_smem()] + [in_vmem()] * 5 + [anywhere()] * 30,
        mlp_scratch(width, ff) + [pltpu.VMEM((rows, width), jnp.bfloat16)],
        56,
        (2 * rows * width * (width + 3 * ff), 2 * width * (width + 3 * ff)),
        "mlp_rows_back",
    )(place, incoming, one, two, gate, up, *first_parts, *gate_up_parts, *down_parts)


def project_rows_back(place, dqueries, sums, dresid_one, cosine, sine, pieces):
    rows, width = dqueries.shape
    half = 3 * width // 2
    count = len(sums)

    def body(place_ref, dq_ref, resid_ref, cos_ref, sin_ref, *refs):
        parts, rest = refs[:10], refs[10:]
        sum_refs, (keep_ref, send_ref, dhidden_ref, weight, sems, dmixed_ref) = rest[:count], rest[count:]
        core = place_ref[1]
        loads = start_loads(place_ref, parts, 0, half, weight, sems, 0)
        for column in range(0, 3 * width, 128):
            which, lane = column // width, column % width
            span = slice(lane, lane + 128)
            if which == 0:
                part = dq_ref[:, span]
            else:
                part = sum(ref[which - 1, :, span].astype(jnp.float32) for ref in sum_refs)
            if which < 2:
                part = turn(part, cos_ref[...], -sin_ref[...])
            dmixed_ref[:, column : column + 128] = part.astype(jnp.bfloat16)
        for index in range(2):
            @pl.when(core == index)
            def _():
                keep_ref[...] = dmixed_ref[:, index * half : (index + 1) * half]
                send_ref[...] = dmixed_ref[:, (1 - index) * half : (2 - index) * half]

        wait_all(loads)
        dhidden_ref[...] = resid_ref[...] + mm(dmixed_ref[...], weight[...], NT)

    return kernel_call(
        body,
        [
            shape_of((rows, half), jnp.bfloat16),
            shape_of((rows, half), jnp.bfloat16),
            shape_of((rows, width), jnp.float32),
        ],
        [in_smem()] + [in_vmem()] * 4 + [anywhere()] * 10 + [in_vmem()] * count,
        [
            pltpu.VMEM((width, 3 * width), jnp.bfloat16),
            pltpu.SemaphoreType.DMA((10,)),
            pltpu.VMEM((rows, 3 * width), jnp.bfloat16),
        ],
        48,
        (6 * rows * width * width, 6 * width * width + 8 * rows * width),
        "project_rows_back",
    )(place, dqueries, dresid_one, cosine, sine, *pieces, *sums)


def grad_parts(place, lefts, rights, left_span, right_span, sums=()):
    rows = lefts[0].shape[0]
    depth = left_span[1] - left_span[0]
    width = right_span[1] - right_span[0]
    extra = 128 if sums else 0
    count = depth // 4
    tile = min(width, 512) if width % 512 == 0 else 384

    def body(place_ref, l0, l1, r0, r1, *refs):
        sum_refs, refs = refs[: len(sums)], refs[len(sums) :]
        own_ref, x_ref, y_ref, xl_ref, yu_ref, left_t, right, block = refs[:8]
        left_t[:, :rows] = l0[:, left_span[0] : left_span[1]].T
        left_t[:, rows:] = l1[:, left_span[0] : left_span[1]].T
        right[:rows] = r0[:, right_span[0] : right_span[1]]
        right[rows:] = r1[:, right_span[0] : right_span[1]]
        if sums:
            padded, turned = refs[8:]
            padded[...] = jnp.zeros_like(padded)
            padded[:8] = sum_refs[0][...] + sum_refs[1][...]
            turned[...] = padded[...].T
        upper, lower = slice(0, count // 2), slice(count // 2, count)
        for flip in range(4):
            begin = pl.multiple_of((place_ref[0] ^ flip) * count, count)
            for column in range(0, width, tile):
                span = slice(column, column + tile)
                block[:, span] = mm(left_t[pl.ds(begin, count), :], right[:, span]).astype(jnp.bfloat16)
            if sums:
                block[:, width:] = turned[pl.ds(begin, count), :].astype(jnp.bfloat16)
            if flip == 0:
                own_ref[...] = block[...]
            elif flip == 1:
                x_ref[upper] = block[upper]
                xl_ref[...] = block[lower]
            elif flip == 2:
                y_ref[upper] = block[lower]
                yu_ref[...] = block[upper]
            else:
                x_ref[lower] = block[upper]
                y_ref[lower] = block[lower]

    out_width = width + extra
    return kernel_call(
        body,
        [
            shape_of((count, out_width), jnp.bfloat16),
            shape_of((count, out_width), jnp.bfloat16),
            shape_of((count, out_width), jnp.bfloat16),
            shape_of((count // 2, out_width), jnp.bfloat16),
            shape_of((count // 2, out_width), jnp.bfloat16),
        ],
        [in_smem()] + [in_vmem()] * (4 + len(sums)),
        [
            pltpu.VMEM((depth, 2 * rows), jnp.bfloat16),
            pltpu.VMEM((2 * rows, width), jnp.bfloat16),
            pltpu.VMEM((count, out_width), jnp.bfloat16),
        ]
        + ([pltpu.VMEM((128, depth), jnp.float32), pltpu.VMEM((depth, 128), jnp.float32)] if sums else []),
        56,
        (4 * rows * depth * width, 4 * rows * (depth + width) + 2 * depth * width),
        "grad_parts",
    )(place, *lefts, *rights, *sums)


def to_core(value, pairs=((0, 1), (1, 0))):
    return lax.ppermute(value, "section", list(pairs))


def along_x(value):
    return lax.ppermute(value, "dp", [(i, i ^ 1) for i in range(4)])


def along_y(value):
    return lax.ppermute(value, "dp", [(i, i ^ 2) for i in range(4)])


def along_z(value):
    return lax.ppermute(value, "ctx", [(i, i ^ 1) for i in range(4)])


def z_swap(value):
    pairs = [(4 + i, 4 + (i ^ 2)) for i in range(4)]
    return lax.ppermute(value, ("section", "ctx"), pairs)


def lowered(value):
    return value.astype(jnp.bfloat16)


def wide(value):
    return value.astype(jnp.float32)


def by_core(core, mine, theirs, axis):
    return jnp.where(
        core == 0,
        jnp.concatenate([mine, theirs], axis=axis),
        jnp.concatenate([theirs, mine], axis=axis),
    )


def half_of(array, which):
    width = array.shape[-1] // 2
    return lax.dynamic_slice_in_dim(array, which * width, width, array.ndim - 1)


def gathered(piece):
    rows = piece.shape[0] // 2
    from_x, from_y = along_x(piece), along_y(piece)
    upper, lower = along_x(from_y[:rows]), along_y(from_x[rows:])
    mine = [piece, from_x, from_y, upper, lower]
    return mine + [to_core(part) for part in mine]


def reduced(parts, ctx_rank):
    own, x_message, y_message, x_lower, y_upper = parts
    rows = own.shape[0] // 2
    from_x, from_y = along_x(x_message), along_y(y_message)
    x_last = along_x(lowered(wide(x_lower) + wide(from_y[rows:])))
    y_last = along_y(lowered(wide(y_upper) + wide(from_x[rows:])))
    summed = lowered(
        wide(own)
        + jnp.concatenate(
            [wide(from_x[:rows]) + wide(y_last), wide(from_y[:rows]) + wide(x_last)], axis=0
        )
    )
    inner = lax.ppermute(summed, "ctx", [(0, 1), (3, 2)])
    pair = lowered(wide(summed) + wide(inner))
    across = lax.ppermute(pair, "ctx", [(1, 2), (2, 1)])
    total = lowered(wide(pair) + wide(across))
    outer = lax.ppermute(total, "ctx", [(1, 0), (2, 3)])
    return jnp.where((ctx_rank == 0) | (ctx_rank == 3), outer, total)


def paired_on_device(
    tokens,
    seg_ids,
    query_key_value_weight,
    output_weight,
    gate_weight,
    up_weight,
    down_weight,
    norm1_gain,
    norm1_bias,
    norm2_gain,
    norm2_bias,
    cotangent,
):
    core, ctx_rank, dp_rank = (lax.axis_index(a) for a in ("section", "ctx", "dp"))
    span, width = tokens.shape[1], tokens.shape[2]
    sequence = ctx_rank // 2
    block = ctx_rank ^ (2 * core)
    place = jnp.stack([dp_rank, core]).astype(jnp.int32)
    pick = lambda array, index: lax.dynamic_index_in_dim(array, index, 0, keepdims=False)

    def rows_of(array):
        return jnp.where(core == 0, pick(array, sequence), z_swap(pick(array, 1 - sequence)))

    norm_columns = jnp.concatenate([norm1_gain, norm1_bias, norm2_gain, norm2_bias], axis=0).T
    norm_columns = jnp.pad(norm_columns, ((0, 0), (0, 124)))

    def packs(which):
        return (
            jnp.concatenate(
                [half_of(query_key_value_weight[0], which), half_of(output_weight[0], which), norm_columns],
                axis=1,
            ),
            jnp.concatenate([half_of(gate_weight[0], which), half_of(up_weight[0], which)], axis=1),
            half_of(down_weight[0], which),
        )

    own_packs = packs(core)
    sent_packs = [to_core(pack) for pack in packs(1 - core)]
    weights = [
        [gathered(jnp.where(core == layer, own, sent)) for own, sent in zip(own_packs, sent_packs)]
        for layer in range(2)
    ]

    seg = pick(seg_ids, sequence)
    seg_rows = lax.dynamic_slice_in_dim(seg, block * span, span, 0)
    seg_keys = jnp.concatenate(
        [lax.dynamic_slice_in_dim(seg, (block ^ flip) * span, span, 0) for flip in (0, 2, 1, 3)]
    )
    begins = jnp.sum((seg[None, :] < seg_rows[:, None]).astype(jnp.int32), axis=1)
    places = block * span + jnp.arange(span, dtype=jnp.int32) - begins
    lanes = jnp.arange(128, dtype=jnp.int32) % HEAD
    half = HEAD // 2
    spread = 1000.0 ** (-2.0 * (lanes % half).astype(jnp.float32) / HEAD)
    angles = places.astype(jnp.float32)[:, None] * spread[None, :]
    cosine, sine = jnp.cos(angles), jnp.where(lanes < half, -1.0, 1.0) * jnp.sin(angles)

    hidden = rows_of(tokens)
    incoming = rows_of(cotangent)
    kept, outputs = [], []
    for layer in range(2):
        first, gate_up, down = weights[layer]
        queries, own = project_rows(place, hidden, cosine, sine, first)
        from_z = along_z(own)
        blocks = [own, to_core(own), from_z, to_core(from_z)]
        attended = attend_rows(queries, blocks, seg_rows[:, None], seg_keys[None, :])
        output, one, two, acts, gate, up = mlp_rows(place, hidden, attended, first, gate_up, down)
        kept.append((hidden, queries, blocks, attended, one, two, acts, gate, up))
        outputs.append(output)
        hidden = output

    totals, input_rows = [None, None], [None, None]
    ff = acts.shape[1] - width
    for layer in (1, 0):
        first, gate_up, down = weights[layer]
        hidden, queries, blocks, attended, one, two, acts, gate, up = kept[layer]
        both = lambda value: (value, to_core(value))
        keep, send, dresid_one, dattended, sums = mlp_rows_back(
            place, incoming, one, two, gate, up, first, gate_up, down
        )
        right = (keep, to_core(send))
        acts = both(acts)
        low = lambda value: (value, wide(to_core(lowered(value))))
        totals[layer] = [
            reduced(grad_parts(place, acts, right, (0, width), (0, ff)), ctx_rank),
            reduced(grad_parts(place, acts, right, (width, width + ff), (ff, ff + width // 2)), ctx_rank),
            reduced(
                grad_parts(
                    place, both(attended), right, (0, width), (ff + width // 2, ff + width), low(sums)
                ),
                ctx_rank,
            ),
        ]
        dqueries, own, near, across = attend_rows_back(
            queries, blocks, seg_rows[None, :], seg_keys[:, None], dattended
        )
        across = to_core(across)
        from_z = along_z(lowered(wide(near) + wide(across[1])))
        keep, send, dhidden = project_rows_back(
            place, dqueries, (own, across[0], from_z), dresid_one, cosine, sine, first
        )
        totals[layer].append(
            reduced(
                grad_parts(place, both(hidden), (keep, to_core(send)), (0, width), (0, 3 * width // 2)),
                ctx_rank,
            )
        )
        input_rows[layer] = dhidden
        incoming = lowered(dhidden)

    def whole(first, second):
        from_first = to_core(first, ((1, 0),))
        from_second = to_core(second, ((0, 1),))
        return jnp.where(core == 0, first, second), jnp.where(core == 0, from_first, from_second)

    pairs = [whole(first, second) for first, second in zip(*totals)]
    joined = lambda index, begin, end: wide(
        by_core(core, pairs[index][0][:, begin:end], pairs[index][1][:, begin:end], 1)
    )[None]
    norm_grads = wide(pairs[2][0][:, width // 2 : width // 2 + 4]).T

    def placed_rows(first, second):
        first, second = lowered(first), lowered(second)
        near = jnp.where(core == 0, first, to_core(second, ((0, 1),)))
        swapped = z_swap(jnp.stack([first, second]))
        far = jnp.where(core == 0, to_core(swapped[0], ((1, 0),)), swapped[1])
        return jnp.where(sequence == 0, jnp.stack([near, far]), jnp.stack([far, near]))[None]

    return (
        placed_rows(*outputs),
        wide(placed_rows(*input_rows)),
        joined(3, 0, 3 * width // 2),
        joined(2, 0, width // 2),
        joined(0, 0, ff // 2),
        joined(0, ff // 2, ff),
        joined(1, 0, width // 2),
        *(norm_grads[i : i + 1] for i in range(4)),
    )


def solution(mesh):
    placed = (
        P("dp", "ctx", None),
        P("dp", None),
        P("section", "dp", None),
        P("section", "dp", None),
        P("section", "dp", None),
        P("section", "dp", None),
        P("section", "dp", None),
        P("section", "dp"),
        P("section", "dp"),
        P("section", "dp"),
        P("section", "dp"),
        P("dp", "ctx", None),
    )
    paired = mesh.shape["section"] == 2 and mesh.shape["ctx"] == 4 and mesh.shape["dp"] == 4
    return jax.shard_map(
        paired_on_device if paired else relay_on_device,
        mesh=mesh,
        in_specs=placed,
        out_specs=(
            P("section", "dp", "ctx", None),
            P("section", "dp", "ctx", None),
            P("section", "dp", None),
            P("section", "dp", None),
            P("section", "dp", None),
            P("section", "dp", None),
            P("section", "dp", None),
            P("section", "dp"),
            P("section", "dp"),
            P("section", "dp"),
            P("section", "dp"),
        ),
        check_vma=False,
    )
```

```python
import jax
import jax.numpy as jnp
from jax import lax
from jax.experimental import pallas as pl
from jax.experimental.pallas import tpu as pltpu
from jax.sharding import PartitionSpec as P

HEAD = 64
MICRO = 2


EPS = 1e-05
NEG = -1e30


def passed_along(value, axis, steps):
    count = lax.axis_size(axis)
    first, last = (max(0, -steps), min(count, count - steps))
    return lax.ppermute(value, axis, [(source, source + steps) for source in range(first, last)])


def for_sending(array):
    return jax.tree.map(lambda a: a.astype(jnp.bfloat16) if a.dtype == jnp.float32 else a, array)


def positions(seg_ids):
    places = lax.broadcasted_iota(jnp.int32, seg_ids.shape, 1)
    begins = jnp.concatenate(
        [jnp.ones_like(seg_ids[:, :1]), (seg_ids[:, 1:] != seg_ids[:, :-1]).astype(jnp.int32)],
        axis=1,
    )
    return places - lax.cummax(places * begins, axis=1)


def rope_tables(places, half_dim):
    spread = 1000.0 ** (-2.0 * jnp.arange(half_dim, dtype=jnp.float32) / (2 * half_dim))
    angles = places.astype(jnp.float32)[..., None] * spread
    return (jnp.cos(angles), jnp.sin(angles))


def rotate(values, cosine, sine_table):
    half_dim = values.shape[-1] // 2
    former, latter = (values[..., :half_dim], values[..., half_dim:])
    cosine, sine_table = (cosine[..., None, :], sine_table[..., None, :])
    return jnp.concatenate(
        [former * cosine - latter * sine_table, latter * cosine + former * sine_table], axis=-1
    )


def unrotate(values, cosine, sine_table):
    half_dim = values.shape[-1] // 2
    former, latter = (values[..., :half_dim], values[..., half_dim:])
    cosine, sine_table = (cosine[..., None, :], sine_table[..., None, :])
    return jnp.concatenate(
        [former * cosine + latter * sine_table, latter * cosine - former * sine_table], axis=-1
    )


def norm_parts(resid, gain, bias):
    centred = resid - jnp.mean(resid, axis=-1, keepdims=True)
    scaling = lax.rsqrt(jnp.mean(centred * centred, axis=-1, keepdims=True) + EPS)
    unit_rows = centred * scaling
    return (unit_rows * gain + bias, unit_rows, scaling)


def norm_back(incoming, unit_rows, scaling, gain):
    scaled = incoming * gain
    inner = (
        scaled
        - jnp.mean(scaled, axis=-1, keepdims=True)
        - unit_rows * jnp.mean(scaled * unit_rows, axis=-1, keepdims=True)
    )
    return (
        scaling * inner,
        jnp.sum(incoming * unit_rows, axis=(0, 1)),
        jnp.sum(incoming, axis=(0, 1)),
    )


def masked_scores(queries, all_keys, seg_rows, seg_keys):
    row_count, model_width = queries.shape
    head_count = model_width // HEAD
    scores = jnp.einsum(
        "qhd,khd->hqk",
        queries.reshape(row_count, head_count, HEAD),
        all_keys.reshape(all_keys.shape[0], head_count, HEAD),
        preferred_element_type=jnp.float32,
    ) * HEAD ** (-0.5)
    return jnp.where((seg_rows[:, None] == seg_keys[None, :])[None], scores, NEG)


def attend(operands):
    queries, all_keys, all_values, seg_rows, seg_keys = operands
    row_count, model_width = queries.shape
    head_count = model_width // HEAD
    scores = masked_scores(queries, all_keys, seg_rows, seg_keys)
    row_max = jnp.max(scores, axis=-1, keepdims=True)
    exponent = jnp.exp(scores - row_max)
    row_sum = jnp.sum(exponent, axis=-1, keepdims=True)
    probs_low = (exponent / row_sum).astype(jnp.bfloat16)
    result = jnp.einsum(
        "hqk,khd->qhd",
        probs_low,
        all_values.reshape(all_values.shape[0], head_count, HEAD),
        preferred_element_type=jnp.float32,
    )
    return (result.reshape(row_count, model_width), (row_max + jnp.log(row_sum))[..., 0])


def attend_back(operands):
    queries, all_keys, all_values, seg_rows, seg_keys, log_sum, incoming = operands
    row_count, model_width = queries.shape
    head_count = model_width // HEAD
    key_count = all_keys.shape[0]
    probs = jnp.exp(masked_scores(queries, all_keys, seg_rows, seg_keys) - log_sum[..., None])
    heads_in = incoming.reshape(row_count, head_count, HEAD)
    dprobs = jnp.einsum(
        "qhd,khd->hqk",
        heads_in,
        all_values.reshape(key_count, head_count, HEAD),
        preferred_element_type=jnp.float32,
    )
    dscores = (probs * (dprobs - jnp.sum(probs * dprobs, axis=-1, keepdims=True))).astype(
        jnp.bfloat16
    )
    dquery = jnp.einsum(
        "hqk,khd->qhd",
        dscores,
        all_keys.reshape(key_count, head_count, HEAD),
        preferred_element_type=jnp.float32,
    ) * HEAD ** (-0.5)
    dkeys_part = jnp.einsum(
        "hqk,qhd->khd",
        dscores,
        queries.reshape(row_count, head_count, HEAD),
        preferred_element_type=jnp.float32,
    ) * HEAD ** (-0.5)
    dvalue = jnp.einsum(
        "hqk,qhd->khd", probs.astype(jnp.bfloat16), heads_in, preferred_element_type=jnp.float32
    )
    return (
        dquery.reshape(row_count, model_width),
        dkeys_part.reshape(key_count, model_width),
        dvalue.reshape(key_count, model_width),
    )


def layer_forward(hidden_state, weights_full, seg_rows, seg_keys, cosine, sine_table):
    query_key_value_weight, output_weight, gate_weight, up_weight, down_weight, norm_params = (
        weights_full
    )
    model_width = hidden_state.shape[-1]
    shaped = hidden_state.shape[:2] + (model_width // HEAD, HEAD)
    mixed_query_key_value = jnp.einsum(
        "bld,de->ble", hidden_state, query_key_value_weight, preferred_element_type=jnp.float32
    )
    queries = (
        rotate(mixed_query_key_value[..., :model_width].reshape(shaped), cosine, sine_table)
        .reshape(hidden_state.shape)
        .astype(jnp.bfloat16)
    )
    key_rows = (
        rotate(
            mixed_query_key_value[..., model_width : 2 * model_width].reshape(shaped),
            cosine,
            sine_table,
        )
        .reshape(hidden_state.shape)
        .astype(jnp.bfloat16)
    )
    value_rows = mixed_query_key_value[..., 2 * model_width :].astype(jnp.bfloat16)
    all_keys, all_values = (
        lax.all_gather(key_rows, "ctx", axis=1, tiled=True),
        lax.all_gather(value_rows, "ctx", axis=1, tiled=True),
    )
    attention_output, log_sum = lax.map(attend, (queries, all_keys, all_values, seg_rows, seg_keys))
    attention_output = attention_output.astype(jnp.bfloat16)
    residual_first = hidden_state.astype(jnp.float32) + jnp.einsum(
        "bld,de->ble", attention_output, output_weight, preferred_element_type=jnp.float32
    )
    normalized_rows, unit_one, scale_one = norm_parts(
        residual_first, norm_params[0], norm_params[1]
    )
    normalized_lowered = normalized_rows.astype(jnp.bfloat16)
    gate_projected = jnp.einsum(
        "bld,df->blf", normalized_lowered, gate_weight, preferred_element_type=jnp.float32
    )
    up_projected = jnp.einsum(
        "bld,df->blf", normalized_lowered, up_weight, preferred_element_type=jnp.float32
    )
    middle_state = (gate_projected * jax.nn.sigmoid(gate_projected) * up_projected).astype(
        jnp.bfloat16
    )
    residual_second = normalized_rows + jnp.einsum(
        "blf,fd->bld", middle_state, down_weight, preferred_element_type=jnp.float32
    )
    output, unit_two, scale_two = norm_parts(residual_second, norm_params[2], norm_params[3])
    extra = (all_keys, all_values)
    kept = (
        hidden_state,
        queries,
        key_rows,
        value_rows,
        log_sum,
        attention_output,
        unit_one,
        scale_one,
        gate_projected,
        up_projected,
        unit_two,
        scale_two,
    ) + extra
    return (output, kept)


def layer_backward(incoming, kept, weights_full, seg_rows, seg_keys, cosine, sine_table):
    query_key_value_weight, output_weight, gate_weight, up_weight, down_weight, norm_params = (
        weights_full
    )
    (
        hidden_state,
        queries,
        key_rows,
        value_rows,
        log_sum,
        attention_output,
        unit_one,
        scale_one,
        gate_projected,
        up_projected,
        unit_two,
        scale_two,
    ) = kept[:12]
    all_keys, all_values = (kept[12], kept[13])
    dresid_two, dgain_two, dbias_two = norm_back(incoming, unit_two, scale_two, norm_params[2])
    normalized_lowered = (unit_one * norm_params[0] + norm_params[1]).astype(jnp.bfloat16)
    sigmoid_gate = jax.nn.sigmoid(gate_projected)
    swish_gate = gate_projected * sigmoid_gate
    middle_state = (swish_gate * up_projected).astype(jnp.bfloat16)
    dout_two = dresid_two.astype(jnp.bfloat16)
    grad_down = jnp.einsum(
        "blf,bld->fd", middle_state, dout_two, preferred_element_type=jnp.float32
    )
    dmiddle = jnp.einsum("bld,fd->blf", dout_two, down_weight, preferred_element_type=jnp.float32)
    dgate_proj = (
        dmiddle * up_projected * sigmoid_gate * (1.0 + gate_projected * (1.0 - sigmoid_gate))
    ).astype(jnp.bfloat16)
    dup_proj = (dmiddle * swish_gate).astype(jnp.bfloat16)
    grad_gate = jnp.einsum(
        "bld,blf->df", normalized_lowered, dgate_proj, preferred_element_type=jnp.float32
    )
    grad_up = jnp.einsum(
        "bld,blf->df", normalized_lowered, dup_proj, preferred_element_type=jnp.float32
    )
    dnormed = (
        dresid_two
        + jnp.einsum("blf,df->bld", dgate_proj, gate_weight, preferred_element_type=jnp.float32)
        + jnp.einsum("blf,df->bld", dup_proj, up_weight, preferred_element_type=jnp.float32)
    )
    dresid_one, dgain_one, dbias_one = norm_back(dnormed, unit_one, scale_one, norm_params[0])
    dattn_out = dresid_one.astype(jnp.bfloat16)
    grad_out = jnp.einsum(
        "ble,bld->ed", attention_output, dattn_out, preferred_element_type=jnp.float32
    )
    dattended = jnp.einsum(
        "bld,ed->ble", dattn_out, output_weight, preferred_element_type=jnp.float32
    ).astype(jnp.bfloat16)
    dqueries, dkeys_all, dvalues_all = lax.map(
        attend_back, (queries, all_keys, all_values, seg_rows, seg_keys, log_sum, dattended)
    )
    dkey_rows, dvalue_rows = (
        lax.psum_scatter(
            dkeys_all.astype(jnp.bfloat16), "ctx", scatter_dimension=1, tiled=True
        ).astype(jnp.float32),
        lax.psum_scatter(
            dvalues_all.astype(jnp.bfloat16), "ctx", scatter_dimension=1, tiled=True
        ).astype(jnp.float32),
    )
    shaped = dqueries.shape[:2] + (dqueries.shape[2] // HEAD, HEAD)
    dmixed = jnp.concatenate(
        [
            unrotate(dqueries.reshape(shaped), cosine, sine_table).reshape(dqueries.shape),
            unrotate(dkey_rows.reshape(shaped), cosine, sine_table).reshape(dqueries.shape),
            dvalue_rows,
        ],
        axis=-1,
    ).astype(jnp.bfloat16)
    grad_qkv = jnp.einsum("bld,ble->de", hidden_state, dmixed, preferred_element_type=jnp.float32)
    dhidden = dresid_one + jnp.einsum(
        "ble,de->bld", dmixed, query_key_value_weight, preferred_element_type=jnp.float32
    )
    return (
        dhidden,
        (
            grad_qkv,
            grad_out,
            grad_gate,
            grad_up,
            grad_down,
            jnp.stack([dgain_one, dbias_one, dgain_two, dbias_two]),
        ),
    )


def relay_on_device(
    tokens,
    seg_ids,
    query_key_value_weight,
    output_weight,
    gate_weight,
    up_weight,
    down_weight,
    norm1_gain,
    norm1_bias,
    norm2_gain,
    norm2_bias,
    cotangent,
):
    leading = lax.axis_index("section") == 0
    ctx_rank = lax.axis_index("ctx")
    span_len = tokens.shape[1]
    per_micro = tokens.shape[0] // MICRO
    seg_near = lax.dynamic_slice_in_dim(seg_ids, ctx_rank * span_len, span_len, 1)
    cosine_rows, sine_rows = rope_tables(
        lax.dynamic_slice_in_dim(positions(seg_ids), ctx_rank * span_len, span_len, 1), HEAD // 2
    )
    shards = (
        query_key_value_weight[0],
        output_weight[0],
        gate_weight[0],
        up_weight[0],
        down_weight[0],
        jnp.stack([norm1_gain[0], norm1_bias[0], norm2_gain[0], norm2_bias[0]]),
    )
    gathered = (
        lax.all_gather(shards[0], "dp", axis=0, tiled=True),
        lax.all_gather(shards[1], "dp", axis=0, tiled=True),
        lax.all_gather(shards[2], "dp", axis=0, tiled=True),
        lax.all_gather(shards[3], "dp", axis=0, tiled=True),
        lax.all_gather(shards[4], "dp", axis=0, tiled=True),
        lax.all_gather(shards[5], "dp", axis=1, tiled=True),
    )
    weights_full = gathered[:5] + (gathered[5].astype(jnp.float32),)

    def select(array, micro_idx):
        return lax.dynamic_slice_in_dim(array, micro_idx * per_micro, per_micro, 0)

    delay_fwd = jnp.where(leading, 0, 1)
    received = jnp.zeros((per_micro,) + tokens.shape[1:], jnp.bfloat16)
    outputs = []
    stored = []
    for tick_no in range(MICRO + 1):
        micro_idx = jnp.clip(tick_no - delay_fwd, 0, MICRO - 1)
        hidden_state = jnp.where(leading, select(tokens, micro_idx), received)
        output, kept = layer_forward(
            hidden_state,
            weights_full,
            select(seg_near, micro_idx),
            select(seg_ids, micro_idx),
            select(cosine_rows, micro_idx),
            select(sine_rows, micro_idx),
        )
        sent_rows = output.astype(jnp.bfloat16)
        outputs.append(sent_rows)
        stored.append(kept)
        if tick_no < MICRO:
            received = passed_along(sent_rows, "section", 1)
    gathered = (
        lax.all_gather(shards[0], "dp", axis=0, tiled=True),
        lax.all_gather(shards[1], "dp", axis=0, tiled=True),
        lax.all_gather(shards[2], "dp", axis=0, tiled=True),
        lax.all_gather(shards[3], "dp", axis=0, tiled=True),
        lax.all_gather(shards[4], "dp", axis=0, tiled=True),
        lax.all_gather(shards[5], "dp", axis=1, tiled=True),
    )
    weights_full = gathered[:5] + (gathered[5].astype(jnp.float32),)
    returned = jnp.zeros_like(received)
    totals = None
    input_parts = []
    for tick_no in range(MICRO + 1):
        micro_idx = jnp.clip(tick_no - 1 + delay_fwd, 0, MICRO - 1)
        active = jnp.where(leading, tick_no >= 1, tick_no < MICRO)
        incoming = jnp.where(
            leading, returned.astype(jnp.float32), select(cotangent, micro_idx).astype(jnp.float32)
        )
        incoming = jnp.where(active, incoming, 0.0)
        kept = jax.tree.map(
            lambda early, later: jnp.where(leading, early, later),
            stored[max(tick_no - 1, 0)],
            stored[min(tick_no + 1, MICRO)],
        )
        dhidden, grad_terms = layer_backward(
            incoming,
            kept,
            weights_full,
            select(seg_near, micro_idx),
            select(seg_ids, micro_idx),
            select(cosine_rows, micro_idx),
            select(sine_rows, micro_idx),
        )
        totals = (
            grad_terms
            if totals is None
            else tuple((early + later for early, later in zip(totals, grad_terms)))
        )
        input_parts.append(dhidden)
        if tick_no < MICRO:
            returned = passed_along(dhidden.astype(jnp.bfloat16), "section", -1)
    summed = (
        lax.psum_scatter(
            totals[0].astype(jnp.bfloat16), "dp", scatter_dimension=0, tiled=True
        ).astype(jnp.float32),
        lax.psum_scatter(
            totals[1].astype(jnp.bfloat16), "dp", scatter_dimension=0, tiled=True
        ).astype(jnp.float32),
        lax.psum_scatter(
            totals[2].astype(jnp.bfloat16), "dp", scatter_dimension=0, tiled=True
        ).astype(jnp.float32),
        lax.psum_scatter(
            totals[3].astype(jnp.bfloat16), "dp", scatter_dimension=0, tiled=True
        ).astype(jnp.float32),
        lax.psum_scatter(
            totals[4].astype(jnp.bfloat16), "dp", scatter_dimension=0, tiled=True
        ).astype(jnp.float32),
        lax.psum_scatter(
            totals[5].astype(jnp.bfloat16), "dp", scatter_dimension=1, tiled=True
        ).astype(jnp.float32),
    )
    summed = jax.tree.map(
        lambda part: part.astype(jnp.float32), lax.psum(for_sending(summed), "ctx")
    )
    last_rows = jnp.concatenate(
        [jnp.where(leading, outputs[micro_no], outputs[micro_no + 1]) for micro_no in range(MICRO)],
        axis=0,
    )
    input_grads = jnp.concatenate(
        [
            jnp.where(leading, input_parts[micro_no + 1], input_parts[micro_no])
            for micro_no in range(MICRO)
        ],
        axis=0,
    )
    norm_grads = summed[5]
    return (
        last_rows[None],
        input_grads[None],
        summed[0][None],
        summed[1][None],
        summed[2][None],
        summed[3][None],
        summed[4][None],
        norm_grads[0][None],
        norm_grads[1][None],
        norm_grads[2][None],
        norm_grads[3][None],
    )


NT = (((1,), (1,)), ((), ()))
TN = (((0,), (0,)), ((), ()))


def mm(left, right, dims=(((1,), (0,)), ((), ()))):
    return lax.dot_general(left, right, dims, preferred_element_type=jnp.float32)


def in_vmem():
    return pl.BlockSpec(memory_space=pltpu.VMEM)


def anywhere():
    return pl.BlockSpec(memory_space=pl.ANY)


def in_smem():
    return pl.BlockSpec(memory_space=pltpu.SMEM)


def kernel_call(body, out_shapes, in_specs, scratch, mbytes, cost, name, out_specs=None, grid=None):
    return pl.pallas_call(
        body,
        out_shape=out_shapes,
        in_specs=in_specs,
        out_specs=[in_vmem()] * len(out_shapes) if out_specs is None else out_specs,
        scratch_shapes=scratch,
        **({} if grid is None else {"grid": grid}),
        compiler_params=pltpu.CompilerParams(vmem_limit_bytes=mbytes * 2**20),
        cost_estimate=pl.CostEstimate(flops=0, bytes_accessed=3 * 10**6 * cost, transcendentals=0),
        name=name,
    )


def shape_of(shape, dtype):
    return jax.ShapeDtypeStruct(shape, dtype)


def start_loads(place, pieces, first, width, scratch, sems, begin, blocks=1):
    dp_rank, core = place[0], place[1]
    count = pieces[0].shape[0]
    copies = []
    cuts = ((0, 0, 2, 0, 0, 0), (1, 0, 2, 1, 0, 0), (2, 0, 2, 2, 0, 0), (3, 0, 1, 3, 0, 0), (4, 0, 1, 3, 1, 0))
    cuts += ((5, 0, 2, 0, 0, 1), (6, 0, 2, 1, 0, 1), (6, 2, 2, 2, 0, 1), (7, 0, 2, 3, 0, 1))
    unit = count // 2
    for piece, source, size, flip, target, other in cuts:
        half = 1 - core if other else core
        for block in range(blocks):
            row = ((dp_rank ^ flip) * blocks + block) * count + target * unit
            copies.append(
                pltpu.make_async_copy(
                    pieces[piece].at[pl.ds(source * unit, size * unit), pl.ds(first + block * width, width)],
                    scratch.at[
                        pl.ds(pl.multiple_of(row, unit), size * unit),
                        pl.ds(pl.multiple_of(half * width, 128), width),
                    ],
                    sems.at[begin + len(copies)],
                )
            )
    for copy in copies:
        copy.start()
    return copies


def wait_all(copies):
    for copy in copies:
        copy.wait()


def turn(values, cosine, sine):
    lane = lax.broadcasted_iota(jnp.int32, values.shape, 1)
    swapped = jnp.where(
        lane % 64 < 32, pltpu.roll(values, 96, 1), pltpu.roll(values, 32, 1)
    )
    return values * cosine + swapped * sine


def project_rows(place, hidden, cosine, sine, pieces):
    rows, width = hidden.shape
    half = 3 * width // 2

    def body(place_ref, hidden_ref, cos_ref, sin_ref, *refs):
        parts, (q_ref, kv_ref, weight, sems) = refs[:8], refs[8:]
        wait_all(start_loads(place_ref, parts, 0, half, weight, sems, 0))
        for step in range(3 * width // 256):
            mixed = mm(hidden_ref[...], weight[:, step * 256 : step * 256 + 256])
            for pair in range(2):
                column = step * 256 + pair * 128
                part = mixed[:, pair * 128 : pair * 128 + 128]
                which, lane = column // width, column % width
                if which < 2:
                    part = turn(part, cos_ref[...], sin_ref[...])
                if which == 0:
                    q_ref[:, lane : lane + 128] = (
                        part.astype(jnp.bfloat16).astype(jnp.float32) * HEAD**-0.5
                    ).astype(jnp.bfloat16)
                else:
                    kv_ref[which - 1, :, lane : lane + 128] = part.astype(jnp.bfloat16)

    return kernel_call(
        body,
        [shape_of((rows, width), jnp.bfloat16), shape_of((2, rows, width), jnp.bfloat16)],
        [in_smem()] + [in_vmem()] * 3 + [anywhere()] * 8,
        [pltpu.VMEM((width, 3 * width), jnp.bfloat16), pltpu.SemaphoreType.DMA((10,))],
        60,
        3,
        "project_rows",
    )(place, hidden, cosine, sine, *pieces)


def attend_rows(queries, blocks, seg_column, seg_row):
    rows, width = queries.shape
    keys = 2 * rows

    def body(col_ref, row_ref, q_ref, b0, b1, out_ref, bias):
        @pl.when(pl.program_id(0) == 0)
        def _():
            bias[...] = jnp.where(col_ref[...] == row_ref[...], 0.0, NEG)

        lane = lax.broadcasted_iota(jnp.int32, (rows, 128), 1)
        query = q_ref[...]
        key = jnp.concatenate([b[0] for b in (b0, b1)], axis=0)
        value = jnp.concatenate([b[1] for b in (b0, b1)], axis=0)
        results = []
        for head in range(2):
            own = (lane < 64) if head == 0 else (lane >= 64)
            scores = mm(jnp.where(own, query, jnp.zeros_like(query)), key, NT) + bias[...]
            top = jnp.max(scores, axis=1, keepdims=True)
            exponent = jnp.exp(scores - top)
            total = jnp.sum(exponent, axis=1, keepdims=True)
            results.append(mm(exponent.astype(jnp.bfloat16), value) / total)
        out_ref[...] = jnp.where(lane < 64, results[0], results[1]).astype(jnp.bfloat16)

    block = pl.BlockSpec((2, rows, 128), lambda j: (0, 0, j))
    return kernel_call(
        body,
        [shape_of((rows, width), jnp.bfloat16)],
        [
            pl.BlockSpec((rows, 1), lambda j: (0, 0)),
            pl.BlockSpec((1, keys), lambda j: (0, 0)),
            pl.BlockSpec((rows, 128), lambda j: (0, j)),
            block, block,
        ],
        [pltpu.VMEM((rows, keys), jnp.float32)],
        60,
        8,
        "attend_rows",
        [pl.BlockSpec((rows, 128), lambda j: (0, j))],
        (width // 128,),
    )(seg_column, seg_row, queries, *blocks)[0]


def attend_rows_back(queries, blocks, seg_row, seg_column, incoming):
    rows, width = queries.shape
    keys = 2 * rows

    def body(row_ref, col_ref, q_ref, in_ref, b0, b1, dq_ref, own_ref, core_ref, bias):
        @pl.when(pl.program_id(0) == 0)
        def _():
            bias[...] = jnp.where(col_ref[...] == row_ref[...], 0.0, NEG)

        lane = lax.broadcasted_iota(jnp.int32, (rows, 128), 1)
        query, given = q_ref[...], in_ref[...]
        key = jnp.concatenate([b[0] for b in (b0, b1)], axis=0)
        value = jnp.concatenate([b[1] for b in (b0, b1)], axis=0)
        key_t = key.T
        dkeys, dvalues, dqueries = [], [], []
        for head in range(2):
            own = (lane < 64) if head == 0 else (lane >= 64)
            scores = mm(key, jnp.where(own, query, jnp.zeros_like(query)), NT) + bias[...]
            exponent = jnp.exp(scores - jnp.max(scores, axis=0, keepdims=True))
            probs = exponent * (1.0 / jnp.sum(exponent, axis=0, keepdims=True))
            dvalues.append(mm(probs.astype(jnp.bfloat16), given))
            dprobs = probs * mm(value, jnp.where(own, given, jnp.zeros_like(given)), NT)
            dscores = dprobs - probs * jnp.sum(dprobs, axis=0, keepdims=True)
            dscores = dscores.astype(jnp.bfloat16)
            dkeys.append(mm(dscores, query))
            dqueries.append(mm(key_t[64 * head : 64 * head + 64], dscores))
        dq_ref[...] = jnp.concatenate(dqueries, axis=0).T * HEAD**-0.5
        wide = lax.broadcasted_iota(jnp.int32, (keys, 128), 1) < 64
        for which, pair in enumerate((dkeys, dvalues)):
            both = jnp.where(wide, pair[0], pair[1]).astype(jnp.bfloat16)
            own_ref[which] = both[:rows]
            core_ref[which] = both[rows:]

    block = pl.BlockSpec((2, rows, 128), lambda j: (0, 0, j))
    columns = pl.BlockSpec((rows, 128), lambda j: (0, j))
    pair_shape = shape_of((2, rows, width), jnp.bfloat16)
    return kernel_call(
        body,
        [
            shape_of((rows, width), jnp.float32),
            pair_shape,
            pair_shape,
        ],
        [
            pl.BlockSpec((1, rows), lambda j: (0, 0)),
            pl.BlockSpec((keys, 1), lambda j: (0, 0)),
            columns, columns, block, block,
        ],
        [pltpu.VMEM((keys, rows), jnp.float32)],
        60,
        18,
        "attend_rows_back",
        [columns, block, block],
        (width // 128,),
    )(seg_row, seg_column, queries, incoming, *blocks)


def unit_of(resid):
    centred = resid - jnp.mean(resid, axis=1, keepdims=True)
    scaling = lax.rsqrt(jnp.mean(centred * centred, axis=1, keepdims=True) + EPS)
    return centred * scaling, scaling


def norm_rows_back(incoming, unit, scaling, gain):
    scaled = incoming * gain
    return scaling * (
        scaled
        - jnp.mean(scaled, axis=1, keepdims=True)
        - unit * jnp.mean(scaled * unit, axis=1, keepdims=True)
    )


FF_STEP = 512


def mlp_scratch(width, hidden_width):
    return [
        pltpu.VMEM((width, width), jnp.bfloat16),
        pltpu.VMEM((width, hidden_width), jnp.bfloat16),
        pltpu.VMEM((width, hidden_width), jnp.bfloat16),
        pltpu.VMEM((hidden_width, width), jnp.bfloat16),
        pltpu.VMEM((width, 256), jnp.bfloat16),
        pltpu.VMEM((128, width), jnp.float32),
        pltpu.SemaphoreType.DMA((80,)),
    ]


def mlp_rows(place, hidden, attended, first_parts, rest_parts):
    rows, width = hidden.shape
    ff_half = (rest_parts[0].shape[1] - 2 * width) // 2
    ff = 2 * ff_half

    def body(place_ref, hidden_ref, att_ref, *refs):
        parts, rest = refs[:16], refs[16:]
        out_ref, one_ref, two_ref, acts_ref, gate_ref, up_ref = rest[:6]
        w_out, w_gate, w_up, w_down, w_norm, norm_ref, sems = rest[6:]
        normed_ref = acts_ref.at[:, :width]
        norm_loads = start_loads(place_ref, parts[:8], 2 * width, 128, w_norm, sems, 70)
        loads = [
            start_loads(place_ref, parts[:8], 3 * width // 2, width // 2, w_out, sems, 0),
            start_loads(place_ref, parts[8:], 0, ff_half, w_gate, sems, 10),
            start_loads(place_ref, parts[8:], ff_half, ff_half, w_up, sems, 20),
            start_loads(place_ref, parts[8:], 2 * ff_half, width // 2, w_down, sems, 30, 4),
        ]
        wait_all(norm_loads)
        norm_ref[...] = w_norm[:, :128].astype(jnp.float32).T
        wait_all(loads[0])
        resid = hidden_ref[...].astype(jnp.float32) + mm(att_ref[...], w_out[...])
        one_ref[...] = resid
        normed = unit_of(resid)[0] * norm_ref[0:1] + norm_ref[1:2]
        normed_ref[...] = normed.astype(jnp.bfloat16)
        two_ref[...] = normed
        wait_all(loads[1])
        wait_all(loads[2])
        wait_all(loads[3])

        @pl.loop(0, ff // FF_STEP)
        def _(step):
            span = pl.ds(pl.multiple_of(step * FF_STEP, FF_STEP), FF_STEP)
            gate = mm(normed_ref[...], w_gate[:, span])
            up = mm(normed_ref[...], w_up[:, span])
            gate_ref[:, span] = gate
            up_ref[:, span] = up
            middle = (gate * jax.nn.sigmoid(gate) * up).astype(jnp.bfloat16)
            acts_ref[:, pl.ds(pl.multiple_of(width + step * FF_STEP, 128), FF_STEP)] = middle
            two_ref[...] += mm(middle, w_down[span, :])

        out_ref[...] = (unit_of(two_ref[...])[0] * norm_ref[2:3] + norm_ref[3:4]).astype(jnp.bfloat16)

    return kernel_call(
        body,
        [
            shape_of((rows, width), jnp.bfloat16),
            shape_of((rows, width), jnp.float32),
            shape_of((rows, width), jnp.float32),
            shape_of((rows, width + ff), jnp.bfloat16),
            shape_of((rows, ff), jnp.float32),
            shape_of((rows, ff), jnp.float32),
        ],
        [in_smem()] + [in_vmem()] * 2 + [anywhere()] * 16,
        mlp_scratch(width, ff),
        60,
        16,
        "mlp_rows",
    )(place, hidden, attended, *first_parts, *rest_parts)


def mlp_rows_back(place, incoming, one, two, gate, up, first_parts, rest_parts):
    rows, width = incoming.shape
    ff_half = (rest_parts[0].shape[1] - 2 * width) // 2
    ff = 2 * ff_half

    def body(place_ref, in_ref, one_ref, two_ref, gate_ref, up_ref, *refs):
        parts, rest = refs[:16], refs[16:]
        keep_ref, send_ref, keep_ff, send_ff, dresid_ref, datt_ref = rest[:6]
        w_out, w_gate, w_up, w_down, w_norm, norm_ref, sems, low_ref, sums_ref = rest[6:]
        core = place_ref[1]
        norm_loads = start_loads(place_ref, parts[:8], 2 * width, 128, w_norm, sems, 70)

        def share(half, columns, value, keep, send):
            @pl.when(half == core)
            def _():
                keep[:rows, columns] = value

            @pl.when(half != core)
            def _():
                send[:rows, columns] = value

        loads = [
            start_loads(place_ref, parts[8:], 2 * ff_half, width // 2, w_down, sems, 30, 4),
            start_loads(place_ref, parts[8:], 0, ff_half, w_gate, sems, 10),
            start_loads(place_ref, parts[8:], ff_half, ff_half, w_up, sems, 20),
            start_loads(place_ref, parts[:8], 3 * width // 2, width // 2, w_out, sems, 0),
        ]
        wait_all(norm_loads)
        norm_ref[...] = w_norm[:, :128].astype(jnp.float32).T
        sums_ref[...] = jnp.zeros_like(sums_ref)
        given = in_ref[...].astype(jnp.float32)
        unit, scaling = unit_of(two_ref[...])
        sums_ref[2:3] = jnp.sum(given * unit, axis=0, keepdims=True)
        sums_ref[3:4] = jnp.sum(given, axis=0, keepdims=True)
        dresid_two = norm_rows_back(given, unit, scaling, norm_ref[2:3])
        dresid_ref[...] = dresid_two
        low_ref[...] = dresid_two.astype(jnp.bfloat16)
        for half in range(2):
            span = slice(half * width // 2, (half + 1) * width // 2)
            share(half, slice(0, width // 2), low_ref[:, span], keep_ref, send_ref)
        for copies in loads:
            wait_all(copies)

        @pl.loop(0, ff // FF_STEP)
        def _(step):
            span = pl.ds(pl.multiple_of(step * FF_STEP, FF_STEP), FF_STEP)
            dmiddle = mm(low_ref[...], w_down[span, :], NT)
            gate_block = gate_ref[:, span]
            sig = jax.nn.sigmoid(gate_block)
            dgate = (dmiddle * up_ref[:, span] * sig * (1.0 + gate_block * (1.0 - sig))).astype(jnp.bfloat16)
            dup = (dmiddle * (gate_block * sig)).astype(jnp.bfloat16)
            half, column = step // (ff_half // FF_STEP), step % (ff_half // FF_STEP) * FF_STEP
            share(half, pl.ds(pl.multiple_of(column, 128), FF_STEP), dgate, keep_ff, send_ff)
            share(half, pl.ds(pl.multiple_of(column + ff_half, 128), FF_STEP), dup, keep_ff, send_ff)
            dresid_ref[...] += mm(dgate, w_gate[:, span], NT) + mm(dup, w_up[:, span], NT)

        dnormed = dresid_ref[...]
        unit, scaling = unit_of(one_ref[...])
        sums_ref[0:1] = jnp.sum(dnormed * unit, axis=0, keepdims=True)
        sums_ref[1:2] = jnp.sum(dnormed, axis=0, keepdims=True)
        dresid_one = norm_rows_back(dnormed, unit, scaling, norm_ref[0:1])
        dresid_ref[...] = dresid_one
        low_ref[...] = dresid_one.astype(jnp.bfloat16)
        for half in range(2):
            span = slice(half * width // 2, (half + 1) * width // 2)
            share(half, slice(width // 2, width), low_ref[:, span], keep_ref, send_ref)
        datt_ref[...] = mm(low_ref[...], w_out[...], NT).astype(jnp.bfloat16)
        for ref in (keep_ref, send_ref):
            ref[rows:] = sums_ref[...].astype(jnp.bfloat16)

    return kernel_call(
        body,
        [
            shape_of((rows + 16, width), jnp.bfloat16),
            shape_of((rows + 16, width), jnp.bfloat16),
            shape_of((rows, ff), jnp.bfloat16),
            shape_of((rows, ff), jnp.bfloat16),
            shape_of((rows, width), jnp.float32),
            shape_of((rows, width), jnp.bfloat16),
        ],
        [in_smem()] + [in_vmem()] * 5 + [anywhere()] * 16,
        mlp_scratch(width, ff)
        + [pltpu.VMEM((rows, width), jnp.bfloat16), pltpu.VMEM((16, width), jnp.float32)],
        60,
        21,
        "mlp_rows_back",
    )(place, incoming, one, two, gate, up, *first_parts, *rest_parts)


def project_rows_back(place, dqueries, sums, dresid_one, cosine, sine, pieces):
    rows, width = dqueries.shape
    half = 3 * width // 2
    count = len(sums)

    def body(place_ref, dq_ref, resid_ref, cos_ref, sin_ref, *refs):
        parts, rest = refs[:8], refs[8:]
        sum_refs, (keep_ref, send_ref, dhidden_ref, weight, sems, dmixed_ref) = rest[:count], rest[count:]
        core = place_ref[1]
        loads = start_loads(place_ref, parts, 0, half, weight, sems, 0)
        for column in range(0, 3 * width, 128):
            which, lane = column // width, column % width
            span = slice(lane, lane + 128)
            if which == 0:
                part = dq_ref[:, span]
            else:
                part = sum(ref[which - 1, :, span].astype(jnp.float32) for ref in sum_refs)
            if which < 2:
                part = turn(part, cos_ref[...], -sin_ref[...])
            dmixed_ref[:, column : column + 128] = part.astype(jnp.bfloat16)
        for index in range(2):
            @pl.when(core == index)
            def _():
                keep_ref[...] = dmixed_ref[:, index * half : (index + 1) * half]
                send_ref[...] = dmixed_ref[:, (1 - index) * half : (2 - index) * half]

        wait_all(loads)
        dhidden_ref[...] = resid_ref[...] + mm(dmixed_ref[...], weight[...], NT)

    return kernel_call(
        body,
        [
            shape_of((rows, half), jnp.bfloat16),
            shape_of((rows, half), jnp.bfloat16),
            shape_of((rows, width), jnp.float32),
        ],
        [in_smem()] + [in_vmem()] * 4 + [anywhere()] * 8 + [in_vmem()] * count,
        [
            pltpu.VMEM((width, 3 * width), jnp.bfloat16),
            pltpu.SemaphoreType.DMA((10,)),
            pltpu.VMEM((rows, 3 * width), jnp.bfloat16),
        ],
        60,
        6,
        "project_rows_back",
    )(place, dqueries, dresid_one, cosine, sine, *pieces, *sums)


def grad_parts(place, groups, sums=None):
    jobs = [job for group in groups for job in group]
    rows = jobs[0][0][0].shape[0]
    lefts, rights, arrays = [], [], []
    for left, left_span, right, right_span, blocks in jobs:
        for known, entry in ((lefts, (left, left_span)), (rights, (right, right_span))):
            if not any(entry[0] is other[0] and entry[1] == other[1] for other in known):
                known.append(entry)
        for array in (*left, *right):
            if not any(array is other for other in arrays):
                arrays.append(array)
    where = lambda array: next(i for i, other in enumerate(arrays) if other is array)
    slot = lambda known, pair, span: next(
        i for i, other in enumerate(known) if other[0] is pair and other[1] == span
    )
    count = (jobs[0][1][1] - jobs[0][1][0]) // 4 // jobs[0][4]
    totals = [sum((job[3][1] - job[3][0]) * job[4] for job in group) for group in groups]
    widths = list(totals)
    if sums is not None:
        widths[0] += 128

    def body(place_ref, *refs):
        inputs, refs = refs[: len(arrays)], refs[len(arrays) :]
        outs, refs = refs[: 5 * len(groups)], refs[5 * len(groups) :]
        block, left_refs, right_refs = refs[0], refs[1 : 1 + len(lefts)], refs[1 + len(lefts) :]
        for ref, (pair, span) in zip(left_refs, lefts):
            for core in range(2):
                ref[:, core * rows : (core + 1) * rows] = inputs[where(pair[core])][:rows, span[0] : span[1]].T
        for ref, (pair, span) in zip(right_refs, rights):
            for core in range(2):
                ref[core * rows : (core + 1) * rows] = inputs[where(pair[core])][:rows, span[0] : span[1]]
        if sums is not None:
            padded, turned = refs[-2:]
            padded[...] = jnp.zeros_like(padded)
            padded[:16] = sum(
                inputs[where(array)][rows:, : 4 * count].astype(jnp.float32) for array in jobs[sums][2]
            )
            turned[...] = padded[...].T
        upper, lower = slice(0, count // 2), slice(count // 2, count)
        for index, group in enumerate(groups):
            own_ref, x_ref, y_ref, xl_ref, yu_ref = outs[5 * index : 5 * index + 5]
            end = widths[index]
            for flip in range(4):
                target = 0
                for left, left_span, right, right_span, blocks in group:
                    left_t, right_all = left_refs[slot(lefts, left, left_span)], right_refs[slot(rights, right, right_span)]
                    width = right_span[1] - right_span[0]
                    tile = 512 if width % 512 == 0 else 384
                    for part in range(blocks):
                        begin = ((place_ref[0] ^ flip) * blocks + part) * count
                        rows_t = left_t[pl.ds(pl.multiple_of(begin, count), count), :]
                        for column in range(0, width, tile):
                            block[:, target : target + tile] = mm(
                                rows_t, right_all[:, column : column + tile]
                            ).astype(jnp.bfloat16)
                            target += tile
                if target < end:
                    begin = pl.multiple_of((place_ref[0] ^ flip) * count, count)
                    block[:, target:end] = turned[pl.ds(begin, count), :].astype(jnp.bfloat16)
                if flip == 0:
                    own_ref[...] = block[:, :end]
                elif flip == 1:
                    x_ref[upper] = block[upper, :end]
                    xl_ref[...] = block[lower, :end]
                elif flip == 2:
                    y_ref[upper] = block[lower, :end]
                    yu_ref[...] = block[upper, :end]
                else:
                    x_ref[lower] = block[upper, :end]
                    y_ref[lower] = block[lower, :end]

    scratch = [pltpu.VMEM((count, max(widths)), jnp.bfloat16)]
    scratch += [pltpu.VMEM((span[1] - span[0], 2 * rows), jnp.bfloat16) for _, span in lefts]
    scratch += [pltpu.VMEM((2 * rows, span[1] - span[0]), jnp.bfloat16) for _, span in rights]
    if sums is not None:
        scratch += [pltpu.VMEM((128, 4 * count), jnp.float32), pltpu.VMEM((4 * count, 128), jnp.float32)]
    shapes = []
    for width in widths:
        shapes += [shape_of((count, width), jnp.bfloat16)] * 3 + [shape_of((count // 2, width), jnp.bfloat16)] * 2
    made = kernel_call(
        body, shapes, [in_smem()] + [in_vmem()] * len(arrays), scratch, 60, 7, "grad_parts"
    )(place, *arrays)
    return [made[5 * index : 5 * index + 5] for index in range(len(groups))]


def to_core(value):
    return lax.ppermute(value, "section", [(0, 1), (1, 0)])


def along_x(value):
    return lax.ppermute(value, "dp", [(i, i ^ 1) for i in range(4)])


def along_y(value):
    return lax.ppermute(value, "dp", [(i, i ^ 2) for i in range(4)])


def along_z(value):
    return lax.ppermute(value, "ctx", [(i, i ^ 1) for i in range(4)])


def near_blocks(value):
    pairs = [(i, i ^ 1) for i in range(4)] + [(4 + i, 4 + (i ^ 2)) for i in range(4)]
    return lax.ppermute(value, ("section", "ctx"), pairs)


def far_blocks(value):
    return lax.ppermute(value, ("section", "ctx"), [(4 + i, 4 + (i ^ 3)) for i in range(4)])


def same_role(value):
    return lax.ppermute(value, "ctx", [(i, i ^ 3) for i in range(4)])


def lowered(value):
    return value.astype(jnp.bfloat16)


def wide(value):
    return value.astype(jnp.float32)


def by_core(core, mine, theirs, axis):
    return jnp.where(
        core == 0,
        jnp.concatenate([mine, theirs], axis=axis),
        jnp.concatenate([theirs, mine], axis=axis),
    )


def half_of(array, which):
    width = array.shape[-1] // 2
    return lax.dynamic_slice_in_dim(array, which * width, width, array.ndim - 1)


def after(value, *others):
    return lax.optimization_barrier((value, *others))[0]


def gather_near(pieces, *others):
    own = after(pieces[0], *others)
    return [own, along_x(own), along_y(own), pieces[1]]


def gather_far(near, *others):
    rows = near[0].shape[0] // 2
    return [along_x(after(near[2][:rows], *others)), along_y(after(near[1][rows:], *others))]


def both_cores(near, far):
    return [
        *near[:3],
        *far,
        near[3],
        to_core(jnp.concatenate(near[1:3], axis=0)),
        to_core(jnp.concatenate(far, axis=0)),
    ]


def reduce_first(parts, *others):
    return along_x(after(parts[1], *others)), along_y(after(parts[2], *others))


def reduce_second(parts, first, *others):
    _, _, _, x_lower, y_upper = after(tuple(parts), *others)
    from_x, from_y = first
    rows = x_lower.shape[0]
    return (
        along_x(lowered(wide(x_lower) + wide(from_y[rows:]))),
        along_y(lowered(wide(y_upper) + wide(from_x[rows:]))),
    )


def reduce_last(parts, first, second):
    from_x, from_y = first
    rows = second[0].shape[0]
    return lowered(
        wide(parts[0])
        + jnp.concatenate(
            [wide(from_x[:rows]) + wide(second[1]), wide(from_y[:rows]) + wide(second[0])], axis=0
        )
    )


def reduce_ctx(piece, middle, *others):
    mine = lowered(wide(piece) + wide(same_role(piece)))
    other = along_z(after(mine, *others))
    return jnp.where(middle, other, mine), jnp.where(middle, mine, other)


def paired_on_device(
    tokens,
    seg_ids,
    query_key_value_weight,
    output_weight,
    gate_weight,
    up_weight,
    down_weight,
    norm1_gain,
    norm1_bias,
    norm2_gain,
    norm2_bias,
    cotangent,
):
    core, ctx_rank, dp_rank = (lax.axis_index(a) for a in ("section", "ctx", "dp"))
    span, width = tokens.shape[1], tokens.shape[2]
    sequence = ctx_rank // 2
    middle = (ctx_rank == 1) | (ctx_rank == 2)
    role = jnp.where(middle, 1, 0)
    even = ctx_rank % 2 == 0
    place = jnp.stack([dp_rank, core]).astype(jnp.int32)
    pick = lambda array, index: lax.dynamic_index_in_dim(array, index, 0, keepdims=False)

    def in_order(left, right):
        return jnp.where(even, jnp.concatenate([left, right]), jnp.concatenate([right, left]))

    def to_rows():
        mine, theirs = jnp.where(middle, cotangent, tokens), jnp.where(middle, tokens, cotangent)
        first = near_blocks(jnp.where(core == 0, pick(theirs, sequence), pick(theirs, 1 - sequence)))
        second = far_blocks(pick(mine, 1 - sequence))
        return in_order(
            jnp.where(core == 0, pick(mine, sequence), first), jnp.where(core == 0, first, second)
        )

    def send_rows(rows):
        halves = rows.reshape(2, span, width)
        left, right = pick(halves, jnp.where(even, 0, 1)), pick(halves, jnp.where(even, 1, 0))
        return left, near_blocks(jnp.where(core == 0, right, left)), far_blocks(right)

    def placed_rows(left, first, second):
        same = jnp.where(core == 0, left, second)
        first_layer, second_layer = jnp.where(middle, first, same), jnp.where(middle, same, first)
        other = to_core(jnp.where(core == 0, second_layer, first_layer))
        mine = jnp.where(core == 0, first_layer, second_layer)
        return jnp.where(
            sequence == core, jnp.stack([mine, other]), jnp.stack([other, mine])
        )[None]

    norm_columns = jnp.concatenate([norm1_gain, norm1_bias, norm2_gain, norm2_bias], axis=0).T
    norm_columns = jnp.pad(norm_columns, ((0, 0), (0, 124)))

    def packs(which):
        return (
            jnp.concatenate(
                [half_of(query_key_value_weight[0], which), half_of(output_weight[0], which), norm_columns],
                axis=1,
            ),
            jnp.concatenate(
                [half_of(gate_weight[0], which), half_of(up_weight[0], which)]
                + jnp.split(half_of(down_weight[0], which), down_weight.shape[1] // gate_weight.shape[1]),
                axis=1,
            ),
        )

    own_halves, other_halves = packs(core), packs(1 - core)
    sent = [to_core(pack) for pack in other_halves]
    sent += [to_core(after(pack, *sent)) for pack in own_halves]
    count = len(own_halves)
    pieces = [
        (
            jnp.where(core == role, own_halves[index], sent[index]),
            jnp.where(core == role, other_halves[index], sent[count + index]),
        )
        for index in range(count)
    ]

    seg = pick(seg_ids, sequence)
    rows = 2 * span
    begin = (sequence ^ core) * rows
    seg_rows = lax.dynamic_slice_in_dim(seg, begin, rows, 0)
    seg_keys = jnp.concatenate([seg_rows, lax.dynamic_slice_in_dim(seg, rows - begin, rows, 0)])
    begins = jnp.sum((seg[None, :] < seg_rows[:, None]).astype(jnp.int32), axis=1)
    places = begin + jnp.arange(rows, dtype=jnp.int32) - begins
    lanes = jnp.arange(128, dtype=jnp.int32) % HEAD
    half = HEAD // 2
    spread = 1000.0 ** (-2.0 * (lanes % half).astype(jnp.float32) / HEAD)
    angles = places.astype(jnp.float32)[:, None] * spread[None, :]
    cosine, sine = jnp.cos(angles), jnp.where(lanes < half, -1.0, 1.0) * jnp.sin(angles)

    def attention(hidden):
        queries, own = project_rows(place, hidden, cosine, sine, first)
        blocks = [own, to_core(own)]
        return queries, blocks, attend_rows(queries, blocks, seg_rows[:, None], seg_keys[None, :])

    given = to_rows()
    near = gather_near(pieces[0])
    far = gather_far(near)
    near_mlp = gather_near(pieces[1], *far)
    first = both_cores(near, far)
    queries, blocks, attended = attention(given)
    near_mlp = [after(part, attended) for part in near_mlp]
    rest = both_cores(near_mlp, gather_far(near_mlp))
    output = mlp_rows(place, given, attended, first, rest)[0]

    hidden = jnp.where(middle, along_z(output), given)
    queries, blocks, attended = attention(hidden)
    output, one, two, acts, gate, up = mlp_rows(place, hidden, attended, first, rest)

    _, _, _, _, dresid_one, dattended = mlp_rows_back(place, given, one, two, gate, up, first, rest)
    sent_outputs = send_rows(output)
    dqueries, own, across = attend_rows_back(
        queries, blocks, seg_rows[None, :], seg_keys[:, None], after(dattended, *sent_outputs)
    )
    dhidden = project_rows_back(
        place, dqueries, (own, to_core(across)), dresid_one, cosine, sine, first
    )[2]
    incoming = jnp.where(middle, given, along_z(lowered(dhidden)))

    both = lambda value: (value, to_core(value))
    acts, attended, hidden = both(acts), both(attended), both(hidden)
    keep, send, keep_ff, send_ff, dresid_one, dattended = mlp_rows_back(
        place, incoming, one, two, gate, up, first, rest
    )
    ff = keep_ff.shape[1]
    right, right_ff = (keep, to_core(send)), (keep_ff, to_core(send_ff))
    parts = grad_parts(
        place,
        [
            [
                (acts, (width, width + ff), right, (0, width // 2), ff // width),
                (attended, (0, width), right, (width // 2, width), 1),
            ]
        ],
        1,
    )
    right_ff = (after(right_ff[0], *parts[0]), right_ff[1])
    parts += grad_parts(
        place, [[(acts, (0, width), right_ff, (half * ff // 2, (half + 1) * ff // 2), 1)] for half in range(2)]
    )
    dqueries, own, across = attend_rows_back(
        queries, blocks, seg_rows[None, :], seg_keys[:, None], after(dattended, *(x for part in parts for x in part))
    )
    near = [reduce_first(parts[0])]
    near.append(reduce_first(parts[1]))
    across = to_core(after(across, *near[0], *near[1]))
    far = [reduce_second(parts[0], near[0], across)]
    near.append(reduce_first(parts[2], across))
    keep, send, dhidden = project_rows_back(place, dqueries, (own, across), dresid_one, cosine, sine, first)
    keep = after(keep, *far[0])
    parts += grad_parts(place, [[(hidden, (0, width), (keep, to_core(send)), (0, 3 * width // 2), 1)]])
    near.append(reduce_first(parts[3]))
    far.append(reduce_second(parts[1], near[1], *parts[3]))
    far.append(reduce_second(parts[2], near[2], *parts[3]))
    far.append(reduce_second(parts[3], near[3]))
    pieces = [reduce_last(*group) for group in zip(parts, near, far)]
    pieces[0] = after(pieces[0], *parts[3])
    totals = [reduce_ctx(piece, middle, *far[3]) for piece in pieces]

    pairs = []
    for first_layer, second_layer in totals:
        pairs.append(
            (
                jnp.where(core == 0, first_layer, second_layer),
                to_core(jnp.where(core == 0, second_layer, first_layer)),
            )
        )
    joined = lambda index, begin, end: wide(
        by_core(core, pairs[index][0][:, begin:end], pairs[index][1][:, begin:end], 1)
    )[None]
    norm_grads = wide(pairs[0][0][:, 5 * width // 2 : 5 * width // 2 + 4]).T
    pick_down = lambda which: jnp.concatenate(
        [pairs[0][which][:, i * width // 2 : (i + 1) * width // 2] for i in range(ff // width)]
    )
    grad_down = wide(by_core(core, pick_down(0), pick_down(1), 1))[None]

    return (
        placed_rows(*after(sent_outputs, *far[3])),
        wide(placed_rows(*send_rows(after(lowered(dhidden), *far[3])))),
        joined(3, 0, 3 * width // 2),
        joined(0, 2 * width, 5 * width // 2),
        joined(1, 0, ff // 2),
        joined(2, 0, ff // 2),
        grad_down,
        *(norm_grads[i : i + 1] for i in range(4)),
    )


def solution(mesh):
    placed = (
        P("dp", "ctx", None),
        P("dp", None),
        P("section", "dp", None),
        P("section", "dp", None),
        P("section", "dp", None),
        P("section", "dp", None),
        P("section", "dp", None),
        P("section", "dp"),
        P("section", "dp"),
        P("section", "dp"),
        P("section", "dp"),
        P("dp", "ctx", None),
    )
    paired = mesh.shape["section"] == 2 and mesh.shape["ctx"] == 4 and mesh.shape["dp"] == 4
    return jax.shard_map(
        paired_on_device if paired else relay_on_device,
        mesh=mesh,
        in_specs=placed,
        out_specs=(
            P("section", "dp", "ctx", None),
            P("section", "dp", "ctx", None),
            P("section", "dp", None),
            P("section", "dp", None),
            P("section", "dp", None),
            P("section", "dp", None),
            P("section", "dp", None),
            P("section", "dp"),
            P("section", "dp"),
            P("section", "dp"),
            P("section", "dp"),
        ),
        check_vma=False,
    )
```

```python
import jax
import jax.numpy as jnp
from jax import lax
from jax.experimental import pallas as pl
from jax.experimental.pallas import tpu as pltpu
from jax.sharding import PartitionSpec as P

HEAD = 64
MICRO = 2


EPS = 1e-05
NEG = -1e30


def passed_along(value, axis, steps):
    count = lax.axis_size(axis)
    first, last = (max(0, -steps), min(count, count - steps))
    return lax.ppermute(value, axis, [(source, source + steps) for source in range(first, last)])


def for_sending(array):
    return jax.tree.map(lambda a: a.astype(jnp.bfloat16) if a.dtype == jnp.float32 else a, array)


def positions(seg_ids):
    places = lax.broadcasted_iota(jnp.int32, seg_ids.shape, 1)
    begins = jnp.concatenate(
        [jnp.ones_like(seg_ids[:, :1]), (seg_ids[:, 1:] != seg_ids[:, :-1]).astype(jnp.int32)],
        axis=1,
    )
    return places - lax.cummax(places * begins, axis=1)


def rope_tables(places, half_dim):
    spread = 1000.0 ** (-2.0 * jnp.arange(half_dim, dtype=jnp.float32) / (2 * half_dim))
    angles = places.astype(jnp.float32)[..., None] * spread
    return (jnp.cos(angles), jnp.sin(angles))


def rotate(values, cosine, sine_table):
    half_dim = values.shape[-1] // 2
    former, latter = (values[..., :half_dim], values[..., half_dim:])
    cosine, sine_table = (cosine[..., None, :], sine_table[..., None, :])
    return jnp.concatenate(
        [former * cosine - latter * sine_table, latter * cosine + former * sine_table], axis=-1
    )


def unrotate(values, cosine, sine_table):
    half_dim = values.shape[-1] // 2
    former, latter = (values[..., :half_dim], values[..., half_dim:])
    cosine, sine_table = (cosine[..., None, :], sine_table[..., None, :])
    return jnp.concatenate(
        [former * cosine + latter * sine_table, latter * cosine - former * sine_table], axis=-1
    )


def norm_parts(resid, gain, bias):
    centred = resid - jnp.mean(resid, axis=-1, keepdims=True)
    scaling = lax.rsqrt(jnp.mean(centred * centred, axis=-1, keepdims=True) + EPS)
    unit_rows = centred * scaling
    return (unit_rows * gain + bias, unit_rows, scaling)


def norm_back(incoming, unit_rows, scaling, gain):
    scaled = incoming * gain
    inner = (
        scaled
        - jnp.mean(scaled, axis=-1, keepdims=True)
        - unit_rows * jnp.mean(scaled * unit_rows, axis=-1, keepdims=True)
    )
    return (
        scaling * inner,
        jnp.sum(incoming * unit_rows, axis=(0, 1)),
        jnp.sum(incoming, axis=(0, 1)),
    )


def masked_scores(queries, all_keys, seg_rows, seg_keys):
    row_count, model_width = queries.shape
    head_count = model_width // HEAD
    scores = jnp.einsum(
        "qhd,khd->hqk",
        queries.reshape(row_count, head_count, HEAD),
        all_keys.reshape(all_keys.shape[0], head_count, HEAD),
        preferred_element_type=jnp.float32,
    ) * HEAD ** (-0.5)
    return jnp.where((seg_rows[:, None] == seg_keys[None, :])[None], scores, NEG)


def attend(operands):
    queries, all_keys, all_values, seg_rows, seg_keys = operands
    row_count, model_width = queries.shape
    head_count = model_width // HEAD
    scores = masked_scores(queries, all_keys, seg_rows, seg_keys)
    row_max = jnp.max(scores, axis=-1, keepdims=True)
    exponent = jnp.exp(scores - row_max)
    row_sum = jnp.sum(exponent, axis=-1, keepdims=True)
    probs_low = (exponent / row_sum).astype(jnp.bfloat16)
    result = jnp.einsum(
        "hqk,khd->qhd",
        probs_low,
        all_values.reshape(all_values.shape[0], head_count, HEAD),
        preferred_element_type=jnp.float32,
    )
    return (result.reshape(row_count, model_width), (row_max + jnp.log(row_sum))[..., 0])


def attend_back(operands):
    queries, all_keys, all_values, seg_rows, seg_keys, log_sum, incoming = operands
    row_count, model_width = queries.shape
    head_count = model_width // HEAD
    key_count = all_keys.shape[0]
    probs = jnp.exp(masked_scores(queries, all_keys, seg_rows, seg_keys) - log_sum[..., None])
    heads_in = incoming.reshape(row_count, head_count, HEAD)
    dprobs = jnp.einsum(
        "qhd,khd->hqk",
        heads_in,
        all_values.reshape(key_count, head_count, HEAD),
        preferred_element_type=jnp.float32,
    )
    dscores = (probs * (dprobs - jnp.sum(probs * dprobs, axis=-1, keepdims=True))).astype(
        jnp.bfloat16
    )
    dquery = jnp.einsum(
        "hqk,khd->qhd",
        dscores,
        all_keys.reshape(key_count, head_count, HEAD),
        preferred_element_type=jnp.float32,
    ) * HEAD ** (-0.5)
    dkeys_part = jnp.einsum(
        "hqk,qhd->khd",
        dscores,
        queries.reshape(row_count, head_count, HEAD),
        preferred_element_type=jnp.float32,
    ) * HEAD ** (-0.5)
    dvalue = jnp.einsum(
        "hqk,qhd->khd", probs.astype(jnp.bfloat16), heads_in, preferred_element_type=jnp.float32
    )
    return (
        dquery.reshape(row_count, model_width),
        dkeys_part.reshape(key_count, model_width),
        dvalue.reshape(key_count, model_width),
    )


def layer_forward(hidden_state, weights_full, seg_rows, seg_keys, cosine, sine_table):
    query_key_value_weight, output_weight, gate_weight, up_weight, down_weight, norm_params = (
        weights_full
    )
    model_width = hidden_state.shape[-1]
    shaped = hidden_state.shape[:2] + (model_width // HEAD, HEAD)
    mixed_query_key_value = jnp.einsum(
        "bld,de->ble", hidden_state, query_key_value_weight, preferred_element_type=jnp.float32
    )
    queries = (
        rotate(mixed_query_key_value[..., :model_width].reshape(shaped), cosine, sine_table)
        .reshape(hidden_state.shape)
        .astype(jnp.bfloat16)
    )
    key_rows = (
        rotate(
            mixed_query_key_value[..., model_width : 2 * model_width].reshape(shaped),
            cosine,
            sine_table,
        )
        .reshape(hidden_state.shape)
        .astype(jnp.bfloat16)
    )
    value_rows = mixed_query_key_value[..., 2 * model_width :].astype(jnp.bfloat16)
    all_keys, all_values = (
        lax.all_gather(key_rows, "ctx", axis=1, tiled=True),
        lax.all_gather(value_rows, "ctx", axis=1, tiled=True),
    )
    attention_output, log_sum = lax.map(attend, (queries, all_keys, all_values, seg_rows, seg_keys))
    attention_output = attention_output.astype(jnp.bfloat16)
    residual_first = hidden_state.astype(jnp.float32) + jnp.einsum(
        "bld,de->ble", attention_output, output_weight, preferred_element_type=jnp.float32
    )
    normalized_rows, unit_one, scale_one = norm_parts(
        residual_first, norm_params[0], norm_params[1]
    )
    normalized_lowered = normalized_rows.astype(jnp.bfloat16)
    gate_projected = jnp.einsum(
        "bld,df->blf", normalized_lowered, gate_weight, preferred_element_type=jnp.float32
    )
    up_projected = jnp.einsum(
        "bld,df->blf", normalized_lowered, up_weight, preferred_element_type=jnp.float32
    )
    middle_state = (gate_projected * jax.nn.sigmoid(gate_projected) * up_projected).astype(
        jnp.bfloat16
    )
    residual_second = normalized_rows + jnp.einsum(
        "blf,fd->bld", middle_state, down_weight, preferred_element_type=jnp.float32
    )
    output, unit_two, scale_two = norm_parts(residual_second, norm_params[2], norm_params[3])
    extra = (all_keys, all_values)
    kept = (
        hidden_state,
        queries,
        key_rows,
        value_rows,
        log_sum,
        attention_output,
        unit_one,
        scale_one,
        gate_projected,
        up_projected,
        unit_two,
        scale_two,
    ) + extra
    return (output, kept)


def layer_backward(incoming, kept, weights_full, seg_rows, seg_keys, cosine, sine_table):
    query_key_value_weight, output_weight, gate_weight, up_weight, down_weight, norm_params = (
        weights_full
    )
    (
        hidden_state,
        queries,
        key_rows,
        value_rows,
        log_sum,
        attention_output,
        unit_one,
        scale_one,
        gate_projected,
        up_projected,
        unit_two,
        scale_two,
    ) = kept[:12]
    all_keys, all_values = (kept[12], kept[13])
    dresid_two, dgain_two, dbias_two = norm_back(incoming, unit_two, scale_two, norm_params[2])
    normalized_lowered = (unit_one * norm_params[0] + norm_params[1]).astype(jnp.bfloat16)
    sigmoid_gate = jax.nn.sigmoid(gate_projected)
    swish_gate = gate_projected * sigmoid_gate
    middle_state = (swish_gate * up_projected).astype(jnp.bfloat16)
    dout_two = dresid_two.astype(jnp.bfloat16)
    grad_down = jnp.einsum(
        "blf,bld->fd", middle_state, dout_two, preferred_element_type=jnp.float32
    )
    dmiddle = jnp.einsum("bld,fd->blf", dout_two, down_weight, preferred_element_type=jnp.float32)
    dgate_proj = (
        dmiddle * up_projected * sigmoid_gate * (1.0 + gate_projected * (1.0 - sigmoid_gate))
    ).astype(jnp.bfloat16)
    dup_proj = (dmiddle * swish_gate).astype(jnp.bfloat16)
    grad_gate = jnp.einsum(
        "bld,blf->df", normalized_lowered, dgate_proj, preferred_element_type=jnp.float32
    )
    grad_up = jnp.einsum(
        "bld,blf->df", normalized_lowered, dup_proj, preferred_element_type=jnp.float32
    )
    dnormed = (
        dresid_two
        + jnp.einsum("blf,df->bld", dgate_proj, gate_weight, preferred_element_type=jnp.float32)
        + jnp.einsum("blf,df->bld", dup_proj, up_weight, preferred_element_type=jnp.float32)
    )
    dresid_one, dgain_one, dbias_one = norm_back(dnormed, unit_one, scale_one, norm_params[0])
    dattn_out = dresid_one.astype(jnp.bfloat16)
    grad_out = jnp.einsum(
        "ble,bld->ed", attention_output, dattn_out, preferred_element_type=jnp.float32
    )
    dattended = jnp.einsum(
        "bld,ed->ble", dattn_out, output_weight, preferred_element_type=jnp.float32
    ).astype(jnp.bfloat16)
    dqueries, dkeys_all, dvalues_all = lax.map(
        attend_back, (queries, all_keys, all_values, seg_rows, seg_keys, log_sum, dattended)
    )
    dkey_rows, dvalue_rows = (
        lax.psum_scatter(
            dkeys_all.astype(jnp.bfloat16), "ctx", scatter_dimension=1, tiled=True
        ).astype(jnp.float32),
        lax.psum_scatter(
            dvalues_all.astype(jnp.bfloat16), "ctx", scatter_dimension=1, tiled=True
        ).astype(jnp.float32),
    )
    shaped = dqueries.shape[:2] + (dqueries.shape[2] // HEAD, HEAD)
    dmixed = jnp.concatenate(
        [
            unrotate(dqueries.reshape(shaped), cosine, sine_table).reshape(dqueries.shape),
            unrotate(dkey_rows.reshape(shaped), cosine, sine_table).reshape(dqueries.shape),
            dvalue_rows,
        ],
        axis=-1,
    ).astype(jnp.bfloat16)
    grad_qkv = jnp.einsum("bld,ble->de", hidden_state, dmixed, preferred_element_type=jnp.float32)
    dhidden = dresid_one + jnp.einsum(
        "ble,de->bld", dmixed, query_key_value_weight, preferred_element_type=jnp.float32
    )
    return (
        dhidden,
        (
            grad_qkv,
            grad_out,
            grad_gate,
            grad_up,
            grad_down,
            jnp.stack([dgain_one, dbias_one, dgain_two, dbias_two]),
        ),
    )


def relay_on_device(
    tokens,
    seg_ids,
    query_key_value_weight,
    output_weight,
    gate_weight,
    up_weight,
    down_weight,
    norm1_gain,
    norm1_bias,
    norm2_gain,
    norm2_bias,
    cotangent,
):
    leading = lax.axis_index("section") == 0
    ctx_rank = lax.axis_index("ctx")
    span_len = tokens.shape[1]
    per_micro = tokens.shape[0] // MICRO
    seg_near = lax.dynamic_slice_in_dim(seg_ids, ctx_rank * span_len, span_len, 1)
    cosine_rows, sine_rows = rope_tables(
        lax.dynamic_slice_in_dim(positions(seg_ids), ctx_rank * span_len, span_len, 1), HEAD // 2
    )
    shards = (
        query_key_value_weight[0],
        output_weight[0],
        gate_weight[0],
        up_weight[0],
        down_weight[0],
        jnp.stack([norm1_gain[0], norm1_bias[0], norm2_gain[0], norm2_bias[0]]),
    )
    gathered = (
        lax.all_gather(shards[0], "dp", axis=0, tiled=True),
        lax.all_gather(shards[1], "dp", axis=0, tiled=True),
        lax.all_gather(shards[2], "dp", axis=0, tiled=True),
        lax.all_gather(shards[3], "dp", axis=0, tiled=True),
        lax.all_gather(shards[4], "dp", axis=0, tiled=True),
        lax.all_gather(shards[5], "dp", axis=1, tiled=True),
    )
    weights_full = gathered[:5] + (gathered[5].astype(jnp.float32),)

    def select(array, micro_idx):
        return lax.dynamic_slice_in_dim(array, micro_idx * per_micro, per_micro, 0)

    delay_fwd = jnp.where(leading, 0, 1)
    received = jnp.zeros((per_micro,) + tokens.shape[1:], jnp.bfloat16)
    outputs = []
    stored = []
    for tick_no in range(MICRO + 1):
        micro_idx = jnp.clip(tick_no - delay_fwd, 0, MICRO - 1)
        hidden_state = jnp.where(leading, select(tokens, micro_idx), received)
        output, kept = layer_forward(
            hidden_state,
            weights_full,
            select(seg_near, micro_idx),
            select(seg_ids, micro_idx),
            select(cosine_rows, micro_idx),
            select(sine_rows, micro_idx),
        )
        sent_rows = output.astype(jnp.bfloat16)
        outputs.append(sent_rows)
        stored.append(kept)
        if tick_no < MICRO:
            received = passed_along(sent_rows, "section", 1)
    gathered = (
        lax.all_gather(shards[0], "dp", axis=0, tiled=True),
        lax.all_gather(shards[1], "dp", axis=0, tiled=True),
        lax.all_gather(shards[2], "dp", axis=0, tiled=True),
        lax.all_gather(shards[3], "dp", axis=0, tiled=True),
        lax.all_gather(shards[4], "dp", axis=0, tiled=True),
        lax.all_gather(shards[5], "dp", axis=1, tiled=True),
    )
    weights_full = gathered[:5] + (gathered[5].astype(jnp.float32),)
    returned = jnp.zeros_like(received)
    totals = None
    input_parts = []
    for tick_no in range(MICRO + 1):
        micro_idx = jnp.clip(tick_no - 1 + delay_fwd, 0, MICRO - 1)
        active = jnp.where(leading, tick_no >= 1, tick_no < MICRO)
        incoming = jnp.where(
            leading, returned.astype(jnp.float32), select(cotangent, micro_idx).astype(jnp.float32)
        )
        incoming = jnp.where(active, incoming, 0.0)
        kept = jax.tree.map(
            lambda early, later: jnp.where(leading, early, later),
            stored[max(tick_no - 1, 0)],
            stored[min(tick_no + 1, MICRO)],
        )
        dhidden, grad_terms = layer_backward(
            incoming,
            kept,
            weights_full,
            select(seg_near, micro_idx),
            select(seg_ids, micro_idx),
            select(cosine_rows, micro_idx),
            select(sine_rows, micro_idx),
        )
        totals = (
            grad_terms
            if totals is None
            else tuple((early + later for early, later in zip(totals, grad_terms)))
        )
        input_parts.append(dhidden)
        if tick_no < MICRO:
            returned = passed_along(dhidden.astype(jnp.bfloat16), "section", -1)
    summed = (
        lax.psum_scatter(
            totals[0].astype(jnp.bfloat16), "dp", scatter_dimension=0, tiled=True
        ).astype(jnp.float32),
        lax.psum_scatter(
            totals[1].astype(jnp.bfloat16), "dp", scatter_dimension=0, tiled=True
        ).astype(jnp.float32),
        lax.psum_scatter(
            totals[2].astype(jnp.bfloat16), "dp", scatter_dimension=0, tiled=True
        ).astype(jnp.float32),
        lax.psum_scatter(
            totals[3].astype(jnp.bfloat16), "dp", scatter_dimension=0, tiled=True
        ).astype(jnp.float32),
        lax.psum_scatter(
            totals[4].astype(jnp.bfloat16), "dp", scatter_dimension=0, tiled=True
        ).astype(jnp.float32),
        lax.psum_scatter(
            totals[5].astype(jnp.bfloat16), "dp", scatter_dimension=1, tiled=True
        ).astype(jnp.float32),
    )
    summed = jax.tree.map(
        lambda part: part.astype(jnp.float32), lax.psum(for_sending(summed), "ctx")
    )
    last_rows = jnp.concatenate(
        [jnp.where(leading, outputs[micro_no], outputs[micro_no + 1]) for micro_no in range(MICRO)],
        axis=0,
    )
    input_grads = jnp.concatenate(
        [
            jnp.where(leading, input_parts[micro_no + 1], input_parts[micro_no])
            for micro_no in range(MICRO)
        ],
        axis=0,
    )
    norm_grads = summed[5]
    return (
        last_rows[None],
        input_grads[None],
        summed[0][None],
        summed[1][None],
        summed[2][None],
        summed[3][None],
        summed[4][None],
        norm_grads[0][None],
        norm_grads[1][None],
        norm_grads[2][None],
        norm_grads[3][None],
    )


NT = (((1,), (1,)), ((), ()))
TN = (((0,), (0,)), ((), ()))


def mm(left, right, dims=(((1,), (0,)), ((), ()))):
    return lax.dot_general(left, right, dims, preferred_element_type=jnp.float32)


def in_vmem():
    return pl.BlockSpec(memory_space=pltpu.VMEM)


def anywhere():
    return pl.BlockSpec(memory_space=pl.ANY)


def in_smem():
    return pl.BlockSpec(memory_space=pltpu.SMEM)


def kernel_call(
    body, out_shapes, in_specs, scratch, mbytes, cost, name, out_specs=None, grid=None, prefetch=False
):
    out_specs = [in_vmem()] * len(out_shapes) if out_specs is None else out_specs
    if prefetch:
        spec = {
            "grid_spec": pltpu.PrefetchScalarGridSpec(
                num_scalar_prefetch=1, grid=grid, in_specs=in_specs, out_specs=out_specs, scratch_shapes=scratch
            )
        }
    else:
        spec = {"in_specs": in_specs, "out_specs": out_specs, "scratch_shapes": scratch}
        if grid is not None:
            spec["grid"] = grid
    return pl.pallas_call(
        body,
        out_shape=out_shapes,
        **spec,
        compiler_params=pltpu.CompilerParams(vmem_limit_bytes=mbytes * 2**20),
        cost_estimate=pl.CostEstimate(flops=0, bytes_accessed=3 * 10**6 * cost, transcendentals=0),
        name=name,
    )


def shape_of(shape, dtype):
    return jax.ShapeDtypeStruct(shape, dtype)


def loads_of(place, pieces, first, width, scratch, sems, begin, blocks=1):
    dp_rank, core = place[0], place[1]
    count = pieces[0].shape[0]
    copies = []
    cuts = ((0, 0, 2, 0, 0, 0), (1, 0, 2, 1, 0, 0), (2, 0, 2, 2, 0, 0), (3, 0, 1, 3, 0, 0), (4, 0, 1, 3, 1, 0))
    cuts += ((5, 0, 2, 0, 0, 1), (6, 0, 2, 1, 0, 1), (6, 2, 2, 2, 0, 1), (7, 0, 2, 3, 0, 1))
    unit = count // 2
    for piece, source, size, flip, target, other in cuts:
        half = 1 - core if other else core
        for block in range(blocks):
            row = ((dp_rank ^ flip) * blocks + block) * count + target * unit
            copies.append(
                pltpu.make_async_copy(
                    pieces[piece].at[pl.ds(source * unit, size * unit), pl.ds(first + block * width, width)],
                    scratch.at[
                        pl.ds(pl.multiple_of(row, unit), size * unit),
                        pl.ds(pl.multiple_of(half * width, 128), width),
                    ],
                    sems.at[begin + len(copies)],
                )
            )
    return copies


def start_loads(*arguments):
    copies = loads_of(*arguments)
    start_all(copies)
    return copies


def start_all(copies):
    for copy in copies:
        copy.start()


def wait_all(copies):
    for copy in copies:
        copy.wait()


def turn(values, cosine, sine):
    lane = lax.broadcasted_iota(jnp.int32, values.shape, 1)
    swapped = jnp.where(
        lane % 64 < 32, pltpu.roll(values, 96, 1), pltpu.roll(values, 32, 1)
    )
    return values * cosine + swapped * sine


def project_rows(place, hidden, cosine, sine, pieces):
    rows, width = hidden.shape
    half = 3 * width // 2

    def body(place_ref, hidden_ref, cos_ref, sin_ref, *refs):
        parts, (q_ref, kv_ref, weight, sems) = refs[:8], refs[8:]
        wait_all(start_loads(place_ref, parts, 0, half, weight, sems, 0))
        for step in range(3 * width // 256):
            mixed = mm(hidden_ref[...], weight[:, step * 256 : step * 256 + 256])
            for pair in range(2):
                column = step * 256 + pair * 128
                part = mixed[:, pair * 128 : pair * 128 + 128]
                which, lane = column // width, column % width
                if which < 2:
                    part = turn(part, cos_ref[...], sin_ref[...])
                if which == 0:
                    q_ref[:, lane : lane + 128] = (
                        part.astype(jnp.bfloat16).astype(jnp.float32) * HEAD**-0.5
                    ).astype(jnp.bfloat16)
                else:
                    kv_ref[which - 1, :, lane : lane + 128] = part.astype(jnp.bfloat16)

    return kernel_call(
        body,
        [shape_of((rows, width), jnp.bfloat16), shape_of((2, rows, width), jnp.bfloat16)],
        [in_smem()] + [in_vmem()] * 3 + [anywhere()] * 8,
        [pltpu.VMEM((width, 3 * width), jnp.bfloat16), pltpu.SemaphoreType.DMA((10,))],
        60,
        3,
        "project_rows",
    )(place, hidden, cosine, sine, *pieces)


def attend_rows(queries, blocks, seg_column, seg_row):
    rows, width = queries.shape
    keys = 2 * rows

    def body(col_ref, row_ref, q_ref, b0, b1, out_ref, sum_ref, bias, sums):
        step = pl.program_id(0)

        @pl.when(step == 0)
        def _():
            bias[...] = jnp.where(col_ref[...] == row_ref[...], 0.0, NEG)
            sums[...] = jnp.zeros_like(sums)

        lane = lax.broadcasted_iota(jnp.int32, (rows, 128), 1)
        query = q_ref[...]
        key = jnp.concatenate([b[0] for b in (b0, b1)], axis=0)
        value = jnp.concatenate([b[1] for b in (b0, b1)], axis=0)
        results = []
        for head in range(2):
            own = (lane < 64) if head == 0 else (lane >= 64)
            scores = mm(jnp.where(own, query, jnp.zeros_like(query)), key, NT) + bias[...]
            top = jnp.max(scores, axis=1, keepdims=True)
            exponent = jnp.exp(scores - top)
            total = jnp.sum(exponent, axis=1, keepdims=True)
            results.append(mm(exponent.astype(jnp.bfloat16), value) / total)
            sums[...] = jnp.where(lane == 2 * step + head, top + jnp.log(total), sums[...])
        out_ref[...] = jnp.where(lane < 64, results[0], results[1]).astype(jnp.bfloat16)

        @pl.when(step == width // 128 - 1)
        def _():
            sum_ref[...] = sums[...].T

    block = pl.BlockSpec((2, rows, 128), lambda j: (0, 0, j))
    return kernel_call(
        body,
        [shape_of((rows, width), jnp.bfloat16), shape_of((128, rows), jnp.float32)],
        [
            pl.BlockSpec((rows, 1), lambda j: (0, 0)),
            pl.BlockSpec((1, keys), lambda j: (0, 0)),
            pl.BlockSpec((rows, 128), lambda j: (0, j)),
            block, block,
        ],
        [pltpu.VMEM((rows, keys), jnp.float32), pltpu.VMEM((rows, 128), jnp.float32)],
        60,
        8,
        "attend_rows",
        [pl.BlockSpec((rows, 128), lambda j: (0, j)), pl.BlockSpec((128, rows), lambda j: (0, 0))],
        (width // 128,),
    )(seg_column, seg_row, queries, *blocks)


def attend_rows_back(queries, blocks, seg_row, seg_column, attended, sums, incoming):
    rows, width = queries.shape
    keys = 2 * rows

    def body(row_ref, col_ref, sum_ref, q_ref, att_ref, in_ref, b0, b1, dq_ref, own_ref, core_ref, bias):
        step = pl.program_id(0)

        @pl.when(step == 0)
        def _():
            bias[...] = jnp.where(col_ref[...] == row_ref[...], 0.0, NEG)

        lane = lax.broadcasted_iota(jnp.int32, (rows, 128), 1)
        query, given = q_ref[...], in_ref[...]
        key = jnp.concatenate([b[0] for b in (b0, b1)], axis=0)
        value = jnp.concatenate([b[1] for b in (b0, b1)], axis=0)
        key_t = key.T
        inner = (given.astype(jnp.float32) * att_ref[...].astype(jnp.float32)).T
        dkeys, dvalues, dqueries = [], [], []
        for head in range(2):
            own = (lane < 64) if head == 0 else (lane >= 64)
            scores = mm(key, jnp.where(own, query, jnp.zeros_like(query)), NT) + bias[...]
            probs = jnp.exp(scores - sum_ref[pl.ds(2 * step + head, 1), :])
            dvalues.append(mm(probs.astype(jnp.bfloat16), given))
            dprobs = mm(value, jnp.where(own, given, jnp.zeros_like(given)), NT)
            inner_row = jnp.sum(inner[64 * head : 64 * head + 64], axis=0, keepdims=True)
            dscores = (probs * (dprobs - inner_row)).astype(jnp.bfloat16)
            dkeys.append(mm(dscores, query))
            dqueries.append(mm(key_t[64 * head : 64 * head + 64], dscores))
        dq_ref[...] = jnp.concatenate(dqueries, axis=0).T * HEAD**-0.5
        wide = lax.broadcasted_iota(jnp.int32, (keys, 128), 1) < 64
        for which, pair in enumerate((dkeys, dvalues)):
            both = jnp.where(wide, pair[0], pair[1]).astype(jnp.bfloat16)
            own_ref[which] = both[:rows]
            core_ref[which] = both[rows:]

    block = pl.BlockSpec((2, rows, 128), lambda j: (0, 0, j))
    columns = pl.BlockSpec((rows, 128), lambda j: (0, j))
    pair_shape = shape_of((2, rows, width), jnp.bfloat16)
    return kernel_call(
        body,
        [
            shape_of((rows, width), jnp.float32),
            pair_shape,
            pair_shape,
        ],
        [
            pl.BlockSpec((1, rows), lambda j: (0, 0)),
            pl.BlockSpec((keys, 1), lambda j: (0, 0)),
            pl.BlockSpec((128, rows), lambda j: (0, 0)),
            columns, columns, columns, block, block,
        ],
        [pltpu.VMEM((keys, rows), jnp.float32)],
        60,
        18,
        "attend_rows_back",
        [columns, block, block],
        (width // 128,),
    )(seg_row, seg_column, sums, queries, attended, incoming, *blocks)


def unit_of(resid):
    centred = resid - jnp.mean(resid, axis=1, keepdims=True)
    scaling = lax.rsqrt(jnp.mean(centred * centred, axis=1, keepdims=True) + EPS)
    return centred * scaling, scaling


def norm_rows_back(incoming, unit, scaling, gain):
    scaled = incoming * gain
    return scaling * (
        scaled
        - jnp.mean(scaled, axis=1, keepdims=True)
        - unit * jnp.mean(scaled * unit, axis=1, keepdims=True)
    )


FF_STEP = 512


def mlp_scratch(width, hidden_width):
    return [
        pltpu.VMEM((width, width), jnp.bfloat16),
        pltpu.VMEM((width, hidden_width), jnp.bfloat16),
        pltpu.VMEM((width, hidden_width), jnp.bfloat16),
        pltpu.VMEM((hidden_width, width), jnp.bfloat16),
        pltpu.VMEM((width, 256), jnp.bfloat16),
        pltpu.VMEM((128, width), jnp.float32),
        pltpu.SemaphoreType.DMA((80,)),
    ]


def mlp_loads(place_ref, parts, scratch, width, ff_half):
    w_out, w_gate, w_up, w_down, w_norm, _, sems = scratch
    return (
        loads_of(place_ref, parts[:8], 2 * width, 128, w_norm, sems, 70),
        loads_of(place_ref, parts[:8], 3 * width // 2, width // 2, w_out, sems, 0),
        loads_of(place_ref, parts[8:], 0, ff_half, w_gate, sems, 10),
        loads_of(place_ref, parts[8:], ff_half, ff_half, w_up, sems, 20),
        loads_of(place_ref, parts[8:], 2 * ff_half, width // 2, w_down, sems, 30, 4),
    )


MINE = 5


def mlp_blocks(ff):
    steps = ff // FF_STEP
    return steps, lambda j, place: (place[1] ^ (j // (steps // 2))) * (steps // 2) + j % (steps // 2)


def mlp_rows(place, hidden, attended, first_parts, rest_parts):
    rows, width = hidden.shape
    ff_half = (rest_parts[0].shape[1] - 2 * width) // 2
    ff = 2 * ff_half
    steps, block_of = mlp_blocks(ff)

    def body(place_ref, hidden_ref, att_ref, *refs):
        parts, rest = refs[:16], refs[16:]
        out_ref, one_ref, two_ref, normed_ref, mid_ref, gate_ref, up_ref = rest[:7]
        w_out, w_gate, w_up, w_down, w_norm, norm_ref, _ = rest[7:]
        step = pl.program_id(0)
        norm, out, gates, ups, downs = mlp_loads(place_ref, parts, rest[7:], width, ff_half)

        @pl.when(step == 0)
        def _():
            for copies in (norm, out, gates[:MINE], ups[:MINE], downs, gates[MINE:], ups[MINE:]):
                start_all(copies)
            wait_all(norm)
            norm_ref[...] = w_norm[:, :128].astype(jnp.float32).T
            wait_all(out)
            resid = hidden_ref[...].astype(jnp.float32) + mm(att_ref[...], w_out[...])
            one_ref[...] = resid
            normed = unit_of(resid)[0] * norm_ref[0:1] + norm_ref[1:2]
            normed_ref[...] = normed.astype(jnp.bfloat16)
            two_ref[...] = normed
            wait_all(gates[:MINE])
            wait_all(ups[:MINE])

        @pl.when(step == steps // 2)
        def _():
            wait_all(gates[MINE:])
            wait_all(ups[MINE:])

        span = pl.ds(pl.multiple_of(block_of(step, place_ref) * FF_STEP, FF_STEP), FF_STEP)
        gate = mm(normed_ref[...], w_gate[:, span])
        up = mm(normed_ref[...], w_up[:, span])
        gate_ref[...] = gate.astype(jnp.bfloat16)
        up_ref[...] = up.astype(jnp.bfloat16)
        middle = (gate * jax.nn.sigmoid(gate) * up).astype(jnp.bfloat16)
        mid_ref[...] = middle

        @pl.when(step == 0)
        def _():
            wait_all(downs)

        two_ref[...] += mm(middle, w_down[span, :])

        @pl.when(step == steps - 1)
        def _():
            out_ref[...] = (unit_of(two_ref[...])[0] * norm_ref[2:3] + norm_ref[3:4]).astype(jnp.bfloat16)

    whole = pl.BlockSpec((rows, width), lambda j, place: (0, 0))
    part = pl.BlockSpec((rows, FF_STEP), lambda j, place: (0, block_of(j, place)))
    return kernel_call(
        body,
        [
            shape_of((rows, width), jnp.bfloat16),
            shape_of((rows, width), jnp.float32),
            shape_of((rows, width), jnp.float32),
            shape_of((rows, width), jnp.bfloat16),
            shape_of((rows, ff), jnp.bfloat16),
            shape_of((rows, ff), jnp.bfloat16),
            shape_of((rows, ff), jnp.bfloat16),
        ],
        [whole, whole] + [anywhere()] * 16,
        mlp_scratch(width, ff),
        60,
        16,
        "mlp_rows",
        [whole] * 4 + [part] * 3,
        (steps,),
        True,
    )(place, hidden, attended, *first_parts, *rest_parts)


def mlp_rows_back(place, incoming, one, two, gate, up, first_parts, rest_parts, for_weights):
    rows, width = incoming.shape
    ff_half = (rest_parts[0].shape[1] - 2 * width) // 2
    ff = 2 * ff_half
    steps, block_of = mlp_blocks(ff)
    extra = 6 if for_weights else 0

    def body(place_ref, in_ref, one_ref, two_ref, gate_ref, up_ref, *refs):
        parts, outs, rest = refs[:16], refs[16 : 18 + extra], refs[18 + extra :]
        dresid_ref, datt_ref = outs[:2]
        w_out, w_gate, w_up, w_down, w_norm, norm_ref, _, low_ref, sums_ref = rest
        step = pl.program_id(0)
        norm, out, gates, ups, downs = mlp_loads(place_ref, parts, rest[:7], width, ff_half)

        def share(column):
            half = width // 2
            low, first = low_ref[...], place_ref[1] == 0
            for ref, mine in ((outs[2], True), (outs[3], False)):
                ref[:rows, column : column + half] = jnp.where(
                    first == mine, low[:, :half], low[:, half:]
                )

        @pl.when(step == 0)
        def _():
            for copies in (norm, downs, gates[:MINE], ups[:MINE], gates[MINE:], ups[MINE:], out):
                start_all(copies)
            wait_all(norm)
            norm_ref[...] = w_norm[:, :128].astype(jnp.float32).T
            given = in_ref[...].astype(jnp.float32)
            unit, scaling = unit_of(two_ref[...])
            dresid_two = norm_rows_back(given, unit, scaling, norm_ref[2:3])
            dresid_ref[...] = dresid_two
            low_ref[...] = dresid_two.astype(jnp.bfloat16)
            if for_weights:
                sums_ref[...] = jnp.zeros_like(sums_ref)
                sums_ref[2:3] = jnp.sum(given * unit, axis=0, keepdims=True)
                sums_ref[3:4] = jnp.sum(given, axis=0, keepdims=True)
                share(0)
            wait_all(downs)
            wait_all(gates[:MINE])
            wait_all(ups[:MINE])

        @pl.when(step == steps // 2)
        def _():
            wait_all(gates[MINE:])
            wait_all(ups[MINE:])

        span = pl.ds(pl.multiple_of(block_of(step, place_ref) * FF_STEP, FF_STEP), FF_STEP)
        dmiddle = mm(low_ref[...], w_down[span, :], NT)
        gate_block = gate_ref[...].astype(jnp.float32)
        sig = jax.nn.sigmoid(gate_block)
        swish = gate_block * sig
        dup = (dmiddle * swish).astype(jnp.bfloat16)
        dgate = (dmiddle * up_ref[...].astype(jnp.float32) * (sig + swish * (1.0 - sig))).astype(jnp.bfloat16)
        if for_weights:
            @pl.when(step < steps // 2)
            def _():
                outs[4][...], outs[5][...] = dgate, dup

            @pl.when(step >= steps // 2)
            def _():
                outs[6][...], outs[7][...] = dgate, dup

        dresid_ref[...] += mm(dgate, w_gate[:, span], NT) + mm(dup, w_up[:, span], NT)

        @pl.when(step == steps - 1)
        def _():
            wait_all(out)
            dnormed = dresid_ref[...]
            unit, scaling = unit_of(one_ref[...])
            dresid_one = norm_rows_back(dnormed, unit, scaling, norm_ref[0:1])
            dresid_ref[...] = dresid_one
            low_ref[...] = dresid_one.astype(jnp.bfloat16)
            if for_weights:
                sums_ref[0:1] = jnp.sum(dnormed * unit, axis=0, keepdims=True)
                sums_ref[1:2] = jnp.sum(dnormed, axis=0, keepdims=True)
                share(width // 2)
                for ref in outs[2:4]:
                    ref[rows:] = sums_ref[...].astype(jnp.bfloat16)
            datt_ref[...] = mm(low_ref[...], w_out[...], NT).astype(jnp.bfloat16)

    half_steps = steps // 2
    whole = pl.BlockSpec((rows, width), lambda j, place: (0, 0))
    longer = pl.BlockSpec((rows + 16, width), lambda j, place: (0, 0))
    part = pl.BlockSpec((rows, FF_STEP), lambda j, place: (0, block_of(j, place)))
    mine = pl.BlockSpec((rows, FF_STEP), lambda j, place: (0, jnp.minimum(j, half_steps - 1)))
    theirs = pl.BlockSpec((rows, FF_STEP), lambda j, place: (0, jnp.maximum(j - half_steps, 0)))
    shapes = [shape_of((rows, width), jnp.float32), shape_of((rows, width), jnp.bfloat16)]
    specs = [whole, whole]
    if for_weights:
        shapes += [shape_of((rows + 16, width), jnp.bfloat16)] * 2 + [shape_of((rows, ff_half), jnp.bfloat16)] * 4
        specs += [longer] * 2 + [mine] * 2 + [theirs] * 2
    return kernel_call(
        body,
        shapes,
        [whole, whole, whole, part, part] + [anywhere()] * 16,
        mlp_scratch(width, ff) + [pltpu.VMEM((rows, width), jnp.bfloat16), pltpu.VMEM((16, width), jnp.float32)],
        60,
        21,
        "mlp_rows_back",
        specs,
        (steps,),
        True,
    )(place, incoming, one, two, gate, up, *first_parts, *rest_parts)


def project_rows_back(place, dqueries, sums, dresid_one, cosine, sine, pieces):
    rows, width = dqueries.shape
    half = 3 * width // 2
    count = len(sums)

    def body(place_ref, dq_ref, resid_ref, cos_ref, sin_ref, *refs):
        parts, rest = refs[:8], refs[8:]
        sum_refs, (keep_ref, send_ref, dhidden_ref, weight, sems, dmixed_ref) = rest[:count], rest[count:]
        core = place_ref[1]
        loads = start_loads(place_ref, parts, 0, half, weight, sems, 0)
        for column in range(0, 3 * width, 128):
            which, lane = column // width, column % width
            span = slice(lane, lane + 128)
            if which == 0:
                part = dq_ref[:, span]
            else:
                part = sum(ref[which - 1, :, span].astype(jnp.float32) for ref in sum_refs)
            if which < 2:
                part = turn(part, cos_ref[...], -sin_ref[...])
            dmixed_ref[:, column : column + 128] = part.astype(jnp.bfloat16)
        for index in range(2):
            @pl.when(core == index)
            def _():
                keep_ref[...] = dmixed_ref[:, index * half : (index + 1) * half]
                send_ref[...] = dmixed_ref[:, (1 - index) * half : (2 - index) * half]

        wait_all(loads)
        dhidden_ref[...] = resid_ref[...] + mm(dmixed_ref[...], weight[...], NT)

    return kernel_call(
        body,
        [
            shape_of((rows, half), jnp.bfloat16),
            shape_of((rows, half), jnp.bfloat16),
            shape_of((rows, width), jnp.float32),
        ],
        [in_smem()] + [in_vmem()] * 4 + [anywhere()] * 8 + [in_vmem()] * count,
        [
            pltpu.VMEM((width, 3 * width), jnp.bfloat16),
            pltpu.SemaphoreType.DMA((10,)),
            pltpu.VMEM((rows, 3 * width), jnp.bfloat16),
        ],
        60,
        6,
        "project_rows_back",
    )(place, dqueries, dresid_one, cosine, sine, *pieces, *sums)


def grad_parts(place, groups, sums=None):
    jobs = [job for group in groups for job in group]
    rows = jobs[0][0][0].shape[0]
    lefts, rights, arrays = [], [], []
    for left, left_span, right, right_span, blocks in jobs:
        for known, entry in ((lefts, (left, left_span)), (rights, (right, right_span))):
            if not any(entry[0] is other[0] and entry[1] == other[1] for other in known):
                known.append(entry)
        for array in (*left, *right):
            if not any(array is other for other in arrays):
                arrays.append(array)
    where = lambda array: next(i for i, other in enumerate(arrays) if other is array)
    slot = lambda known, pair, span: next(
        i for i, other in enumerate(known) if other[0] is pair and other[1] == span
    )
    count = (jobs[0][1][1] - jobs[0][1][0]) // 4 // jobs[0][4]
    totals = [sum((job[3][1] - job[3][0]) * job[4] for job in group) for group in groups]
    widths = list(totals)
    if sums is not None:
        widths[0] += 128

    def body(place_ref, *refs):
        inputs, refs = refs[: len(arrays)], refs[len(arrays) :]
        outs, refs = refs[: 5 * len(groups)], refs[5 * len(groups) :]
        block, left_refs, right_refs = refs[0], refs[1 : 1 + len(lefts)], refs[1 + len(lefts) :]
        for ref, (pair, span) in zip(left_refs, lefts):
            for core in range(2):
                ref[:, core * rows : (core + 1) * rows] = inputs[where(pair[core])][:rows, span[0] : span[1]].T
        for ref, (pair, span) in zip(right_refs, rights):
            for core in range(2):
                ref[core * rows : (core + 1) * rows] = inputs[where(pair[core])][:rows, span[0] : span[1]]
        if sums is not None:
            padded, turned = refs[-2:]
            padded[...] = jnp.zeros_like(padded)
            padded[:16] = sum(
                inputs[where(array)][rows:, : 4 * count].astype(jnp.float32) for array in jobs[sums][2]
            )
            turned[...] = padded[...].T
        upper, lower = slice(0, count // 2), slice(count // 2, count)
        for index, group in enumerate(groups):
            own_ref, x_ref, y_ref, xl_ref, yu_ref = outs[5 * index : 5 * index + 5]
            end = widths[index]
            for flip in range(4):
                target = 0
                for left, left_span, right, right_span, blocks in group:
                    left_t, right_all = left_refs[slot(lefts, left, left_span)], right_refs[slot(rights, right, right_span)]
                    width = right_span[1] - right_span[0]
                    tile = 512 if width % 512 == 0 else 384
                    for part in range(blocks):
                        begin = ((place_ref[0] ^ flip) * blocks + part) * count
                        rows_t = left_t[pl.ds(pl.multiple_of(begin, count), count), :]
                        for column in range(0, width, tile):
                            block[:, target : target + tile] = mm(
                                rows_t, right_all[:, column : column + tile]
                            ).astype(jnp.bfloat16)
                            target += tile
                if target < end:
                    begin = pl.multiple_of((place_ref[0] ^ flip) * count, count)
                    block[:, target:end] = turned[pl.ds(begin, count), :].astype(jnp.bfloat16)
                if flip == 0:
                    own_ref[...] = block[:, :end]
                elif flip == 1:
                    x_ref[upper] = block[upper, :end]
                    xl_ref[...] = block[lower, :end]
                elif flip == 2:
                    y_ref[upper] = block[lower, :end]
                    yu_ref[...] = block[upper, :end]
                else:
                    x_ref[lower] = block[upper, :end]
                    y_ref[lower] = block[lower, :end]

    scratch = [pltpu.VMEM((count, max(widths)), jnp.bfloat16)]
    scratch += [pltpu.VMEM((span[1] - span[0], 2 * rows), jnp.bfloat16) for _, span in lefts]
    scratch += [pltpu.VMEM((2 * rows, span[1] - span[0]), jnp.bfloat16) for _, span in rights]
    if sums is not None:
        scratch += [pltpu.VMEM((128, 4 * count), jnp.float32), pltpu.VMEM((4 * count, 128), jnp.float32)]
    shapes = []
    for width in widths:
        shapes += [shape_of((count, width), jnp.bfloat16)] * 3 + [shape_of((count // 2, width), jnp.bfloat16)] * 2
    made = kernel_call(
        body, shapes, [in_smem()] + [in_vmem()] * len(arrays), scratch, 60, 7, "grad_parts"
    )(place, *arrays)
    return [made[5 * index : 5 * index + 5] for index in range(len(groups))]


def to_core(value):
    return lax.ppermute(value, "section", [(0, 1), (1, 0)])


def along_x(value):
    return lax.ppermute(value, "dp", [(i, i ^ 1) for i in range(4)])


def along_y(value):
    return lax.ppermute(value, "dp", [(i, i ^ 2) for i in range(4)])


def along_z(value):
    return lax.ppermute(value, "ctx", [(i, i ^ 1) for i in range(4)])


def near_blocks(value):
    pairs = [(i, i ^ 1) for i in range(4)] + [(4 + i, 4 + (i ^ 2)) for i in range(4)]
    return lax.ppermute(value, ("section", "ctx"), pairs)


def far_blocks(value):
    return lax.ppermute(value, ("section", "ctx"), [(4 + i, 4 + (i ^ 3)) for i in range(4)])


def same_role(value):
    return lax.ppermute(value, "ctx", [(i, i ^ 3) for i in range(4)])


def lowered(value):
    return value.astype(jnp.bfloat16)


def wide(value):
    return value.astype(jnp.float32)


def by_core(core, mine, theirs, axis):
    return jnp.where(
        core == 0,
        jnp.concatenate([mine, theirs], axis=axis),
        jnp.concatenate([theirs, mine], axis=axis),
    )


def half_of(array, which):
    width = array.shape[-1] // 2
    return lax.dynamic_slice_in_dim(array, which * width, width, array.ndim - 1)


def after(value, *others):
    return lax.optimization_barrier((value, *others))[0]


def gather_near(pieces, *others):
    own = after(pieces[0], *others)
    return [own, along_x(own), along_y(own), pieces[1]]


def gather_far(near, *others):
    rows = near[0].shape[0] // 2
    return [along_x(after(near[2][:rows], *others)), along_y(after(near[1][rows:], *others))]


def both_cores(near, far):
    return [
        *near[:3],
        *far,
        near[3],
        to_core(jnp.concatenate(near[1:3], axis=0)),
        to_core(jnp.concatenate(far, axis=0)),
    ]


def reduce_first(parts, *others):
    return along_x(after(parts[1], *others)), along_y(after(parts[2], *others))


def reduce_second(parts, first, *others):
    _, _, _, x_lower, y_upper = after(tuple(parts), *others)
    from_x, from_y = first
    rows = x_lower.shape[0]
    return (
        along_x(lowered(wide(x_lower) + wide(from_y[rows:]))),
        along_y(lowered(wide(y_upper) + wide(from_x[rows:]))),
    )


def reduce_last(parts, first, second):
    from_x, from_y = first
    rows = second[0].shape[0]
    return lowered(
        wide(parts[0])
        + jnp.concatenate(
            [wide(from_x[:rows]) + wide(second[1]), wide(from_y[:rows]) + wide(second[0])], axis=0
        )
    )


def reduce_ctx(pieces, middle, last):
    received = [same_role(pieces[0])]
    mine, others = [], []
    for index, piece in enumerate(pieces):
        mine.append(lowered(wide(piece) + wide(after(received[index], *last))))
        last = (mine[index],)
        others.append(along_z(mine[index]))
        if index + 1 < len(pieces):
            ready = pieces[index + 1] if index == 0 else after(pieces[index + 1], received[index - 1], mine[index - 1])
            received.append(same_role(ready))
    return [
        (jnp.where(middle, theirs, own), jnp.where(middle, own, theirs)) for own, theirs in zip(mine, others)
    ]


def paired_on_device(
    tokens,
    seg_ids,
    query_key_value_weight,
    output_weight,
    gate_weight,
    up_weight,
    down_weight,
    norm1_gain,
    norm1_bias,
    norm2_gain,
    norm2_bias,
    cotangent,
):
    core, ctx_rank, dp_rank = (lax.axis_index(a) for a in ("section", "ctx", "dp"))
    span, width = tokens.shape[1], tokens.shape[2]
    sequence = ctx_rank // 2
    middle = (ctx_rank == 1) | (ctx_rank == 2)
    role = jnp.where(middle, 1, 0)
    even = ctx_rank % 2 == 0
    place = jnp.stack([dp_rank, core]).astype(jnp.int32)
    pick = lambda array, index: lax.dynamic_index_in_dim(array, index, 0, keepdims=False)

    def in_order(left, right):
        return jnp.where(even, jnp.concatenate([left, right]), jnp.concatenate([right, left]))

    def to_rows():
        mine, theirs = jnp.where(middle, cotangent, tokens), jnp.where(middle, tokens, cotangent)
        first = near_blocks(jnp.where(core == 0, pick(theirs, sequence), pick(theirs, 1 - sequence)))
        second = far_blocks(pick(mine, 1 - sequence))
        return in_order(
            jnp.where(core == 0, pick(mine, sequence), first), jnp.where(core == 0, first, second)
        )

    def send_rows(rows):
        halves = rows.reshape(2, span, width)
        left, right = pick(halves, jnp.where(even, 0, 1)), pick(halves, jnp.where(even, 1, 0))
        return left, near_blocks(jnp.where(core == 0, right, left)), far_blocks(right)

    def placed_rows(left, first, second):
        same = jnp.where(core == 0, left, second)
        first_layer, second_layer = jnp.where(middle, first, same), jnp.where(middle, same, first)
        other = to_core(jnp.where(core == 0, second_layer, first_layer))
        mine = jnp.where(core == 0, first_layer, second_layer)
        return jnp.where(
            sequence == core, jnp.stack([mine, other]), jnp.stack([other, mine])
        )[None]

    norm_columns = jnp.concatenate([norm1_gain, norm1_bias, norm2_gain, norm2_bias], axis=0).T
    norm_columns = jnp.pad(norm_columns, ((0, 0), (0, 124)))

    def first_pack(which):
        return jnp.concatenate(
            [half_of(query_key_value_weight[0], which), half_of(output_weight[0], which), norm_columns], axis=1
        )

    def rest_pack(which, *others):
        gate, up, down = after((gate_weight[0], up_weight[0], down_weight[0]), *others)
        return jnp.concatenate(
            [half_of(gate, which), half_of(up, which)]
            + jnp.split(half_of(down, which), down.shape[0] // gate.shape[0]),
            axis=1,
        )

    def choose(own, other, other_sent, own_sent):
        return jnp.where(core == role, own, other_sent), jnp.where(core == role, other, own_sent)

    own, other = first_pack(core), first_pack(1 - core)
    other_sent = to_core(other)
    first_pieces = choose(own, other, other_sent, to_core(after(own, other_sent)))
    own, other = rest_pack(core, other_sent), rest_pack(1 - core, other_sent)
    rest_pieces = choose(own, other, to_core(other), to_core(after(own, other_sent)))
    tokens, cotangent = after((tokens, cotangent), other_sent)

    seg = pick(seg_ids, sequence)
    rows = 2 * span
    begin = (sequence ^ core) * rows
    seg_rows = lax.dynamic_slice_in_dim(seg, begin, rows, 0)
    seg_keys = jnp.concatenate([seg_rows, lax.dynamic_slice_in_dim(seg, rows - begin, rows, 0)])
    begins = jnp.sum((seg[None, :] < seg_rows[:, None]).astype(jnp.int32), axis=1)
    places = begin + jnp.arange(rows, dtype=jnp.int32) - begins
    lanes = jnp.arange(128, dtype=jnp.int32) % HEAD
    half = HEAD // 2
    spread = 1000.0 ** (-2.0 * (lanes % half).astype(jnp.float32) / HEAD)
    angles = places.astype(jnp.float32)[:, None] * spread[None, :]
    cosine, sine = jnp.cos(angles), jnp.where(lanes < half, -1.0, 1.0) * jnp.sin(angles)

    def attention(hidden):
        queries, own = project_rows(place, hidden, cosine, sine, first)
        blocks = [own, to_core(own)]
        return queries, blocks, *attend_rows(queries, blocks, seg_rows[:, None], seg_keys[None, :])

    given = to_rows()
    near = gather_near(first_pieces)
    far = gather_far(near)
    near_mlp = gather_near(rest_pieces, *far)
    first = both_cores(near, far)
    queries, blocks, attended, sums = attention(given)
    near_mlp = [after(part, attended) for part in near_mlp]
    rest = both_cores(near_mlp, gather_far(near_mlp))
    output = mlp_rows(place, given, attended, first, rest)[0]

    hidden = jnp.where(middle, along_z(output), given)
    queries, blocks, attended, sums = attention(hidden)
    output, one, two, normed, mids, gate, up = mlp_rows(place, hidden, attended, first, rest)

    dresid_one, dattended = mlp_rows_back(place, given, one, two, gate, up, first, rest, False)
    sent_outputs = send_rows(output)
    dqueries, own, across = attend_rows_back(
        queries, blocks, seg_rows[None, :], seg_keys[:, None], attended, sums, after(dattended, *sent_outputs)
    )
    dhidden = project_rows_back(
        place, dqueries, (own, to_core(across)), dresid_one, cosine, sine, first
    )[2]
    incoming = jnp.where(middle, given, along_z(lowered(dhidden)))

    both = lambda value: (value, to_core(value))
    mids, normed, attended, hidden = both(mids), both(normed), both(attended), both(hidden)
    dresid_one, dattended, keep, send, keep_gate, keep_up, send_gate, send_up = mlp_rows_back(
        place, incoming, one, two, gate, up, first, rest, True
    )
    ff = mids[0].shape[1]
    right, right_gate, right_up = (keep, to_core(send)), (keep_gate, to_core(send_gate)), (keep_up, to_core(send_up))
    parts = grad_parts(
        place,
        [
            [
                (mids, (0, ff), right, (0, width // 2), ff // width),
                (attended, (0, width), right, (width // 2, width), 1),
            ]
        ],
        1,
    )
    normed = (after(normed[0], *parts[0]), normed[1])
    parts += grad_parts(place, [[(normed, (0, width), pair, (0, ff // 2), 1)] for pair in (right_gate, right_up)])
    dqueries, own, across = attend_rows_back(
        queries, blocks, seg_rows[None, :], seg_keys[:, None], attended[0], sums, after(dattended, *(x for part in parts for x in part))
    )
    near = [reduce_first(parts[0])]
    near.append(reduce_first(parts[1]))
    across = to_core(after(across, *near[0], *near[1]))
    far = [reduce_second(parts[0], near[0], across)]
    near.append(reduce_first(parts[2], across))
    keep, send, dhidden = project_rows_back(place, dqueries, (own, across), dresid_one, cosine, sine, first)
    keep = after(keep, *far[0])
    parts += grad_parts(place, [[(hidden, (0, width), (keep, to_core(send)), (0, 3 * width // 2), 1)]])
    near.append(reduce_first(parts[3]))
    far.append(reduce_second(parts[1], near[1], *parts[3]))
    far.append(reduce_second(parts[2], near[2], *parts[3]))
    far.append(reduce_second(parts[3], near[3]))
    pieces = [reduce_last(*group) for group in zip(parts, near, far)]
    pieces[1:] = [after(piece, *parts[3]) for piece in pieces[1:]]
    totals = reduce_ctx(pieces, middle, parts[3])

    pairs = []
    for first_layer, second_layer in totals:
        pairs.append(
            (
                jnp.where(core == 0, first_layer, second_layer),
                to_core(jnp.where(core == 0, second_layer, first_layer)),
            )
        )
    joined = lambda index, begin, end: wide(
        by_core(core, pairs[index][0][:, begin:end], pairs[index][1][:, begin:end], 1)
    )[None]
    norm_grads = wide(pairs[0][0][:, 5 * width // 2 : 5 * width // 2 + 4]).T
    pick_down = lambda which: jnp.concatenate(
        [pairs[0][which][:, i * width // 2 : (i + 1) * width // 2] for i in range(ff // width)]
    )
    grad_down = wide(by_core(core, pick_down(0), pick_down(1), 1))[None]

    return (
        placed_rows(*after(sent_outputs, *far[3])),
        wide(placed_rows(*send_rows(after(lowered(dhidden), *far[3])))),
        joined(3, 0, 3 * width // 2),
        joined(0, 2 * width, 5 * width // 2),
        joined(1, 0, ff // 2),
        joined(2, 0, ff // 2),
        grad_down,
        *(norm_grads[i : i + 1] for i in range(4)),
    )


def solution(mesh):
    placed = (
        P("dp", "ctx", None),
        P("dp", None),
        P("section", "dp", None),
        P("section", "dp", None),
        P("section", "dp", None),
        P("section", "dp", None),
        P("section", "dp", None),
        P("section", "dp"),
        P("section", "dp"),
        P("section", "dp"),
        P("section", "dp"),
        P("dp", "ctx", None),
    )
    paired = mesh.shape["section"] == 2 and mesh.shape["ctx"] == 4 and mesh.shape["dp"] == 4
    return jax.shard_map(
        paired_on_device if paired else relay_on_device,
        mesh=mesh,
        in_specs=placed,
        out_specs=(
            P("section", "dp", "ctx", None),
            P("section", "dp", "ctx", None),
            P("section", "dp", None),
            P("section", "dp", None),
            P("section", "dp", None),
            P("section", "dp", None),
            P("section", "dp", None),
            P("section", "dp"),
            P("section", "dp"),
            P("section", "dp"),
            P("section", "dp"),
        ),
        check_vma=False,
    )
```

```python
import jax
import jax.numpy as jnp
from jax import lax
from jax.experimental import pallas as pl
from jax.experimental.pallas import tpu as pltpu
from jax.sharding import PartitionSpec as P

HEAD = 64
MICRO = 2


EPS = 1e-05
NEG = -1e30


def passed_along(value, axis, steps):
    count = lax.axis_size(axis)
    first, last = (max(0, -steps), min(count, count - steps))
    return lax.ppermute(value, axis, [(source, source + steps) for source in range(first, last)])


def for_sending(array):
    return jax.tree.map(lambda a: a.astype(jnp.bfloat16) if a.dtype == jnp.float32 else a, array)


def positions(seg_ids):
    places = lax.broadcasted_iota(jnp.int32, seg_ids.shape, 1)
    begins = jnp.concatenate(
        [jnp.ones_like(seg_ids[:, :1]), (seg_ids[:, 1:] != seg_ids[:, :-1]).astype(jnp.int32)],
        axis=1,
    )
    return places - lax.cummax(places * begins, axis=1)


def rope_tables(places, half_dim):
    spread = 1000.0 ** (-2.0 * jnp.arange(half_dim, dtype=jnp.float32) / (2 * half_dim))
    angles = places.astype(jnp.float32)[..., None] * spread
    return (jnp.cos(angles), jnp.sin(angles))


def rotate(values, cosine, sine_table):
    half_dim = values.shape[-1] // 2
    former, latter = (values[..., :half_dim], values[..., half_dim:])
    cosine, sine_table = (cosine[..., None, :], sine_table[..., None, :])
    return jnp.concatenate(
        [former * cosine - latter * sine_table, latter * cosine + former * sine_table], axis=-1
    )


def unrotate(values, cosine, sine_table):
    half_dim = values.shape[-1] // 2
    former, latter = (values[..., :half_dim], values[..., half_dim:])
    cosine, sine_table = (cosine[..., None, :], sine_table[..., None, :])
    return jnp.concatenate(
        [former * cosine + latter * sine_table, latter * cosine - former * sine_table], axis=-1
    )


def norm_parts(resid, gain, bias):
    centred = resid - jnp.mean(resid, axis=-1, keepdims=True)
    scaling = lax.rsqrt(jnp.mean(centred * centred, axis=-1, keepdims=True) + EPS)
    unit_rows = centred * scaling
    return (unit_rows * gain + bias, unit_rows, scaling)


def norm_back(incoming, unit_rows, scaling, gain):
    scaled = incoming * gain
    inner = (
        scaled
        - jnp.mean(scaled, axis=-1, keepdims=True)
        - unit_rows * jnp.mean(scaled * unit_rows, axis=-1, keepdims=True)
    )
    return (
        scaling * inner,
        jnp.sum(incoming * unit_rows, axis=(0, 1)),
        jnp.sum(incoming, axis=(0, 1)),
    )


def masked_scores(queries, all_keys, seg_rows, seg_keys):
    row_count, model_width = queries.shape
    head_count = model_width // HEAD
    scores = jnp.einsum(
        "qhd,khd->hqk",
        queries.reshape(row_count, head_count, HEAD),
        all_keys.reshape(all_keys.shape[0], head_count, HEAD),
        preferred_element_type=jnp.float32,
    ) * HEAD ** (-0.5)
    return jnp.where((seg_rows[:, None] == seg_keys[None, :])[None], scores, NEG)


def attend(operands):
    queries, all_keys, all_values, seg_rows, seg_keys = operands
    row_count, model_width = queries.shape
    head_count = model_width // HEAD
    scores = masked_scores(queries, all_keys, seg_rows, seg_keys)
    row_max = jnp.max(scores, axis=-1, keepdims=True)
    exponent = jnp.exp(scores - row_max)
    row_sum = jnp.sum(exponent, axis=-1, keepdims=True)
    probs_low = (exponent / row_sum).astype(jnp.bfloat16)
    result = jnp.einsum(
        "hqk,khd->qhd",
        probs_low,
        all_values.reshape(all_values.shape[0], head_count, HEAD),
        preferred_element_type=jnp.float32,
    )
    return (result.reshape(row_count, model_width), (row_max + jnp.log(row_sum))[..., 0])


def attend_back(operands):
    queries, all_keys, all_values, seg_rows, seg_keys, log_sum, incoming = operands
    row_count, model_width = queries.shape
    head_count = model_width // HEAD
    key_count = all_keys.shape[0]
    probs = jnp.exp(masked_scores(queries, all_keys, seg_rows, seg_keys) - log_sum[..., None])
    heads_in = incoming.reshape(row_count, head_count, HEAD)
    dprobs = jnp.einsum(
        "qhd,khd->hqk",
        heads_in,
        all_values.reshape(key_count, head_count, HEAD),
        preferred_element_type=jnp.float32,
    )
    dscores = (probs * (dprobs - jnp.sum(probs * dprobs, axis=-1, keepdims=True))).astype(
        jnp.bfloat16
    )
    dquery = jnp.einsum(
        "hqk,khd->qhd",
        dscores,
        all_keys.reshape(key_count, head_count, HEAD),
        preferred_element_type=jnp.float32,
    ) * HEAD ** (-0.5)
    dkeys_part = jnp.einsum(
        "hqk,qhd->khd",
        dscores,
        queries.reshape(row_count, head_count, HEAD),
        preferred_element_type=jnp.float32,
    ) * HEAD ** (-0.5)
    dvalue = jnp.einsum(
        "hqk,qhd->khd", probs.astype(jnp.bfloat16), heads_in, preferred_element_type=jnp.float32
    )
    return (
        dquery.reshape(row_count, model_width),
        dkeys_part.reshape(key_count, model_width),
        dvalue.reshape(key_count, model_width),
    )


def layer_forward(hidden_state, weights_full, seg_rows, seg_keys, cosine, sine_table):
    query_key_value_weight, output_weight, gate_weight, up_weight, down_weight, norm_params = (
        weights_full
    )
    model_width = hidden_state.shape[-1]
    shaped = hidden_state.shape[:2] + (model_width // HEAD, HEAD)
    mixed_query_key_value = jnp.einsum(
        "bld,de->ble", hidden_state, query_key_value_weight, preferred_element_type=jnp.float32
    )
    queries = (
        rotate(mixed_query_key_value[..., :model_width].reshape(shaped), cosine, sine_table)
        .reshape(hidden_state.shape)
        .astype(jnp.bfloat16)
    )
    key_rows = (
        rotate(
            mixed_query_key_value[..., model_width : 2 * model_width].reshape(shaped),
            cosine,
            sine_table,
        )
        .reshape(hidden_state.shape)
        .astype(jnp.bfloat16)
    )
    value_rows = mixed_query_key_value[..., 2 * model_width :].astype(jnp.bfloat16)
    all_keys, all_values = (
        lax.all_gather(key_rows, "ctx", axis=1, tiled=True),
        lax.all_gather(value_rows, "ctx", axis=1, tiled=True),
    )
    attention_output, log_sum = lax.map(attend, (queries, all_keys, all_values, seg_rows, seg_keys))
    attention_output = attention_output.astype(jnp.bfloat16)
    residual_first = hidden_state.astype(jnp.float32) + jnp.einsum(
        "bld,de->ble", attention_output, output_weight, preferred_element_type=jnp.float32
    )
    normalized_rows, unit_one, scale_one = norm_parts(
        residual_first, norm_params[0], norm_params[1]
    )
    normalized_lowered = normalized_rows.astype(jnp.bfloat16)
    gate_projected = jnp.einsum(
        "bld,df->blf", normalized_lowered, gate_weight, preferred_element_type=jnp.float32
    )
    up_projected = jnp.einsum(
        "bld,df->blf", normalized_lowered, up_weight, preferred_element_type=jnp.float32
    )
    middle_state = (gate_projected * jax.nn.sigmoid(gate_projected) * up_projected).astype(
        jnp.bfloat16
    )
    residual_second = normalized_rows + jnp.einsum(
        "blf,fd->bld", middle_state, down_weight, preferred_element_type=jnp.float32
    )
    output, unit_two, scale_two = norm_parts(residual_second, norm_params[2], norm_params[3])
    extra = (all_keys, all_values)
    kept = (
        hidden_state,
        queries,
        key_rows,
        value_rows,
        log_sum,
        attention_output,
        unit_one,
        scale_one,
        gate_projected,
        up_projected,
        unit_two,
        scale_two,
    ) + extra
    return (output, kept)


def layer_backward(incoming, kept, weights_full, seg_rows, seg_keys, cosine, sine_table):
    query_key_value_weight, output_weight, gate_weight, up_weight, down_weight, norm_params = (
        weights_full
    )
    (
        hidden_state,
        queries,
        key_rows,
        value_rows,
        log_sum,
        attention_output,
        unit_one,
        scale_one,
        gate_projected,
        up_projected,
        unit_two,
        scale_two,
    ) = kept[:12]
    all_keys, all_values = (kept[12], kept[13])
    dresid_two, dgain_two, dbias_two = norm_back(incoming, unit_two, scale_two, norm_params[2])
    normalized_lowered = (unit_one * norm_params[0] + norm_params[1]).astype(jnp.bfloat16)
    sigmoid_gate = jax.nn.sigmoid(gate_projected)
    swish_gate = gate_projected * sigmoid_gate
    middle_state = (swish_gate * up_projected).astype(jnp.bfloat16)
    dout_two = dresid_two.astype(jnp.bfloat16)
    grad_down = jnp.einsum(
        "blf,bld->fd", middle_state, dout_two, preferred_element_type=jnp.float32
    )
    dmiddle = jnp.einsum("bld,fd->blf", dout_two, down_weight, preferred_element_type=jnp.float32)
    dgate_proj = (
        dmiddle * up_projected * sigmoid_gate * (1.0 + gate_projected * (1.0 - sigmoid_gate))
    ).astype(jnp.bfloat16)
    dup_proj = (dmiddle * swish_gate).astype(jnp.bfloat16)
    grad_gate = jnp.einsum(
        "bld,blf->df", normalized_lowered, dgate_proj, preferred_element_type=jnp.float32
    )
    grad_up = jnp.einsum(
        "bld,blf->df", normalized_lowered, dup_proj, preferred_element_type=jnp.float32
    )
    dnormed = (
        dresid_two
        + jnp.einsum("blf,df->bld", dgate_proj, gate_weight, preferred_element_type=jnp.float32)
        + jnp.einsum("blf,df->bld", dup_proj, up_weight, preferred_element_type=jnp.float32)
    )
    dresid_one, dgain_one, dbias_one = norm_back(dnormed, unit_one, scale_one, norm_params[0])
    dattn_out = dresid_one.astype(jnp.bfloat16)
    grad_out = jnp.einsum(
        "ble,bld->ed", attention_output, dattn_out, preferred_element_type=jnp.float32
    )
    dattended = jnp.einsum(
        "bld,ed->ble", dattn_out, output_weight, preferred_element_type=jnp.float32
    ).astype(jnp.bfloat16)
    dqueries, dkeys_all, dvalues_all = lax.map(
        attend_back, (queries, all_keys, all_values, seg_rows, seg_keys, log_sum, dattended)
    )
    dkey_rows, dvalue_rows = (
        lax.psum_scatter(
            dkeys_all.astype(jnp.bfloat16), "ctx", scatter_dimension=1, tiled=True
        ).astype(jnp.float32),
        lax.psum_scatter(
            dvalues_all.astype(jnp.bfloat16), "ctx", scatter_dimension=1, tiled=True
        ).astype(jnp.float32),
    )
    shaped = dqueries.shape[:2] + (dqueries.shape[2] // HEAD, HEAD)
    dmixed = jnp.concatenate(
        [
            unrotate(dqueries.reshape(shaped), cosine, sine_table).reshape(dqueries.shape),
            unrotate(dkey_rows.reshape(shaped), cosine, sine_table).reshape(dqueries.shape),
            dvalue_rows,
        ],
        axis=-1,
    ).astype(jnp.bfloat16)
    grad_qkv = jnp.einsum("bld,ble->de", hidden_state, dmixed, preferred_element_type=jnp.float32)
    dhidden = dresid_one + jnp.einsum(
        "ble,de->bld", dmixed, query_key_value_weight, preferred_element_type=jnp.float32
    )
    return (
        dhidden,
        (
            grad_qkv,
            grad_out,
            grad_gate,
            grad_up,
            grad_down,
            jnp.stack([dgain_one, dbias_one, dgain_two, dbias_two]),
        ),
    )


def relay_on_device(
    tokens,
    seg_ids,
    query_key_value_weight,
    output_weight,
    gate_weight,
    up_weight,
    down_weight,
    norm1_gain,
    norm1_bias,
    norm2_gain,
    norm2_bias,
    cotangent,
):
    leading = lax.axis_index("section") == 0
    ctx_rank = lax.axis_index("ctx")
    span_len = tokens.shape[1]
    per_micro = tokens.shape[0] // MICRO
    seg_near = lax.dynamic_slice_in_dim(seg_ids, ctx_rank * span_len, span_len, 1)
    cosine_rows, sine_rows = rope_tables(
        lax.dynamic_slice_in_dim(positions(seg_ids), ctx_rank * span_len, span_len, 1), HEAD // 2
    )
    shards = (
        query_key_value_weight[0],
        output_weight[0],
        gate_weight[0],
        up_weight[0],
        down_weight[0],
        jnp.stack([norm1_gain[0], norm1_bias[0], norm2_gain[0], norm2_bias[0]]),
    )
    gathered = (
        lax.all_gather(shards[0], "dp", axis=0, tiled=True),
        lax.all_gather(shards[1], "dp", axis=0, tiled=True),
        lax.all_gather(shards[2], "dp", axis=0, tiled=True),
        lax.all_gather(shards[3], "dp", axis=0, tiled=True),
        lax.all_gather(shards[4], "dp", axis=0, tiled=True),
        lax.all_gather(shards[5], "dp", axis=1, tiled=True),
    )
    weights_full = gathered[:5] + (gathered[5].astype(jnp.float32),)

    def select(array, micro_idx):
        return lax.dynamic_slice_in_dim(array, micro_idx * per_micro, per_micro, 0)

    delay_fwd = jnp.where(leading, 0, 1)
    received = jnp.zeros((per_micro,) + tokens.shape[1:], jnp.bfloat16)
    outputs = []
    stored = []
    for tick_no in range(MICRO + 1):
        micro_idx = jnp.clip(tick_no - delay_fwd, 0, MICRO - 1)
        hidden_state = jnp.where(leading, select(tokens, micro_idx), received)
        output, kept = layer_forward(
            hidden_state,
            weights_full,
            select(seg_near, micro_idx),
            select(seg_ids, micro_idx),
            select(cosine_rows, micro_idx),
            select(sine_rows, micro_idx),
        )
        sent_rows = output.astype(jnp.bfloat16)
        outputs.append(sent_rows)
        stored.append(kept)
        if tick_no < MICRO:
            received = passed_along(sent_rows, "section", 1)
    gathered = (
        lax.all_gather(shards[0], "dp", axis=0, tiled=True),
        lax.all_gather(shards[1], "dp", axis=0, tiled=True),
        lax.all_gather(shards[2], "dp", axis=0, tiled=True),
        lax.all_gather(shards[3], "dp", axis=0, tiled=True),
        lax.all_gather(shards[4], "dp", axis=0, tiled=True),
        lax.all_gather(shards[5], "dp", axis=1, tiled=True),
    )
    weights_full = gathered[:5] + (gathered[5].astype(jnp.float32),)
    returned = jnp.zeros_like(received)
    totals = None
    input_parts = []
    for tick_no in range(MICRO + 1):
        micro_idx = jnp.clip(tick_no - 1 + delay_fwd, 0, MICRO - 1)
        active = jnp.where(leading, tick_no >= 1, tick_no < MICRO)
        incoming = jnp.where(
            leading, returned.astype(jnp.float32), select(cotangent, micro_idx).astype(jnp.float32)
        )
        incoming = jnp.where(active, incoming, 0.0)
        kept = jax.tree.map(
            lambda early, later: jnp.where(leading, early, later),
            stored[max(tick_no - 1, 0)],
            stored[min(tick_no + 1, MICRO)],
        )
        dhidden, grad_terms = layer_backward(
            incoming,
            kept,
            weights_full,
            select(seg_near, micro_idx),
            select(seg_ids, micro_idx),
            select(cosine_rows, micro_idx),
            select(sine_rows, micro_idx),
        )
        totals = (
            grad_terms
            if totals is None
            else tuple((early + later for early, later in zip(totals, grad_terms)))
        )
        input_parts.append(dhidden)
        if tick_no < MICRO:
            returned = passed_along(dhidden.astype(jnp.bfloat16), "section", -1)
    summed = (
        lax.psum_scatter(
            totals[0].astype(jnp.bfloat16), "dp", scatter_dimension=0, tiled=True
        ).astype(jnp.float32),
        lax.psum_scatter(
            totals[1].astype(jnp.bfloat16), "dp", scatter_dimension=0, tiled=True
        ).astype(jnp.float32),
        lax.psum_scatter(
            totals[2].astype(jnp.bfloat16), "dp", scatter_dimension=0, tiled=True
        ).astype(jnp.float32),
        lax.psum_scatter(
            totals[3].astype(jnp.bfloat16), "dp", scatter_dimension=0, tiled=True
        ).astype(jnp.float32),
        lax.psum_scatter(
            totals[4].astype(jnp.bfloat16), "dp", scatter_dimension=0, tiled=True
        ).astype(jnp.float32),
        lax.psum_scatter(
            totals[5].astype(jnp.bfloat16), "dp", scatter_dimension=1, tiled=True
        ).astype(jnp.float32),
    )
    summed = jax.tree.map(
        lambda part: part.astype(jnp.float32), lax.psum(for_sending(summed), "ctx")
    )
    last_rows = jnp.concatenate(
        [jnp.where(leading, outputs[micro_no], outputs[micro_no + 1]) for micro_no in range(MICRO)],
        axis=0,
    )
    input_grads = jnp.concatenate(
        [
            jnp.where(leading, input_parts[micro_no + 1], input_parts[micro_no])
            for micro_no in range(MICRO)
        ],
        axis=0,
    )
    norm_grads = summed[5]
    return (
        last_rows[None],
        input_grads[None],
        summed[0][None],
        summed[1][None],
        summed[2][None],
        summed[3][None],
        summed[4][None],
        norm_grads[0][None],
        norm_grads[1][None],
        norm_grads[2][None],
        norm_grads[3][None],
    )


NT = (((1,), (1,)), ((), ()))
TN = (((0,), (0,)), ((), ()))


def mm(left, right, dims=(((1,), (0,)), ((), ()))):
    return lax.dot_general(left, right, dims, preferred_element_type=jnp.float32)


def in_vmem():
    return pl.BlockSpec(memory_space=pltpu.VMEM)


def anywhere():
    return pl.BlockSpec(memory_space=pl.ANY)


def in_smem():
    return pl.BlockSpec(memory_space=pltpu.SMEM)


def kernel_call(
    body, out_shapes, in_specs, scratch, mbytes, cost, name, out_specs=None, grid=None, prefetch=False
):
    out_specs = [in_vmem()] * len(out_shapes) if out_specs is None else out_specs
    if prefetch:
        spec = {
            "grid_spec": pltpu.PrefetchScalarGridSpec(
                num_scalar_prefetch=1, grid=grid, in_specs=in_specs, out_specs=out_specs, scratch_shapes=scratch
            )
        }
    else:
        spec = {"in_specs": in_specs, "out_specs": out_specs, "scratch_shapes": scratch}
        if grid is not None:
            spec["grid"] = grid
    return pl.pallas_call(
        body,
        out_shape=out_shapes,
        **spec,
        compiler_params=pltpu.CompilerParams(vmem_limit_bytes=mbytes * 2**20),
        cost_estimate=pl.CostEstimate(flops=0, bytes_accessed=3 * 10**6 * cost, transcendentals=0),
        name=name,
    )


def shape_of(shape, dtype):
    return jax.ShapeDtypeStruct(shape, dtype)


def loads_of(place, pieces, first, width, scratch, sems, begin, blocks=1):
    dp_rank, core = place[0], place[1]
    count = pieces[0].shape[0]
    copies = []
    cuts = ((0, 0, 2, 0, 0, 0), (1, 0, 2, 1, 0, 0), (2, 0, 2, 2, 0, 0), (3, 0, 1, 3, 0, 0), (4, 0, 1, 3, 1, 0))
    cuts += ((5, 0, 2, 0, 0, 1), (6, 0, 2, 1, 0, 1), (6, 2, 2, 2, 0, 1), (7, 0, 2, 3, 0, 1))
    unit = count // 2
    for piece, source, size, flip, target, other in cuts:
        half = 1 - core if other else core
        for block in range(blocks):
            row = ((dp_rank ^ flip) * blocks + block) * count + target * unit
            copies.append(
                pltpu.make_async_copy(
                    pieces[piece].at[pl.ds(source * unit, size * unit), pl.ds(first + block * width, width)],
                    scratch.at[
                        pl.ds(pl.multiple_of(row, unit), size * unit),
                        pl.ds(pl.multiple_of(half * width, 128), width),
                    ],
                    sems.at[begin + len(copies)],
                )
            )
    return copies


def start_loads(*arguments):
    copies = loads_of(*arguments)
    start_all(copies)
    return copies


def start_all(copies):
    for copy in copies:
        copy.start()


def wait_all(copies):
    for copy in copies:
        copy.wait()


def turn(values, cosine, sine):
    lane = lax.broadcasted_iota(jnp.int32, values.shape, 1)
    swapped = jnp.where(
        lane % 64 < 32, pltpu.roll(values, 96, 1), pltpu.roll(values, 32, 1)
    )
    return values * cosine + swapped * sine


def project_rows(place, hidden, cosine, sine, pieces):
    rows, width = hidden.shape
    half = 3 * width // 2

    def body(place_ref, hidden_ref, cos_ref, sin_ref, *refs):
        parts, (q_ref, kv_ref, weight, sems) = refs[:8], refs[8:]
        wait_all(start_loads(place_ref, parts, 0, half, weight, sems, 0))
        for step in range(3 * width // 256):
            mixed = mm(hidden_ref[...], weight[:, step * 256 : step * 256 + 256])
            for pair in range(2):
                column = step * 256 + pair * 128
                part = mixed[:, pair * 128 : pair * 128 + 128]
                which, lane = column // width, column % width
                if which < 2:
                    part = turn(part, cos_ref[...], sin_ref[...])
                if which == 0:
                    q_ref[:, lane : lane + 128] = (
                        part.astype(jnp.bfloat16).astype(jnp.float32) * HEAD**-0.5
                    ).astype(jnp.bfloat16)
                else:
                    kv_ref[which - 1, :, lane : lane + 128] = part.astype(jnp.bfloat16)

    return kernel_call(
        body,
        [shape_of((rows, width), jnp.bfloat16), shape_of((2, rows, width), jnp.bfloat16)],
        [in_smem()] + [in_vmem()] * 3 + [anywhere()] * 8,
        [pltpu.VMEM((width, 3 * width), jnp.bfloat16), pltpu.SemaphoreType.DMA((10,))],
        60,
        3,
        "project_rows",
    )(place, hidden, cosine, sine, *pieces)


def attend_rows(queries, blocks, seg_column, seg_row):
    rows, width = queries.shape
    keys = 2 * rows

    def body(col_ref, row_ref, q_ref, b0, b1, out_ref, sum_ref, bias, sums):
        step = pl.program_id(0)

        @pl.when(step == 0)
        def _():
            bias[...] = jnp.where(col_ref[...] == row_ref[...], 0.0, NEG)
            sums[...] = jnp.zeros_like(sums)

        lane = lax.broadcasted_iota(jnp.int32, (rows, 128), 1)
        query = q_ref[...]
        key = jnp.concatenate([b[0] for b in (b0, b1)], axis=0)
        value = jnp.concatenate([b[1] for b in (b0, b1)], axis=0)
        results = []
        for head in range(2):
            own = (lane < 64) if head == 0 else (lane >= 64)
            scores = mm(jnp.where(own, query, jnp.zeros_like(query)), key, NT) + bias[...]
            top = jnp.max(scores, axis=1, keepdims=True)
            exponent = jnp.exp(scores - top)
            total = jnp.sum(exponent, axis=1, keepdims=True)
            results.append(mm(exponent.astype(jnp.bfloat16), value) / total)
            sums[...] = jnp.where(lane == 2 * step + head, top + jnp.log(total), sums[...])
        out_ref[...] = jnp.where(lane < 64, results[0], results[1]).astype(jnp.bfloat16)

        @pl.when(step == width // 128 - 1)
        def _():
            sum_ref[...] = sums[...].T

    block = pl.BlockSpec((2, rows, 128), lambda j: (0, 0, j))
    return kernel_call(
        body,
        [shape_of((rows, width), jnp.bfloat16), shape_of((128, rows), jnp.float32)],
        [
            pl.BlockSpec((rows, 1), lambda j: (0, 0)),
            pl.BlockSpec((1, keys), lambda j: (0, 0)),
            pl.BlockSpec((rows, 128), lambda j: (0, j)),
            block, block,
        ],
        [pltpu.VMEM((rows, keys), jnp.float32), pltpu.VMEM((rows, 128), jnp.float32)],
        60,
        8,
        "attend_rows",
        [pl.BlockSpec((rows, 128), lambda j: (0, j)), pl.BlockSpec((128, rows), lambda j: (0, 0))],
        (width // 128,),
    )(seg_column, seg_row, queries, *blocks)


def attend_rows_back(queries, blocks, seg_row, seg_column, attended, sums, incoming):
    rows, width = queries.shape
    keys = 2 * rows

    def body(row_ref, col_ref, sum_ref, q_ref, att_ref, in_ref, b0, b1, dq_ref, own_ref, core_ref, bias):
        step = pl.program_id(0)

        @pl.when(step == 0)
        def _():
            bias[...] = jnp.where(col_ref[...] == row_ref[...], 0.0, NEG)

        lane = lax.broadcasted_iota(jnp.int32, (rows, 128), 1)
        query, given = q_ref[...], in_ref[...]
        key = jnp.concatenate([b[0] for b in (b0, b1)], axis=0)
        value = jnp.concatenate([b[1] for b in (b0, b1)], axis=0)
        key_t = key.T
        inner = (given.astype(jnp.float32) * att_ref[...].astype(jnp.float32)).T
        dkeys, dvalues, dqueries = [], [], []
        for head in range(2):
            own = (lane < 64) if head == 0 else (lane >= 64)
            scores = mm(key, jnp.where(own, query, jnp.zeros_like(query)), NT) + bias[...]
            probs = jnp.exp(scores - sum_ref[pl.ds(2 * step + head, 1), :])
            dvalues.append(mm(probs.astype(jnp.bfloat16), given))
            dprobs = mm(value, jnp.where(own, given, jnp.zeros_like(given)), NT)
            inner_row = jnp.sum(inner[64 * head : 64 * head + 64], axis=0, keepdims=True)
            dscores = (probs * (dprobs - inner_row)).astype(jnp.bfloat16)
            dkeys.append(mm(dscores, query))
            dqueries.append(mm(key_t[64 * head : 64 * head + 64], dscores))
        dq_ref[...] = jnp.concatenate(dqueries, axis=0).T * HEAD**-0.5
        wide = lax.broadcasted_iota(jnp.int32, (keys, 128), 1) < 64
        for which, pair in enumerate((dkeys, dvalues)):
            both = jnp.where(wide, pair[0], pair[1]).astype(jnp.bfloat16)
            own_ref[which] = both[:rows]
            core_ref[which] = both[rows:]

    block = pl.BlockSpec((2, rows, 128), lambda j: (0, 0, j))
    columns = pl.BlockSpec((rows, 128), lambda j: (0, j))
    pair_shape = shape_of((2, rows, width), jnp.bfloat16)
    return kernel_call(
        body,
        [
            shape_of((rows, width), jnp.float32),
            pair_shape,
            pair_shape,
        ],
        [
            pl.BlockSpec((1, rows), lambda j: (0, 0)),
            pl.BlockSpec((keys, 1), lambda j: (0, 0)),
            pl.BlockSpec((128, rows), lambda j: (0, 0)),
            columns, columns, columns, block, block,
        ],
        [pltpu.VMEM((keys, rows), jnp.float32)],
        60,
        18,
        "attend_rows_back",
        [columns, block, block],
        (width // 128,),
    )(seg_row, seg_column, sums, queries, attended, incoming, *blocks)


def unit_of(resid):
    centred = resid - jnp.mean(resid, axis=1, keepdims=True)
    scaling = lax.rsqrt(jnp.mean(centred * centred, axis=1, keepdims=True) + EPS)
    return centred * scaling, scaling


def norm_rows_back(incoming, unit, scaling, gain):
    scaled = incoming * gain
    return scaling * (
        scaled
        - jnp.mean(scaled, axis=1, keepdims=True)
        - unit * jnp.mean(scaled * unit, axis=1, keepdims=True)
    )


FF_STEP = 768


def mlp_scratch(width, hidden_width):
    return [
        pltpu.VMEM((width, width), jnp.bfloat16),
        pltpu.VMEM((width, hidden_width), jnp.bfloat16),
        pltpu.VMEM((width, hidden_width), jnp.bfloat16),
        pltpu.VMEM((hidden_width, width), jnp.bfloat16),
        pltpu.VMEM((width, 256), jnp.bfloat16),
        pltpu.VMEM((128, width), jnp.float32),
        pltpu.SemaphoreType.DMA((80,)),
    ]


def mlp_loads(place_ref, parts, scratch, width, ff_half):
    w_out, w_gate, w_up, w_down, w_norm, _, sems = scratch
    return (
        loads_of(place_ref, parts[:8], 2 * width, 128, w_norm, sems, 70),
        loads_of(place_ref, parts[:8], 3 * width // 2, width // 2, w_out, sems, 0),
        loads_of(place_ref, parts[8:], 0, ff_half, w_gate, sems, 10),
        loads_of(place_ref, parts[8:], ff_half, ff_half, w_up, sems, 20),
        loads_of(place_ref, parts[8:], 2 * ff_half, width // 2, w_down, sems, 30, 4),
    )


MINE = 5


def mlp_blocks(ff):
    steps = ff // FF_STEP
    return steps, lambda j, place: (place[1] ^ (j // (steps // 2))) * (steps // 2) + j % (steps // 2)


def mlp_rows(place, hidden, attended, first_parts, rest_parts, keep_all):
    rows, width = hidden.shape
    ff_half = (rest_parts[0].shape[1] - 2 * width) // 2
    ff = 2 * ff_half
    steps, block_of = mlp_blocks(ff)

    def body(place_ref, hidden_ref, att_ref, *refs):
        parts, rest = refs[:16], refs[16:]
        if keep_all:
            (out_ref, one_ref, two_ref, normed_ref, mid_ref, gate_ref, up_ref), rest = rest[:7], rest[7:]
        else:
            out_ref, rest, (two_ref, normed_ref) = rest[0], rest[1:-2], rest[-2:]
        w_out, w_gate, w_up, w_down, w_norm, norm_ref, _ = rest
        step = pl.program_id(0)
        norm, out, gates, ups, downs = mlp_loads(place_ref, parts, rest, width, ff_half)

        @pl.when(step == 0)
        def _():
            for copies in (norm, out, gates[:MINE], ups[:MINE], downs, gates[MINE:], ups[MINE:]):
                start_all(copies)
            wait_all(norm)
            norm_ref[...] = w_norm[:, :128].astype(jnp.float32).T
            wait_all(out)
            resid = hidden_ref[...].astype(jnp.float32) + mm(att_ref[...], w_out[...])
            if keep_all:
                one_ref[...] = resid
            normed = unit_of(resid)[0] * norm_ref[0:1] + norm_ref[1:2]
            normed_ref[...] = normed.astype(jnp.bfloat16)
            two_ref[...] = normed
            wait_all(gates[:MINE])
            wait_all(ups[:MINE])

        @pl.when(step == steps // 2)
        def _():
            wait_all(gates[MINE:])
            wait_all(ups[MINE:])

        span = pl.ds(pl.multiple_of(block_of(step, place_ref) * FF_STEP, FF_STEP), FF_STEP)
        gate = mm(normed_ref[...], w_gate[:, span])
        up = mm(normed_ref[...], w_up[:, span])
        middle = (gate * jax.nn.sigmoid(gate) * up).astype(jnp.bfloat16)
        if keep_all:
            gate_ref[...], up_ref[...], mid_ref[...] = gate.astype(jnp.bfloat16), up.astype(jnp.bfloat16), middle

        @pl.when(step == 0)
        def _():
            wait_all(downs)

        two_ref[...] += mm(middle, w_down[span, :])

        @pl.when(step == steps - 1)
        def _():
            out_ref[...] = (unit_of(two_ref[...])[0] * norm_ref[2:3] + norm_ref[3:4]).astype(jnp.bfloat16)

    whole = pl.BlockSpec((rows, width), lambda j, place: (0, 0))
    part = pl.BlockSpec((rows, FF_STEP), lambda j, place: (0, block_of(j, place)))
    shapes, scratch = [shape_of((rows, width), jnp.bfloat16)], mlp_scratch(width, ff)
    if keep_all:
        shapes += [shape_of((rows, width), jnp.float32)] * 2 + [shape_of((rows, width), jnp.bfloat16)]
        shapes += [shape_of((rows, ff), jnp.bfloat16)] * 3
    else:
        scratch += [pltpu.VMEM((rows, width), jnp.float32), pltpu.VMEM((rows, width), jnp.bfloat16)]
    return kernel_call(
        body,
        shapes,
        [whole, whole] + [anywhere()] * 16,
        scratch,
        60,
        16,
        "mlp_rows",
        [whole] * 4 + [part] * 3 if keep_all else [whole],
        (steps,),
        True,
    )(place, hidden, attended, *first_parts, *rest_parts)


def mlp_rows_back(place, incoming, one, two, gate, up, first_parts, rest_parts, for_weights):
    rows, width = incoming.shape
    ff_half = (rest_parts[0].shape[1] - 2 * width) // 2
    ff = 2 * ff_half
    steps, block_of = mlp_blocks(ff)
    extra = 6 if for_weights else 0

    def body(place_ref, in_ref, one_ref, two_ref, gate_ref, up_ref, *refs):
        parts, outs, rest = refs[:16], refs[16 : 18 + extra], refs[18 + extra :]
        dresid_ref, datt_ref = outs[:2]
        w_out, w_gate, w_up, w_down, w_norm, norm_ref, _, low_ref, sums_ref = rest
        step = pl.program_id(0)
        norm, out, gates, ups, downs = mlp_loads(place_ref, parts, rest[:7], width, ff_half)

        def share(column):
            half = width // 2
            low, first = low_ref[...], place_ref[1] == 0
            for ref, mine in ((outs[2], True), (outs[3], False)):
                ref[:rows, column : column + half] = jnp.where(
                    first == mine, low[:, :half], low[:, half:]
                )

        @pl.when(step == 0)
        def _():
            for copies in (norm, downs, gates[:MINE], ups[:MINE], gates[MINE:], ups[MINE:], out):
                start_all(copies)
            wait_all(norm)
            norm_ref[...] = w_norm[:, :128].astype(jnp.float32).T
            given = in_ref[...].astype(jnp.float32)
            unit, scaling = unit_of(two_ref[...])
            dresid_two = norm_rows_back(given, unit, scaling, norm_ref[2:3])
            dresid_ref[...] = dresid_two
            low_ref[...] = dresid_two.astype(jnp.bfloat16)
            if for_weights:
                sums_ref[...] = jnp.zeros_like(sums_ref)
                sums_ref[2:3] = jnp.sum(given * unit, axis=0, keepdims=True)
                sums_ref[3:4] = jnp.sum(given, axis=0, keepdims=True)
                share(0)
            wait_all(downs)
            wait_all(gates[:MINE])
            wait_all(ups[:MINE])

        @pl.when(step == steps // 2)
        def _():
            wait_all(gates[MINE:])
            wait_all(ups[MINE:])

        span = pl.ds(pl.multiple_of(block_of(step, place_ref) * FF_STEP, FF_STEP), FF_STEP)
        dmiddle = mm(low_ref[...], w_down[span, :], NT)
        gate_block = gate_ref[...].astype(jnp.float32)
        sig = jax.nn.sigmoid(gate_block)
        swish = gate_block * sig
        dup = (dmiddle * swish).astype(jnp.bfloat16)
        dgate = (dmiddle * up_ref[...].astype(jnp.float32) * (sig + swish * (1.0 - sig))).astype(jnp.bfloat16)
        if for_weights:
            @pl.when(step < steps // 2)
            def _():
                outs[4][...], outs[5][...] = dgate, dup

            @pl.when(step >= steps // 2)
            def _():
                outs[6][...], outs[7][...] = dgate, dup

        dresid_ref[...] += mm(dgate, w_gate[:, span], NT) + mm(dup, w_up[:, span], NT)

        @pl.when(step == steps - 1)
        def _():
            wait_all(out)
            dnormed = dresid_ref[...]
            unit, scaling = unit_of(one_ref[...])
            dresid_one = norm_rows_back(dnormed, unit, scaling, norm_ref[0:1])
            dresid_ref[...] = dresid_one
            low_ref[...] = dresid_one.astype(jnp.bfloat16)
            if for_weights:
                sums_ref[0:1] = jnp.sum(dnormed * unit, axis=0, keepdims=True)
                sums_ref[1:2] = jnp.sum(dnormed, axis=0, keepdims=True)
                share(width // 2)
                for ref in outs[2:4]:
                    ref[rows:] = sums_ref[...].astype(jnp.bfloat16)
            datt_ref[...] = mm(low_ref[...], w_out[...], NT).astype(jnp.bfloat16)

    half_steps = steps // 2
    whole = pl.BlockSpec((rows, width), lambda j, place: (0, 0))
    longer = pl.BlockSpec((rows + 16, width), lambda j, place: (0, 0))
    part = pl.BlockSpec((rows, FF_STEP), lambda j, place: (0, block_of(j, place)))
    mine = pl.BlockSpec((rows, FF_STEP), lambda j, place: (0, jnp.minimum(j, half_steps - 1)))
    theirs = pl.BlockSpec((rows, FF_STEP), lambda j, place: (0, jnp.maximum(j - half_steps, 0)))
    shapes = [shape_of((rows, width), jnp.float32), shape_of((rows, width), jnp.bfloat16)]
    specs = [whole, whole]
    if for_weights:
        shapes += [shape_of((rows + 16, width), jnp.bfloat16)] * 2 + [shape_of((rows, ff_half), jnp.bfloat16)] * 4
        specs += [longer] * 2 + [mine] * 2 + [theirs] * 2
    return kernel_call(
        body,
        shapes,
        [whole, whole, whole, part, part] + [anywhere()] * 16,
        mlp_scratch(width, ff) + [pltpu.VMEM((rows, width), jnp.bfloat16), pltpu.VMEM((16, width), jnp.float32)],
        60,
        21,
        "mlp_rows_back",
        specs,
        (steps,),
        True,
    )(place, incoming, one, two, gate, up, *first_parts, *rest_parts)


def project_rows_back(place, dqueries, sums, dresid_one, cosine, sine, pieces):
    rows, width = dqueries.shape
    half = 3 * width // 2
    count = len(sums)

    def body(place_ref, dq_ref, resid_ref, cos_ref, sin_ref, *refs):
        parts, rest = refs[:8], refs[8:]
        sum_refs, (keep_ref, send_ref, dhidden_ref, weight, sems, dmixed_ref) = rest[:count], rest[count:]
        core = place_ref[1]
        loads = start_loads(place_ref, parts, 0, half, weight, sems, 0)
        for column in range(0, 3 * width, 128):
            which, lane = column // width, column % width
            span = slice(lane, lane + 128)
            if which == 0:
                part = dq_ref[:, span]
            else:
                part = sum(ref[which - 1, :, span].astype(jnp.float32) for ref in sum_refs)
            if which < 2:
                part = turn(part, cos_ref[...], -sin_ref[...])
            dmixed_ref[:, column : column + 128] = part.astype(jnp.bfloat16)
        for index in range(2):
            @pl.when(core == index)
            def _():
                keep_ref[...] = dmixed_ref[:, index * half : (index + 1) * half]
                send_ref[...] = dmixed_ref[:, (1 - index) * half : (2 - index) * half]

        wait_all(loads)
        dhidden_ref[...] = resid_ref[...] + mm(dmixed_ref[...], weight[...], NT)

    return kernel_call(
        body,
        [
            shape_of((rows, half), jnp.bfloat16),
            shape_of((rows, half), jnp.bfloat16),
            shape_of((rows, width), jnp.float32),
        ],
        [in_smem()] + [in_vmem()] * 4 + [anywhere()] * 8 + [in_vmem()] * count,
        [
            pltpu.VMEM((width, 3 * width), jnp.bfloat16),
            pltpu.SemaphoreType.DMA((10,)),
            pltpu.VMEM((rows, 3 * width), jnp.bfloat16),
        ],
        60,
        6,
        "project_rows_back",
    )(place, dqueries, dresid_one, cosine, sine, *pieces, *sums)


def grad_parts(place, groups, sums=None):
    jobs = [job for group in groups for job in group]
    rows = jobs[0][0][0].shape[0]
    lefts, rights, arrays = [], [], []
    for left, left_span, right, right_span, blocks in jobs:
        for known, entry in ((lefts, (left, left_span)), (rights, (right, right_span))):
            if not any(entry[0] is other[0] and entry[1] == other[1] for other in known):
                known.append(entry)
        for array in (*left, *right):
            if not any(array is other for other in arrays):
                arrays.append(array)
    where = lambda array: next(i for i, other in enumerate(arrays) if other is array)
    slot = lambda known, pair, span: next(
        i for i, other in enumerate(known) if other[0] is pair and other[1] == span
    )
    count = (jobs[0][1][1] - jobs[0][1][0]) // 4 // jobs[0][4]
    totals = [sum((job[3][1] - job[3][0]) * job[4] for job in group) for group in groups]
    widths = list(totals)
    if sums is not None:
        widths[0] += 128

    def body(place_ref, *refs):
        inputs, refs = refs[: len(arrays)], refs[len(arrays) :]
        outs, refs = refs[: 5 * len(groups)], refs[5 * len(groups) :]
        block, left_refs, right_refs = refs[0], refs[1 : 1 + len(lefts)], refs[1 + len(lefts) :]
        for ref, (pair, span) in zip(left_refs, lefts):
            for core in range(2):
                ref[:, core * rows : (core + 1) * rows] = inputs[where(pair[core])][:rows, span[0] : span[1]].T
        for ref, (pair, span) in zip(right_refs, rights):
            for core in range(2):
                ref[core * rows : (core + 1) * rows] = inputs[where(pair[core])][:rows, span[0] : span[1]]
        if sums is not None:
            padded, turned = refs[-2:]
            padded[...] = jnp.zeros_like(padded)
            padded[:16] = sum(
                inputs[where(array)][rows:, : 4 * count].astype(jnp.float32) for array in jobs[sums][2]
            )
            turned[...] = padded[...].T
        upper, lower = slice(0, count // 2), slice(count // 2, count)
        for index, group in enumerate(groups):
            own_ref, x_ref, y_ref, xl_ref, yu_ref = outs[5 * index : 5 * index + 5]
            end = widths[index]
            for flip in range(4):
                target = 0
                for left, left_span, right, right_span, blocks in group:
                    left_t, right_all = left_refs[slot(lefts, left, left_span)], right_refs[slot(rights, right, right_span)]
                    width = right_span[1] - right_span[0]
                    tile = 512 if width % 512 == 0 else 384
                    for part in range(blocks):
                        begin = ((place_ref[0] ^ flip) * blocks + part) * count
                        rows_t = left_t[pl.ds(pl.multiple_of(begin, count), count), :]
                        for column in range(0, width, tile):
                            block[:, target : target + tile] = mm(
                                rows_t, right_all[:, column : column + tile]
                            ).astype(jnp.bfloat16)
                            target += tile
                if target < end:
                    begin = pl.multiple_of((place_ref[0] ^ flip) * count, count)
                    block[:, target:end] = turned[pl.ds(begin, count), :].astype(jnp.bfloat16)
                if flip == 0:
                    own_ref[...] = block[:, :end]
                elif flip == 1:
                    x_ref[upper] = block[upper, :end]
                    xl_ref[...] = block[lower, :end]
                elif flip == 2:
                    y_ref[upper] = block[lower, :end]
                    yu_ref[...] = block[upper, :end]
                else:
                    x_ref[lower] = block[upper, :end]
                    y_ref[lower] = block[lower, :end]

    scratch = [pltpu.VMEM((count, max(widths)), jnp.bfloat16)]
    scratch += [pltpu.VMEM((span[1] - span[0], 2 * rows), jnp.bfloat16) for _, span in lefts]
    scratch += [pltpu.VMEM((2 * rows, span[1] - span[0]), jnp.bfloat16) for _, span in rights]
    if sums is not None:
        scratch += [pltpu.VMEM((128, 4 * count), jnp.float32), pltpu.VMEM((4 * count, 128), jnp.float32)]
    shapes = []
    for width in widths:
        shapes += [shape_of((count, width), jnp.bfloat16)] * 3 + [shape_of((count // 2, width), jnp.bfloat16)] * 2
    made = kernel_call(
        body, shapes, [in_smem()] + [in_vmem()] * len(arrays), scratch, 60, 7, "grad_parts"
    )(place, *arrays)
    return [made[5 * index : 5 * index + 5] for index in range(len(groups))]


def first_columns(values):
    rows = values.shape[0]

    def body(values_ref, *refs):
        turned = values_ref[...].astype(jnp.float32).T
        for index, ref in enumerate(refs):
            ref[...] = turned[index : index + 1]

    return kernel_call(
        body, [shape_of((1, rows), jnp.float32)] * 4, [in_vmem()], [], 16, 1, "first_columns"
    )(values)


def to_core(value):
    return lax.ppermute(value, "section", [(0, 1), (1, 0)])


def along_x(value):
    return lax.ppermute(value, "dp", [(i, i ^ 1) for i in range(4)])


def along_y(value):
    return lax.ppermute(value, "dp", [(i, i ^ 2) for i in range(4)])


def along_z(value):
    return lax.ppermute(value, "ctx", [(i, i ^ 1) for i in range(4)])


def near_blocks(value):
    pairs = [(i, i ^ 1) for i in range(4)] + [(4 + i, 4 + (i ^ 2)) for i in range(4)]
    return lax.ppermute(value, ("section", "ctx"), pairs)


def far_blocks(value):
    return lax.ppermute(value, ("section", "ctx"), [(4 + i, 4 + (i ^ 3)) for i in range(4)])


def same_role(value):
    return lax.ppermute(value, "ctx", [(i, i ^ 3) for i in range(4)])


def lowered(value):
    return value.astype(jnp.bfloat16)


def wide(value):
    return value.astype(jnp.float32)


def by_core(core, mine, theirs, axis):
    return jnp.where(
        core == 0,
        jnp.concatenate([mine, theirs], axis=axis),
        jnp.concatenate([theirs, mine], axis=axis),
    )


def half_of(array, which):
    width = array.shape[-1] // 2
    return lax.dynamic_slice_in_dim(array, which * width, width, array.ndim - 1)


def after(value, *others):
    return lax.optimization_barrier((value, *others))[0]


def gather_near(piece, *others):
    own = after(piece, *others)
    return [own, along_x(own), along_y(own)]


def gather_far(near, *others):
    rows = near[0].shape[0] // 2
    return [along_x(after(near[2][:rows], *others)), along_y(after(near[1][rows:], *others))]


def both_cores(near, far, other):
    return [
        *near,
        *far,
        other,
        to_core(jnp.concatenate(near[1:3], axis=0)),
        to_core(jnp.concatenate(far, axis=0)),
    ]


def reduce_first(parts, *others):
    return along_x(after(parts[1], *others)), along_y(after(parts[2], *others))


def reduce_second(parts, first, *others):
    _, _, _, x_lower, y_upper = after(tuple(parts), *others)
    from_x, from_y = first
    rows = x_lower.shape[0]
    return (
        along_x(lowered(wide(x_lower) + wide(from_y[rows:]))),
        along_y(lowered(wide(y_upper) + wide(from_x[rows:]))),
    )


def reduce_last(parts, first, second):
    from_x, from_y = first
    rows = second[0].shape[0]
    return lowered(
        wide(parts[0])
        + jnp.concatenate(
            [wide(from_x[:rows]) + wide(second[1]), wide(from_y[:rows]) + wide(second[0])], axis=0
        )
    )


def reduce_ctx(pieces, middle, last):
    received = [same_role(pieces[0]), same_role(pieces[1])]
    mine, others = [], []
    for index, piece in enumerate(pieces):
        mine.append(lowered(wide(piece) + wide(after(received[index], *last))))
        last = (mine[index],)
        others.append(along_z(mine[index]))
        if index + 2 < len(pieces):
            received.append(same_role(after(pieces[index + 2], received[index])))
    sums = [(jnp.where(middle, theirs, own), jnp.where(middle, own, theirs)) for own, theirs in zip(mine, others)]
    return sums, mine[-2]


def paired_on_device(
    tokens,
    seg_ids,
    query_key_value_weight,
    output_weight,
    gate_weight,
    up_weight,
    down_weight,
    norm1_gain,
    norm1_bias,
    norm2_gain,
    norm2_bias,
    cotangent,
):
    core, ctx_rank, dp_rank = (lax.axis_index(a) for a in ("section", "ctx", "dp"))
    span, width = tokens.shape[1], tokens.shape[2]
    sequence = ctx_rank // 2
    middle = (ctx_rank == 1) | (ctx_rank == 2)
    role = jnp.where(middle, 1, 0)
    even = ctx_rank % 2 == 0
    place = jnp.stack([dp_rank, core]).astype(jnp.int32)
    pick = lambda array, index: lax.dynamic_index_in_dim(array, index, 0, keepdims=False)

    def in_order(left, right):
        return jnp.where(even, jnp.concatenate([left, right]), jnp.concatenate([right, left]))

    def to_rows(tokens, cotangent, others):
        mine, theirs = jnp.where(middle, cotangent, tokens), jnp.where(middle, tokens, cotangent)
        first = near_blocks(jnp.where(core == 0, pick(theirs, sequence), pick(theirs, 1 - sequence)))
        second = far_blocks(pick(mine, 1 - sequence))
        first, second = after((first, second), *others)
        return in_order(
            jnp.where(core == 0, pick(mine, sequence), first), jnp.where(core == 0, first, second)
        )

    def send_rows(rows):
        halves = rows.reshape(2, span, width)
        left, right = pick(halves, jnp.where(even, 0, 1)), pick(halves, jnp.where(even, 1, 0))
        return left, near_blocks(jnp.where(core == 0, right, left)), far_blocks(right)

    def placed_rows(left, first, second):
        same = jnp.where(core == 0, left, second)
        first_layer, second_layer = jnp.where(middle, first, same), jnp.where(middle, same, first)
        other = to_core(jnp.where(core == 0, second_layer, first_layer))
        mine = jnp.where(core == 0, first_layer, second_layer)
        return jnp.where(
            sequence == core, jnp.stack([mine, other]), jnp.stack([other, mine])
        )[None]

    norm_columns = jnp.concatenate([norm1_gain, norm1_bias, norm2_gain, norm2_bias], axis=0).T
    norm_columns = jnp.pad(norm_columns, ((0, 0), (0, 124)))

    def first_pack(which):
        return jnp.concatenate(
            [half_of(query_key_value_weight[0], which), half_of(output_weight[0], which), norm_columns], axis=1
        )

    def rest_pack(which, *others):
        gate, up, down = after((gate_weight[0], up_weight[0], down_weight[0]), *others)
        return jnp.concatenate(
            [half_of(gate, which), half_of(up, which)]
            + jnp.split(half_of(down, which), down.shape[0] // gate.shape[0]),
            axis=1,
        )

    def halves(own, other, other_sent):
        return jnp.where(core == role, own, other_sent), lambda near: jnp.where(
            core == role, other, to_core(after(own, *near[1:3]))
        )

    own, other = first_pack(core), first_pack(1 - core)
    other_sent = to_core(other)
    first_piece, first_other = halves(own, other, other_sent)
    near = gather_near(first_piece)
    far = gather_far(near)
    own, other = rest_pack(core, other_sent), rest_pack(1 - core, other_sent)
    rest_piece, rest_other = halves(own, other, to_core(other))
    near_mlp = gather_near(rest_piece, *near[1:3])
    given = to_rows(*after((tokens, cotangent), first_piece), far)

    seg = pick(seg_ids, sequence)
    rows = 2 * span
    begin = (sequence ^ core) * rows
    seg_rows = lax.dynamic_slice_in_dim(seg, begin, rows, 0)
    seg_keys = jnp.concatenate([seg_rows, lax.dynamic_slice_in_dim(seg, rows - begin, rows, 0)])
    begins = jnp.sum((seg[None, :] < seg_rows[:, None]).astype(jnp.int32), axis=1)
    places = begin + jnp.arange(rows, dtype=jnp.int32) - begins
    lanes = jnp.arange(128, dtype=jnp.int32) % HEAD
    half = HEAD // 2
    spread = 1000.0 ** (-2.0 * (lanes % half).astype(jnp.float32) / HEAD)
    angles = places.astype(jnp.float32)[:, None] * spread[None, :]
    cosine, sine = jnp.cos(angles), jnp.where(lanes < half, -1.0, 1.0) * jnp.sin(angles)

    def attention(hidden):
        queries, own = project_rows(place, hidden, cosine, sine, first)
        blocks = [own, to_core(own)]
        return queries, blocks, *attend_rows(queries, blocks, seg_rows[:, None], seg_keys[None, :])

    first = both_cores(near, far, first_other(near))
    queries, blocks, attended, sums = attention(given)
    near_mlp = [after(part, attended) for part in near_mlp]
    rest = both_cores(near_mlp, gather_far(near_mlp), rest_other(near_mlp))
    output = mlp_rows(place, given, attended, first, rest, False)[0]

    hidden = jnp.where(middle, along_z(output), given)
    queries, blocks, attended, sums = attention(hidden)
    output, one, two, normed, mids, gate, up = mlp_rows(place, hidden, attended, first, rest, True)

    dresid_one, dattended = mlp_rows_back(place, given, one, two, gate, up, first, rest, False)
    sent_outputs = send_rows(output)
    dqueries, own, across = attend_rows_back(
        queries, blocks, seg_rows[None, :], seg_keys[:, None], attended, sums, after(dattended, *sent_outputs)
    )
    dhidden = project_rows_back(
        place, dqueries, (own, to_core(across)), dresid_one, cosine, sine, first
    )[2]
    incoming = jnp.where(middle, given, along_z(lowered(dhidden)))

    both = lambda value: (value, to_core(value))
    mids, normed, attended, hidden = both(mids), both(normed), both(attended), both(hidden)
    incoming = after(incoming, mids[1], normed[1], attended[1], hidden[1])
    dresid_one, dattended, keep, send, keep_gate, keep_up, send_gate, send_up = mlp_rows_back(
        place, incoming, one, two, gate, up, first, rest, True
    )
    ff = mids[0].shape[1]
    right, right_gate, right_up = (keep, to_core(send)), (keep_gate, to_core(send_gate)), (keep_up, to_core(send_up))
    parts = grad_parts(place, [[(normed, (0, width), right_gate, (0, ff // 2), 1)]])
    near = [reduce_first(parts[0])]
    normed = (after(normed[0], *parts[0]), normed[1])
    parts += grad_parts(place, [[(normed, (0, width), right_up, (0, ff // 2), 1)]])
    near.append(reduce_first(parts[1]))
    dqueries, own, across = attend_rows_back(
        queries, blocks, seg_rows[None, :], seg_keys[:, None], attended[0], sums, after(dattended, *parts[1])
    )
    across = to_core(after(across, *near[0], *near[1]))
    far = [reduce_second(parts[0], near[0], dqueries), reduce_second(parts[1], near[1], dqueries)]
    mids = (after(mids[0], dqueries), mids[1])
    parts += grad_parts(
        place,
        [
            [
                (mids, (0, ff), right, (0, width // 2), ff // width),
                (attended, (0, width), right, (width // 2, width), 1),
            ]
        ],
        1,
    )
    keep, send, dhidden = project_rows_back(
        place, dqueries, (own, across), after(dresid_one, *parts[2], *far[0], *far[1]), cosine, sine, first
    )
    near.append(reduce_first(parts[2], *far[0], *far[1]))
    parts += grad_parts(place, [[(hidden, (0, width), (keep, to_core(send)), (0, 3 * width // 2), 1)]])
    near.append(reduce_first(parts[3]))
    far.append(reduce_second(parts[2], near[2], *parts[3]))
    far.append(reduce_second(parts[3], near[3]))
    pieces = [reduce_last(*group) for group in zip(parts, near, far)]
    totals, nearly = reduce_ctx(pieces, middle, parts[3])
    sent_grads = send_rows(after(lowered(dhidden), nearly))

    pairs = []
    for first_layer, second_layer in totals:
        pairs.append(
            (
                jnp.where(core == 0, first_layer, second_layer),
                to_core(jnp.where(core == 0, second_layer, first_layer)),
            )
        )
    joined = lambda index, begin, end: wide(
        by_core(core, pairs[index][0][:, begin:end], pairs[index][1][:, begin:end], 1)
    )[None]
    norm_grads = first_columns(pairs[2][0][:, 5 * width // 2 :])
    pick_down = lambda which: jnp.concatenate(
        [pairs[2][which][:, i * width // 2 : (i + 1) * width // 2] for i in range(ff // width)]
    )
    grad_down = wide(by_core(core, pick_down(0), pick_down(1), 1))[None]

    return (
        placed_rows(*after(sent_outputs, *far[3])),
        wide(placed_rows(*sent_grads)),
        joined(3, 0, 3 * width // 2),
        joined(2, 2 * width, 5 * width // 2),
        joined(0, 0, ff // 2),
        joined(1, 0, ff // 2),
        grad_down,
        *norm_grads,
    )


def solution(mesh):
    placed = (
        P("dp", "ctx", None),
        P("dp", None),
        P("section", "dp", None),
        P("section", "dp", None),
        P("section", "dp", None),
        P("section", "dp", None),
        P("section", "dp", None),
        P("section", "dp"),
        P("section", "dp"),
        P("section", "dp"),
        P("section", "dp"),
        P("dp", "ctx", None),
    )
    paired = mesh.shape["section"] == 2 and mesh.shape["ctx"] == 4 and mesh.shape["dp"] == 4
    return jax.shard_map(
        paired_on_device if paired else relay_on_device,
        mesh=mesh,
        in_specs=placed,
        out_specs=(
            P("section", "dp", "ctx", None),
            P("section", "dp", "ctx", None),
            P("section", "dp", None),
            P("section", "dp", None),
            P("section", "dp", None),
            P("section", "dp", None),
            P("section", "dp", None),
            P("section", "dp"),
            P("section", "dp"),
            P("section", "dp"),
            P("section", "dp"),
        ),
        check_vma=False,
    )
```

```python
import jax
import jax.numpy as jnp
from jax import lax
from jax.experimental import pallas as pl
from jax.experimental.pallas import tpu as pltpu
from jax.sharding import PartitionSpec as P

HEAD = 64
MICRO = 2


EPS = 1e-05
NEG = -1e30


def passed_along(value, axis, steps):
    count = lax.axis_size(axis)
    first, last = (max(0, -steps), min(count, count - steps))
    return lax.ppermute(value, axis, [(source, source + steps) for source in range(first, last)])


def for_sending(array):
    return jax.tree.map(lambda a: a.astype(jnp.bfloat16) if a.dtype == jnp.float32 else a, array)


def positions(seg_ids):
    places = lax.broadcasted_iota(jnp.int32, seg_ids.shape, 1)
    begins = jnp.concatenate(
        [jnp.ones_like(seg_ids[:, :1]), (seg_ids[:, 1:] != seg_ids[:, :-1]).astype(jnp.int32)],
        axis=1,
    )
    return places - lax.cummax(places * begins, axis=1)


def rope_tables(places, half_dim):
    spread = 1000.0 ** (-2.0 * jnp.arange(half_dim, dtype=jnp.float32) / (2 * half_dim))
    angles = places.astype(jnp.float32)[..., None] * spread
    return (jnp.cos(angles), jnp.sin(angles))


def rotate(values, cosine, sine_table):
    half_dim = values.shape[-1] // 2
    former, latter = (values[..., :half_dim], values[..., half_dim:])
    cosine, sine_table = (cosine[..., None, :], sine_table[..., None, :])
    return jnp.concatenate(
        [former * cosine - latter * sine_table, latter * cosine + former * sine_table], axis=-1
    )


def unrotate(values, cosine, sine_table):
    half_dim = values.shape[-1] // 2
    former, latter = (values[..., :half_dim], values[..., half_dim:])
    cosine, sine_table = (cosine[..., None, :], sine_table[..., None, :])
    return jnp.concatenate(
        [former * cosine + latter * sine_table, latter * cosine - former * sine_table], axis=-1
    )


def norm_parts(resid, gain, bias):
    centred = resid - jnp.mean(resid, axis=-1, keepdims=True)
    scaling = lax.rsqrt(jnp.mean(centred * centred, axis=-1, keepdims=True) + EPS)
    unit_rows = centred * scaling
    return (unit_rows * gain + bias, unit_rows, scaling)


def norm_back(incoming, unit_rows, scaling, gain):
    scaled = incoming * gain
    inner = (
        scaled
        - jnp.mean(scaled, axis=-1, keepdims=True)
        - unit_rows * jnp.mean(scaled * unit_rows, axis=-1, keepdims=True)
    )
    return (
        scaling * inner,
        jnp.sum(incoming * unit_rows, axis=(0, 1)),
        jnp.sum(incoming, axis=(0, 1)),
    )


def masked_scores(queries, all_keys, seg_rows, seg_keys):
    row_count, model_width = queries.shape
    head_count = model_width // HEAD
    scores = jnp.einsum(
        "qhd,khd->hqk",
        queries.reshape(row_count, head_count, HEAD),
        all_keys.reshape(all_keys.shape[0], head_count, HEAD),
        preferred_element_type=jnp.float32,
    ) * HEAD ** (-0.5)
    return jnp.where((seg_rows[:, None] == seg_keys[None, :])[None], scores, NEG)


def attend(operands):
    queries, all_keys, all_values, seg_rows, seg_keys = operands
    row_count, model_width = queries.shape
    head_count = model_width // HEAD
    scores = masked_scores(queries, all_keys, seg_rows, seg_keys)
    row_max = jnp.max(scores, axis=-1, keepdims=True)
    exponent = jnp.exp(scores - row_max)
    row_sum = jnp.sum(exponent, axis=-1, keepdims=True)
    probs_low = (exponent / row_sum).astype(jnp.bfloat16)
    result = jnp.einsum(
        "hqk,khd->qhd",
        probs_low,
        all_values.reshape(all_values.shape[0], head_count, HEAD),
        preferred_element_type=jnp.float32,
    )
    return (result.reshape(row_count, model_width), (row_max + jnp.log(row_sum))[..., 0])


def attend_back(operands):
    queries, all_keys, all_values, seg_rows, seg_keys, log_sum, incoming = operands
    row_count, model_width = queries.shape
    head_count = model_width // HEAD
    key_count = all_keys.shape[0]
    probs = jnp.exp(masked_scores(queries, all_keys, seg_rows, seg_keys) - log_sum[..., None])
    heads_in = incoming.reshape(row_count, head_count, HEAD)
    dprobs = jnp.einsum(
        "qhd,khd->hqk",
        heads_in,
        all_values.reshape(key_count, head_count, HEAD),
        preferred_element_type=jnp.float32,
    )
    dscores = (probs * (dprobs - jnp.sum(probs * dprobs, axis=-1, keepdims=True))).astype(
        jnp.bfloat16
    )
    dquery = jnp.einsum(
        "hqk,khd->qhd",
        dscores,
        all_keys.reshape(key_count, head_count, HEAD),
        preferred_element_type=jnp.float32,
    ) * HEAD ** (-0.5)
    dkeys_part = jnp.einsum(
        "hqk,qhd->khd",
        dscores,
        queries.reshape(row_count, head_count, HEAD),
        preferred_element_type=jnp.float32,
    ) * HEAD ** (-0.5)
    dvalue = jnp.einsum(
        "hqk,qhd->khd", probs.astype(jnp.bfloat16), heads_in, preferred_element_type=jnp.float32
    )
    return (
        dquery.reshape(row_count, model_width),
        dkeys_part.reshape(key_count, model_width),
        dvalue.reshape(key_count, model_width),
    )


def layer_forward(hidden_state, weights_full, seg_rows, seg_keys, cosine, sine_table):
    query_key_value_weight, output_weight, gate_weight, up_weight, down_weight, norm_params = (
        weights_full
    )
    model_width = hidden_state.shape[-1]
    shaped = hidden_state.shape[:2] + (model_width // HEAD, HEAD)
    mixed_query_key_value = jnp.einsum(
        "bld,de->ble", hidden_state, query_key_value_weight, preferred_element_type=jnp.float32
    )
    queries = (
        rotate(mixed_query_key_value[..., :model_width].reshape(shaped), cosine, sine_table)
        .reshape(hidden_state.shape)
        .astype(jnp.bfloat16)
    )
    key_rows = (
        rotate(
            mixed_query_key_value[..., model_width : 2 * model_width].reshape(shaped),
            cosine,
            sine_table,
        )
        .reshape(hidden_state.shape)
        .astype(jnp.bfloat16)
    )
    value_rows = mixed_query_key_value[..., 2 * model_width :].astype(jnp.bfloat16)
    all_keys, all_values = (
        lax.all_gather(key_rows, "ctx", axis=1, tiled=True),
        lax.all_gather(value_rows, "ctx", axis=1, tiled=True),
    )
    attention_output, log_sum = lax.map(attend, (queries, all_keys, all_values, seg_rows, seg_keys))
    attention_output = attention_output.astype(jnp.bfloat16)
    residual_first = hidden_state.astype(jnp.float32) + jnp.einsum(
        "bld,de->ble", attention_output, output_weight, preferred_element_type=jnp.float32
    )
    normalized_rows, unit_one, scale_one = norm_parts(
        residual_first, norm_params[0], norm_params[1]
    )
    normalized_lowered = normalized_rows.astype(jnp.bfloat16)
    gate_projected = jnp.einsum(
        "bld,df->blf", normalized_lowered, gate_weight, preferred_element_type=jnp.float32
    )
    up_projected = jnp.einsum(
        "bld,df->blf", normalized_lowered, up_weight, preferred_element_type=jnp.float32
    )
    middle_state = (gate_projected * jax.nn.sigmoid(gate_projected) * up_projected).astype(
        jnp.bfloat16
    )
    residual_second = normalized_rows + jnp.einsum(
        "blf,fd->bld", middle_state, down_weight, preferred_element_type=jnp.float32
    )
    output, unit_two, scale_two = norm_parts(residual_second, norm_params[2], norm_params[3])
    extra = (all_keys, all_values)
    kept = (
        hidden_state,
        queries,
        key_rows,
        value_rows,
        log_sum,
        attention_output,
        unit_one,
        scale_one,
        gate_projected,
        up_projected,
        unit_two,
        scale_two,
    ) + extra
    return (output, kept)


def layer_backward(incoming, kept, weights_full, seg_rows, seg_keys, cosine, sine_table):
    query_key_value_weight, output_weight, gate_weight, up_weight, down_weight, norm_params = (
        weights_full
    )
    (
        hidden_state,
        queries,
        key_rows,
        value_rows,
        log_sum,
        attention_output,
        unit_one,
        scale_one,
        gate_projected,
        up_projected,
        unit_two,
        scale_two,
    ) = kept[:12]
    all_keys, all_values = (kept[12], kept[13])
    dresid_two, dgain_two, dbias_two = norm_back(incoming, unit_two, scale_two, norm_params[2])
    normalized_lowered = (unit_one * norm_params[0] + norm_params[1]).astype(jnp.bfloat16)
    sigmoid_gate = jax.nn.sigmoid(gate_projected)
    swish_gate = gate_projected * sigmoid_gate
    middle_state = (swish_gate * up_projected).astype(jnp.bfloat16)
    dout_two = dresid_two.astype(jnp.bfloat16)
    grad_down = jnp.einsum(
        "blf,bld->fd", middle_state, dout_two, preferred_element_type=jnp.float32
    )
    dmiddle = jnp.einsum("bld,fd->blf", dout_two, down_weight, preferred_element_type=jnp.float32)
    dgate_proj = (
        dmiddle * up_projected * sigmoid_gate * (1.0 + gate_projected * (1.0 - sigmoid_gate))
    ).astype(jnp.bfloat16)
    dup_proj = (dmiddle * swish_gate).astype(jnp.bfloat16)
    grad_gate = jnp.einsum(
        "bld,blf->df", normalized_lowered, dgate_proj, preferred_element_type=jnp.float32
    )
    grad_up = jnp.einsum(
        "bld,blf->df", normalized_lowered, dup_proj, preferred_element_type=jnp.float32
    )
    dnormed = (
        dresid_two
        + jnp.einsum("blf,df->bld", dgate_proj, gate_weight, preferred_element_type=jnp.float32)
        + jnp.einsum("blf,df->bld", dup_proj, up_weight, preferred_element_type=jnp.float32)
    )
    dresid_one, dgain_one, dbias_one = norm_back(dnormed, unit_one, scale_one, norm_params[0])
    dattn_out = dresid_one.astype(jnp.bfloat16)
    grad_out = jnp.einsum(
        "ble,bld->ed", attention_output, dattn_out, preferred_element_type=jnp.float32
    )
    dattended = jnp.einsum(
        "bld,ed->ble", dattn_out, output_weight, preferred_element_type=jnp.float32
    ).astype(jnp.bfloat16)
    dqueries, dkeys_all, dvalues_all = lax.map(
        attend_back, (queries, all_keys, all_values, seg_rows, seg_keys, log_sum, dattended)
    )
    dkey_rows, dvalue_rows = (
        lax.psum_scatter(
            dkeys_all.astype(jnp.bfloat16), "ctx", scatter_dimension=1, tiled=True
        ).astype(jnp.float32),
        lax.psum_scatter(
            dvalues_all.astype(jnp.bfloat16), "ctx", scatter_dimension=1, tiled=True
        ).astype(jnp.float32),
    )
    shaped = dqueries.shape[:2] + (dqueries.shape[2] // HEAD, HEAD)
    dmixed = jnp.concatenate(
        [
            unrotate(dqueries.reshape(shaped), cosine, sine_table).reshape(dqueries.shape),
            unrotate(dkey_rows.reshape(shaped), cosine, sine_table).reshape(dqueries.shape),
            dvalue_rows,
        ],
        axis=-1,
    ).astype(jnp.bfloat16)
    grad_qkv = jnp.einsum("bld,ble->de", hidden_state, dmixed, preferred_element_type=jnp.float32)
    dhidden = dresid_one + jnp.einsum(
        "ble,de->bld", dmixed, query_key_value_weight, preferred_element_type=jnp.float32
    )
    return (
        dhidden,
        (
            grad_qkv,
            grad_out,
            grad_gate,
            grad_up,
            grad_down,
            jnp.stack([dgain_one, dbias_one, dgain_two, dbias_two]),
        ),
    )


def relay_on_device(
    tokens,
    seg_ids,
    query_key_value_weight,
    output_weight,
    gate_weight,
    up_weight,
    down_weight,
    norm1_gain,
    norm1_bias,
    norm2_gain,
    norm2_bias,
    cotangent,
):
    leading = lax.axis_index("section") == 0
    ctx_rank = lax.axis_index("ctx")
    span_len = tokens.shape[1]
    per_micro = tokens.shape[0] // MICRO
    seg_near = lax.dynamic_slice_in_dim(seg_ids, ctx_rank * span_len, span_len, 1)
    cosine_rows, sine_rows = rope_tables(
        lax.dynamic_slice_in_dim(positions(seg_ids), ctx_rank * span_len, span_len, 1), HEAD // 2
    )
    shards = (
        query_key_value_weight[0],
        output_weight[0],
        gate_weight[0],
        up_weight[0],
        down_weight[0],
        jnp.stack([norm1_gain[0], norm1_bias[0], norm2_gain[0], norm2_bias[0]]),
    )
    gathered = (
        lax.all_gather(shards[0], "dp", axis=0, tiled=True),
        lax.all_gather(shards[1], "dp", axis=0, tiled=True),
        lax.all_gather(shards[2], "dp", axis=0, tiled=True),
        lax.all_gather(shards[3], "dp", axis=0, tiled=True),
        lax.all_gather(shards[4], "dp", axis=0, tiled=True),
        lax.all_gather(shards[5], "dp", axis=1, tiled=True),
    )
    weights_full = gathered[:5] + (gathered[5].astype(jnp.float32),)

    def select(array, micro_idx):
        return lax.dynamic_slice_in_dim(array, micro_idx * per_micro, per_micro, 0)

    delay_fwd = jnp.where(leading, 0, 1)
    received = jnp.zeros((per_micro,) + tokens.shape[1:], jnp.bfloat16)
    outputs = []
    stored = []
    for tick_no in range(MICRO + 1):
        micro_idx = jnp.clip(tick_no - delay_fwd, 0, MICRO - 1)
        hidden_state = jnp.where(leading, select(tokens, micro_idx), received)
        output, kept = layer_forward(
            hidden_state,
            weights_full,
            select(seg_near, micro_idx),
            select(seg_ids, micro_idx),
            select(cosine_rows, micro_idx),
            select(sine_rows, micro_idx),
        )
        sent_rows = output.astype(jnp.bfloat16)
        outputs.append(sent_rows)
        stored.append(kept)
        if tick_no < MICRO:
            received = passed_along(sent_rows, "section", 1)
    gathered = (
        lax.all_gather(shards[0], "dp", axis=0, tiled=True),
        lax.all_gather(shards[1], "dp", axis=0, tiled=True),
        lax.all_gather(shards[2], "dp", axis=0, tiled=True),
        lax.all_gather(shards[3], "dp", axis=0, tiled=True),
        lax.all_gather(shards[4], "dp", axis=0, tiled=True),
        lax.all_gather(shards[5], "dp", axis=1, tiled=True),
    )
    weights_full = gathered[:5] + (gathered[5].astype(jnp.float32),)
    returned = jnp.zeros_like(received)
    totals = None
    input_parts = []
    for tick_no in range(MICRO + 1):
        micro_idx = jnp.clip(tick_no - 1 + delay_fwd, 0, MICRO - 1)
        active = jnp.where(leading, tick_no >= 1, tick_no < MICRO)
        incoming = jnp.where(
            leading, returned.astype(jnp.float32), select(cotangent, micro_idx).astype(jnp.float32)
        )
        incoming = jnp.where(active, incoming, 0.0)
        kept = jax.tree.map(
            lambda early, later: jnp.where(leading, early, later),
            stored[max(tick_no - 1, 0)],
            stored[min(tick_no + 1, MICRO)],
        )
        dhidden, grad_terms = layer_backward(
            incoming,
            kept,
            weights_full,
            select(seg_near, micro_idx),
            select(seg_ids, micro_idx),
            select(cosine_rows, micro_idx),
            select(sine_rows, micro_idx),
        )
        totals = (
            grad_terms
            if totals is None
            else tuple((early + later for early, later in zip(totals, grad_terms)))
        )
        input_parts.append(dhidden)
        if tick_no < MICRO:
            returned = passed_along(dhidden.astype(jnp.bfloat16), "section", -1)
    summed = (
        lax.psum_scatter(
            totals[0].astype(jnp.bfloat16), "dp", scatter_dimension=0, tiled=True
        ).astype(jnp.float32),
        lax.psum_scatter(
            totals[1].astype(jnp.bfloat16), "dp", scatter_dimension=0, tiled=True
        ).astype(jnp.float32),
        lax.psum_scatter(
            totals[2].astype(jnp.bfloat16), "dp", scatter_dimension=0, tiled=True
        ).astype(jnp.float32),
        lax.psum_scatter(
            totals[3].astype(jnp.bfloat16), "dp", scatter_dimension=0, tiled=True
        ).astype(jnp.float32),
        lax.psum_scatter(
            totals[4].astype(jnp.bfloat16), "dp", scatter_dimension=0, tiled=True
        ).astype(jnp.float32),
        lax.psum_scatter(
            totals[5].astype(jnp.bfloat16), "dp", scatter_dimension=1, tiled=True
        ).astype(jnp.float32),
    )
    summed = jax.tree.map(
        lambda part: part.astype(jnp.float32), lax.psum(for_sending(summed), "ctx")
    )
    last_rows = jnp.concatenate(
        [jnp.where(leading, outputs[micro_no], outputs[micro_no + 1]) for micro_no in range(MICRO)],
        axis=0,
    )
    input_grads = jnp.concatenate(
        [
            jnp.where(leading, input_parts[micro_no + 1], input_parts[micro_no])
            for micro_no in range(MICRO)
        ],
        axis=0,
    )
    norm_grads = summed[5]
    return (
        last_rows[None],
        input_grads[None],
        summed[0][None],
        summed[1][None],
        summed[2][None],
        summed[3][None],
        summed[4][None],
        norm_grads[0][None],
        norm_grads[1][None],
        norm_grads[2][None],
        norm_grads[3][None],
    )


NT = (((1,), (1,)), ((), ()))
TN = (((0,), (0,)), ((), ()))


def mm(left, right, dims=(((1,), (0,)), ((), ()))):
    return lax.dot_general(left, right, dims, preferred_element_type=jnp.float32)


def in_vmem():
    return pl.BlockSpec(memory_space=pltpu.VMEM)


def anywhere():
    return pl.BlockSpec(memory_space=pl.ANY)


def in_smem():
    return pl.BlockSpec(memory_space=pltpu.SMEM)


def kernel_call(
    body, out_shapes, in_specs, scratch, mbytes, cost, name, out_specs=None, grid=None, prefetch=False
):
    out_specs = [in_vmem()] * len(out_shapes) if out_specs is None else out_specs
    if prefetch:
        spec = {
            "grid_spec": pltpu.PrefetchScalarGridSpec(
                num_scalar_prefetch=1, grid=grid, in_specs=in_specs, out_specs=out_specs, scratch_shapes=scratch
            )
        }
    else:
        spec = {"in_specs": in_specs, "out_specs": out_specs, "scratch_shapes": scratch}
        if grid is not None:
            spec["grid"] = grid
    return pl.pallas_call(
        body,
        out_shape=out_shapes,
        **spec,
        compiler_params=pltpu.CompilerParams(vmem_limit_bytes=mbytes * 2**20),
        cost_estimate=pl.CostEstimate(flops=0, bytes_accessed=3 * 10**6 * cost, transcendentals=0),
        name=name,
    )


def shape_of(shape, dtype):
    return jax.ShapeDtypeStruct(shape, dtype)


def loads_of(place, pieces, first, width, scratch, sems, begin, blocks=1):
    dp_rank, core = place[0], place[1]
    count = pieces[0].shape[0]
    copies = []
    cuts = ((0, 0, 2, 0, 0, 0), (1, 0, 2, 1, 0, 0), (2, 0, 2, 2, 0, 0), (3, 0, 1, 3, 0, 0), (4, 0, 1, 3, 1, 0))
    cuts += ((5, 0, 2, 0, 0, 1), (6, 0, 2, 1, 0, 1), (6, 2, 2, 2, 0, 1), (7, 0, 2, 3, 0, 1))
    unit = count // 2
    for piece, source, size, flip, target, other in cuts:
        half = 1 - core if other else core
        for block in range(blocks):
            row = ((dp_rank ^ flip) * blocks + block) * count + target * unit
            copies.append(
                pltpu.make_async_copy(
                    pieces[piece].at[pl.ds(source * unit, size * unit), pl.ds(first + block * width, width)],
                    scratch.at[
                        pl.ds(pl.multiple_of(row, unit), size * unit),
                        pl.ds(pl.multiple_of(half * width, 128), width),
                    ],
                    sems.at[begin + len(copies)],
                )
            )
    return copies


def start_loads(*arguments):
    copies = loads_of(*arguments)
    start_all(copies)
    return copies


def start_all(copies):
    for copy in copies:
        copy.start()


def wait_all(copies):
    for copy in copies:
        copy.wait()


def turn(values, cosine, sine):
    lane = lax.broadcasted_iota(jnp.int32, values.shape, 1)
    swapped = jnp.where(
        lane % 64 < 32, pltpu.roll(values, 96, 1), pltpu.roll(values, 32, 1)
    )
    return values * cosine + swapped * sine


def project_rows(place, hidden, cosine, sine, pieces):
    rows, width = hidden[0].shape
    half = 3 * width // 2
    count = len(hidden)

    def body(place_ref, *refs):
        hidden_refs, (cos_ref, sin_ref), refs = refs[:count], refs[count : count + 2], refs[count + 2 :]
        parts, (q_ref, kv_ref, *chosen, weight, sems) = refs[:8], refs[8:]
        loads = start_loads(place_ref, parts, 0, half, weight, sems, 0)
        rows_ref = hidden_refs[0]
        if count == 2:
            rows_ref = chosen[0]
            for index in range(2):
                @pl.when(place_ref[2] == index)
                def _():
                    rows_ref[...] = hidden_refs[index][...]

        wait_all(loads)
        for step in range(3 * width // 256):
            mixed = mm(rows_ref[...], weight[:, step * 256 : step * 256 + 256])
            for pair in range(2):
                column = step * 256 + pair * 128
                part = mixed[:, pair * 128 : pair * 128 + 128]
                which, lane = column // width, column % width
                if which < 2:
                    part = turn(part, cos_ref[...], sin_ref[...])
                if which == 0:
                    q_ref[:, lane : lane + 128] = (
                        part.astype(jnp.bfloat16).astype(jnp.float32) * HEAD**-0.5
                    ).astype(jnp.bfloat16)
                else:
                    kv_ref[which - 1, :, lane : lane + 128] = part.astype(jnp.bfloat16)

    shapes = [shape_of((rows, width), jnp.bfloat16), shape_of((2, rows, width), jnp.bfloat16)]
    return kernel_call(
        body,
        shapes + [shape_of((rows, width), jnp.bfloat16)] * (count - 1),
        [in_smem()] + [in_vmem()] * (count + 2) + [anywhere()] * 8,
        [pltpu.VMEM((width, 3 * width), jnp.bfloat16), pltpu.SemaphoreType.DMA((10,))],
        60,
        3,
        "project_rows",
    )(place, *hidden, cosine, sine, *pieces)


def attend_rows(queries, blocks, seg_column, seg_row):
    rows, width = queries.shape
    keys = 2 * rows

    def body(col_ref, row_ref, q_ref, b0, b1, out_ref, sum_ref, bias, sums):
        step = pl.program_id(0)

        @pl.when(step == 0)
        def _():
            bias[...] = jnp.where(col_ref[...] == row_ref[...], 0.0, NEG)
            sums[...] = jnp.zeros_like(sums)

        lane = lax.broadcasted_iota(jnp.int32, (rows, 128), 1)
        query = q_ref[...]
        key = jnp.concatenate([b[0] for b in (b0, b1)], axis=0)
        value = jnp.concatenate([b[1] for b in (b0, b1)], axis=0)
        results = []
        for head in range(2):
            own = (lane < 64) if head == 0 else (lane >= 64)
            scores = mm(jnp.where(own, query, jnp.zeros_like(query)), key, NT) + bias[...]
            top = jnp.max(scores, axis=1, keepdims=True)
            exponent = jnp.exp(scores - top)
            total = jnp.sum(exponent, axis=1, keepdims=True)
            results.append(mm(exponent.astype(jnp.bfloat16), value) / total)
            sums[...] = jnp.where(lane == 2 * step + head, top + jnp.log(total), sums[...])
        out_ref[...] = jnp.where(lane < 64, results[0], results[1]).astype(jnp.bfloat16)

        @pl.when(step == width // 128 - 1)
        def _():
            sum_ref[...] = sums[...].T

    block = pl.BlockSpec((2, rows, 128), lambda j: (0, 0, j))
    return kernel_call(
        body,
        [shape_of((rows, width), jnp.bfloat16), shape_of((128, rows), jnp.float32)],
        [
            pl.BlockSpec((rows, 1), lambda j: (0, 0)),
            pl.BlockSpec((1, keys), lambda j: (0, 0)),
            pl.BlockSpec((rows, 128), lambda j: (0, j)),
            block, block,
        ],
        [pltpu.VMEM((rows, keys), jnp.float32), pltpu.VMEM((rows, 128), jnp.float32)],
        60,
        8,
        "attend_rows",
        [pl.BlockSpec((rows, 128), lambda j: (0, j)), pl.BlockSpec((128, rows), lambda j: (0, 0))],
        (width // 128,),
    )(seg_column, seg_row, queries, *blocks)


def attend_rows_back(queries, blocks, seg_row, seg_column, attended, sums, incoming):
    rows, width = queries.shape
    keys = 2 * rows

    def body(row_ref, col_ref, sum_ref, q_ref, att_ref, in_ref, b0, b1, dq_ref, own_ref, core_ref, bias):
        step = pl.program_id(0)

        @pl.when(step == 0)
        def _():
            bias[...] = jnp.where(col_ref[...] == row_ref[...], 0.0, NEG)

        lane = lax.broadcasted_iota(jnp.int32, (rows, 128), 1)
        query, given = q_ref[...], in_ref[...]
        key = jnp.concatenate([b[0] for b in (b0, b1)], axis=0)
        value = jnp.concatenate([b[1] for b in (b0, b1)], axis=0)
        key_t = key.T
        inner = (given.astype(jnp.float32) * att_ref[...].astype(jnp.float32)).T
        dkeys, dvalues, dqueries = [], [], []
        for head in range(2):
            own = (lane < 64) if head == 0 else (lane >= 64)
            scores = mm(key, jnp.where(own, query, jnp.zeros_like(query)), NT) + bias[...]
            probs = jnp.exp(scores - sum_ref[pl.ds(2 * step + head, 1), :])
            dvalues.append(mm(probs.astype(jnp.bfloat16), given))
            dprobs = mm(value, jnp.where(own, given, jnp.zeros_like(given)), NT)
            inner_row = jnp.sum(inner[64 * head : 64 * head + 64], axis=0, keepdims=True)
            dscores = (probs * (dprobs - inner_row)).astype(jnp.bfloat16)
            dkeys.append(mm(dscores, query))
            dqueries.append(mm(key_t[64 * head : 64 * head + 64], dscores))
        dq_ref[...] = jnp.concatenate(dqueries, axis=0).T * HEAD**-0.5
        wide = lax.broadcasted_iota(jnp.int32, (keys, 128), 1) < 64
        for which, pair in enumerate((dkeys, dvalues)):
            both = jnp.where(wide, pair[0], pair[1]).astype(jnp.bfloat16)
            own_ref[which] = both[:rows]
            core_ref[which] = both[rows:]

    block = pl.BlockSpec((2, rows, 128), lambda j: (0, 0, j))
    columns = pl.BlockSpec((rows, 128), lambda j: (0, j))
    pair_shape = shape_of((2, rows, width), jnp.bfloat16)
    return kernel_call(
        body,
        [
            shape_of((rows, width), jnp.float32),
            pair_shape,
            pair_shape,
        ],
        [
            pl.BlockSpec((1, rows), lambda j: (0, 0)),
            pl.BlockSpec((keys, 1), lambda j: (0, 0)),
            pl.BlockSpec((128, rows), lambda j: (0, 0)),
            columns, columns, columns, block, block,
        ],
        [pltpu.VMEM((keys, rows), jnp.float32)],
        60,
        18,
        "attend_rows_back",
        [columns, block, block],
        (width // 128,),
    )(seg_row, seg_column, sums, queries, attended, incoming, *blocks)


def unit_of(resid):
    centred = resid - jnp.mean(resid, axis=1, keepdims=True)
    scaling = lax.rsqrt(jnp.mean(centred * centred, axis=1, keepdims=True) + EPS)
    return centred * scaling, scaling


def norm_rows_back(incoming, unit, scaling, gain):
    scaled = incoming * gain
    return scaling * (
        scaled
        - jnp.mean(scaled, axis=1, keepdims=True)
        - unit * jnp.mean(scaled * unit, axis=1, keepdims=True)
    )


FF_STEP = 768


def mlp_scratch(width, hidden_width):
    return [
        pltpu.VMEM((width, width), jnp.bfloat16),
        pltpu.VMEM((width, hidden_width), jnp.bfloat16),
        pltpu.VMEM((width, hidden_width), jnp.bfloat16),
        pltpu.VMEM((hidden_width, width), jnp.bfloat16),
        pltpu.VMEM((width, 256), jnp.bfloat16),
        pltpu.VMEM((128, width), jnp.float32),
        pltpu.SemaphoreType.DMA((80,)),
    ]


def mlp_loads(place_ref, parts, scratch, width, ff_half):
    w_out, w_gate, w_up, w_down, w_norm, _, sems = scratch
    return (
        loads_of(place_ref, parts[:8], 2 * width, 128, w_norm, sems, 70),
        loads_of(place_ref, parts[:8], 3 * width // 2, width // 2, w_out, sems, 0),
        loads_of(place_ref, parts[8:], 0, ff_half, w_gate, sems, 10),
        loads_of(place_ref, parts[8:], ff_half, ff_half, w_up, sems, 20),
        loads_of(place_ref, parts[8:], 2 * ff_half, width // 2, w_down, sems, 30, 4),
    )


MINE = 5


def mlp_blocks(ff):
    steps = ff // FF_STEP
    return steps, lambda j, place: (place[1] ^ (j // (steps // 2))) * (steps // 2) + j % (steps // 2)


def mlp_rows(place, hidden, attended, first_parts, rest_parts, keep_all):
    rows, width = hidden.shape
    ff_half = (rest_parts[0].shape[1] - 2 * width) // 2
    ff = 2 * ff_half
    steps, block_of = mlp_blocks(ff)

    def body(place_ref, hidden_ref, att_ref, *refs):
        parts, rest = refs[:16], refs[16:]
        if keep_all:
            (out_ref, one_ref, two_ref, normed_ref, mid_ref, gate_ref, up_ref), rest = rest[:7], rest[7:]
        else:
            out_ref, rest, (two_ref, normed_ref) = rest[0], rest[1:-2], rest[-2:]
        w_out, w_gate, w_up, w_down, w_norm, norm_ref, _ = rest
        step = pl.program_id(0)
        norm, out, gates, ups, downs = mlp_loads(place_ref, parts, rest, width, ff_half)

        @pl.when(step == 0)
        def _():
            for copies in (norm, out, gates[:MINE], ups[:MINE], downs, gates[MINE:], ups[MINE:]):
                start_all(copies)
            wait_all(norm)
            norm_ref[...] = w_norm[:, :128].astype(jnp.float32).T
            wait_all(out)
            resid = hidden_ref[...].astype(jnp.float32) + mm(att_ref[...], w_out[...])
            if keep_all:
                one_ref[...] = resid
            normed = unit_of(resid)[0] * norm_ref[0:1] + norm_ref[1:2]
            normed_ref[...] = normed.astype(jnp.bfloat16)
            two_ref[...] = normed
            wait_all(gates[:MINE])
            wait_all(ups[:MINE])

        @pl.when(step == steps // 2)
        def _():
            wait_all(gates[MINE:])
            wait_all(ups[MINE:])

        span = pl.ds(pl.multiple_of(block_of(step, place_ref) * FF_STEP, FF_STEP), FF_STEP)
        gate = mm(normed_ref[...], w_gate[:, span])
        up = mm(normed_ref[...], w_up[:, span])
        middle = (gate * jax.nn.sigmoid(gate) * up).astype(jnp.bfloat16)
        if keep_all:
            gate_ref[...], up_ref[...], mid_ref[...] = gate.astype(jnp.bfloat16), up.astype(jnp.bfloat16), middle

        @pl.when(step == 0)
        def _():
            wait_all(downs)

        two_ref[...] += mm(middle, w_down[span, :])

        @pl.when(step == steps - 1)
        def _():
            out_ref[...] = (unit_of(two_ref[...])[0] * norm_ref[2:3] + norm_ref[3:4]).astype(jnp.bfloat16)

    whole = pl.BlockSpec((rows, width), lambda j, place: (0, 0))
    part = pl.BlockSpec((rows, FF_STEP), lambda j, place: (0, block_of(j, place)))
    shapes, scratch = [shape_of((rows, width), jnp.bfloat16)], mlp_scratch(width, ff)
    if keep_all:
        shapes += [shape_of((rows, width), jnp.float32)] * 2 + [shape_of((rows, width), jnp.bfloat16)]
        shapes += [shape_of((rows, ff), jnp.bfloat16)] * 3
    else:
        scratch += [pltpu.VMEM((rows, width), jnp.float32), pltpu.VMEM((rows, width), jnp.bfloat16)]
    return kernel_call(
        body,
        shapes,
        [whole, whole] + [anywhere()] * 16,
        scratch,
        60,
        16,
        "mlp_rows",
        [whole] * 4 + [part] * 3 if keep_all else [whole],
        (steps,),
        True,
    )(place, hidden, attended, *first_parts, *rest_parts)


def mlp_rows_back(place, incoming, one, two, gate, up, first_parts, rest_parts, for_weights):
    rows, width = incoming[0].shape
    ff_half = (rest_parts[0].shape[1] - 2 * width) // 2
    ff = 2 * ff_half
    steps, block_of = mlp_blocks(ff)
    extra = 6 if for_weights else 0

    def body(place_ref, *refs):
        in_refs, refs = refs[: len(incoming)], refs[len(incoming) :]
        (one_ref, two_ref, gate_ref, up_ref), refs = refs[:4], refs[4:]
        parts, outs, rest = refs[:16], refs[16 : 18 + extra], refs[18 + extra :]
        dresid_ref, datt_ref = outs[:2]
        w_out, w_gate, w_up, w_down, w_norm, norm_ref, _, low_ref, sums_ref = rest
        step = pl.program_id(0)
        norm, out, gates, ups, downs = mlp_loads(place_ref, parts, rest[:7], width, ff_half)

        def share(column):
            half = width // 2
            low, first = low_ref[...], place_ref[1] == 0
            for ref, mine in ((outs[2], True), (outs[3], False)):
                ref[:rows, column : column + half] = jnp.where(
                    first == mine, low[:, :half], low[:, half:]
                )

        @pl.when(step == 0)
        def _():
            for copies in (norm, downs, gates[:MINE], ups[:MINE], gates[MINE:], ups[MINE:], out):
                start_all(copies)
            wait_all(norm)
            norm_ref[...] = w_norm[:, :128].astype(jnp.float32).T
            given = in_refs[0][...]
            if len(in_refs) == 2:
                given = jnp.where(place_ref[2] == 0, given, in_refs[1][...])
            given = given.astype(jnp.float32)
            unit, scaling = unit_of(two_ref[...])
            dresid_two = norm_rows_back(given, unit, scaling, norm_ref[2:3])
            dresid_ref[...] = dresid_two
            low_ref[...] = dresid_two.astype(jnp.bfloat16)
            if for_weights:
                sums_ref[...] = jnp.zeros_like(sums_ref)
                sums_ref[2:3] = jnp.sum(given * unit, axis=0, keepdims=True)
                sums_ref[3:4] = jnp.sum(given, axis=0, keepdims=True)
                share(0)
            wait_all(downs)
            wait_all(gates[:MINE])
            wait_all(ups[:MINE])

        @pl.when(step == steps // 2)
        def _():
            wait_all(gates[MINE:])
            wait_all(ups[MINE:])

        span = pl.ds(pl.multiple_of(block_of(step, place_ref) * FF_STEP, FF_STEP), FF_STEP)
        dmiddle = mm(low_ref[...], w_down[span, :], NT)
        gate_block = gate_ref[...].astype(jnp.float32)
        sig = jax.nn.sigmoid(gate_block)
        swish = gate_block * sig
        dup = (dmiddle * swish).astype(jnp.bfloat16)
        dgate = (dmiddle * up_ref[...].astype(jnp.float32) * (sig + swish * (1.0 - sig))).astype(jnp.bfloat16)
        if for_weights:
            @pl.when(step < steps // 2)
            def _():
                outs[4][...], outs[5][...] = dgate, dup

            @pl.when(step >= steps // 2)
            def _():
                outs[6][...], outs[7][...] = dgate, dup

        dresid_ref[...] += mm(dgate, w_gate[:, span], NT) + mm(dup, w_up[:, span], NT)

        @pl.when(step == steps - 1)
        def _():
            wait_all(out)
            dnormed = dresid_ref[...]
            unit, scaling = unit_of(one_ref[...])
            dresid_one = norm_rows_back(dnormed, unit, scaling, norm_ref[0:1])
            dresid_ref[...] = dresid_one
            low_ref[...] = dresid_one.astype(jnp.bfloat16)
            if for_weights:
                sums_ref[0:1] = jnp.sum(dnormed * unit, axis=0, keepdims=True)
                sums_ref[1:2] = jnp.sum(dnormed, axis=0, keepdims=True)
                share(width // 2)
                for ref in outs[2:4]:
                    ref[rows:] = sums_ref[...].astype(jnp.bfloat16)
            datt_ref[...] = mm(low_ref[...], w_out[...], NT).astype(jnp.bfloat16)

    half_steps = steps // 2
    whole = pl.BlockSpec((rows, width), lambda j, place: (0, 0))
    longer = pl.BlockSpec((rows + 16, width), lambda j, place: (0, 0))
    part = pl.BlockSpec((rows, FF_STEP), lambda j, place: (0, block_of(j, place)))
    mine = pl.BlockSpec((rows, FF_STEP), lambda j, place: (0, jnp.minimum(j, half_steps - 1)))
    theirs = pl.BlockSpec((rows, FF_STEP), lambda j, place: (0, jnp.maximum(j - half_steps, 0)))
    shapes = [shape_of((rows, width), jnp.float32), shape_of((rows, width), jnp.bfloat16)]
    specs = [whole, whole]
    if for_weights:
        shapes += [shape_of((rows + 16, width), jnp.bfloat16)] * 2 + [shape_of((rows, ff_half), jnp.bfloat16)] * 4
        specs += [longer] * 2 + [mine] * 2 + [theirs] * 2
    return kernel_call(
        body,
        shapes,
        [whole] * (len(incoming) + 2) + [part, part] + [anywhere()] * 16,
        mlp_scratch(width, ff) + [pltpu.VMEM((rows, width), jnp.bfloat16), pltpu.VMEM((16, width), jnp.float32)],
        60,
        21,
        "mlp_rows_back",
        specs,
        (steps,),
        True,
    )(place, *incoming, one, two, gate, up, *first_parts, *rest_parts)


def project_rows_back(place, dqueries, sums, dresid_one, cosine, sine, pieces):
    rows, width = dqueries.shape
    half = 3 * width // 2
    count = len(sums)

    def body(place_ref, dq_ref, resid_ref, cos_ref, sin_ref, *refs):
        parts, rest = refs[:8], refs[8:]
        sum_refs, (keep_ref, send_ref, dhidden_ref, weight, sems, dmixed_ref) = rest[:count], rest[count:]
        core = place_ref[1]
        loads = start_loads(place_ref, parts, 0, half, weight, sems, 0)
        for column in range(0, 3 * width, 128):
            which, lane = column // width, column % width
            span = slice(lane, lane + 128)
            if which == 0:
                part = dq_ref[:, span]
            else:
                part = sum(ref[which - 1, :, span].astype(jnp.float32) for ref in sum_refs)
            if which < 2:
                part = turn(part, cos_ref[...], -sin_ref[...])
            dmixed_ref[:, column : column + 128] = part.astype(jnp.bfloat16)
        for index in range(2):
            @pl.when(core == index)
            def _():
                keep_ref[...] = dmixed_ref[:, index * half : (index + 1) * half]
                send_ref[...] = dmixed_ref[:, (1 - index) * half : (2 - index) * half]

        wait_all(loads)
        dhidden_ref[...] = (resid_ref[...] + mm(dmixed_ref[...], weight[...], NT)).astype(jnp.bfloat16)

    return kernel_call(
        body,
        [
            shape_of((rows, half), jnp.bfloat16),
            shape_of((rows, half), jnp.bfloat16),
            shape_of((rows, width), jnp.bfloat16),
        ],
        [in_smem()] + [in_vmem()] * 4 + [anywhere()] * 8 + [in_vmem()] * count,
        [
            pltpu.VMEM((width, 3 * width), jnp.bfloat16),
            pltpu.SemaphoreType.DMA((10,)),
            pltpu.VMEM((rows, 3 * width), jnp.bfloat16),
        ],
        60,
        6,
        "project_rows_back",
    )(place, dqueries, dresid_one, cosine, sine, *pieces, *sums)


def grad_parts(place, groups, sums=None):
    jobs = [job for group in groups for job in group]
    rows = jobs[0][0][0].shape[0]
    lefts, rights, arrays = [], [], []
    for left, left_span, right, right_span, blocks in jobs:
        for known, entry in ((lefts, (left, left_span)), (rights, (right, right_span))):
            if not any(entry[0] is other[0] and entry[1] == other[1] for other in known):
                known.append(entry)
        for array in (*left, *right):
            if not any(array is other for other in arrays):
                arrays.append(array)
    where = lambda array: next(i for i, other in enumerate(arrays) if other is array)
    slot = lambda known, pair, span: next(
        i for i, other in enumerate(known) if other[0] is pair and other[1] == span
    )
    count = (jobs[0][1][1] - jobs[0][1][0]) // 4 // jobs[0][4]
    totals = [sum((job[3][1] - job[3][0]) * job[4] for job in group) for group in groups]
    widths = list(totals)
    if sums is not None:
        widths[0] += 128

    def body(place_ref, *refs):
        inputs, refs = refs[: len(arrays)], refs[len(arrays) :]
        outs, refs = refs[: 5 * len(groups)], refs[5 * len(groups) :]
        block, left_refs, right_refs = refs[0], refs[1 : 1 + len(lefts)], refs[1 + len(lefts) :]
        for ref, (pair, span) in zip(left_refs, lefts):
            for core in range(2):
                ref[:, core * rows : (core + 1) * rows] = inputs[where(pair[core])][:rows, span[0] : span[1]].T
        for ref, (pair, span) in zip(right_refs, rights):
            for core in range(2):
                ref[core * rows : (core + 1) * rows] = inputs[where(pair[core])][:rows, span[0] : span[1]]
        if sums is not None:
            padded, turned = refs[-2:]
            padded[...] = jnp.zeros_like(padded)
            padded[:16] = sum(
                inputs[where(array)][rows:, : 4 * count].astype(jnp.float32) for array in jobs[sums][2]
            )
            turned[...] = padded[...].T
        upper, lower = slice(0, count // 2), slice(count // 2, count)
        for index, group in enumerate(groups):
            own_ref, x_ref, y_ref, xl_ref, yu_ref = outs[5 * index : 5 * index + 5]
            end = widths[index]
            for flip in range(4):
                target = 0
                for left, left_span, right, right_span, blocks in group:
                    left_t, right_all = left_refs[slot(lefts, left, left_span)], right_refs[slot(rights, right, right_span)]
                    width = right_span[1] - right_span[0]
                    tile = 512 if width % 512 == 0 else 384
                    for part in range(blocks):
                        begin = ((place_ref[0] ^ flip) * blocks + part) * count
                        rows_t = left_t[pl.ds(pl.multiple_of(begin, count), count), :]
                        for column in range(0, width, tile):
                            block[:, target : target + tile] = mm(
                                rows_t, right_all[:, column : column + tile]
                            ).astype(jnp.bfloat16)
                            target += tile
                if target < end:
                    begin = pl.multiple_of((place_ref[0] ^ flip) * count, count)
                    block[:, target:end] = turned[pl.ds(begin, count), :].astype(jnp.bfloat16)
                if flip == 0:
                    own_ref[...] = block[:, :end]
                elif flip == 1:
                    x_ref[upper] = block[upper, :end]
                    xl_ref[...] = block[lower, :end]
                elif flip == 2:
                    y_ref[upper] = block[lower, :end]
                    yu_ref[...] = block[upper, :end]
                else:
                    x_ref[lower] = block[upper, :end]
                    y_ref[lower] = block[lower, :end]

    scratch = [pltpu.VMEM((count, max(widths)), jnp.bfloat16)]
    scratch += [pltpu.VMEM((span[1] - span[0], 2 * rows), jnp.bfloat16) for _, span in lefts]
    scratch += [pltpu.VMEM((2 * rows, span[1] - span[0]), jnp.bfloat16) for _, span in rights]
    if sums is not None:
        scratch += [pltpu.VMEM((128, 4 * count), jnp.float32), pltpu.VMEM((4 * count, 128), jnp.float32)]
    shapes = []
    for width in widths:
        shapes += [shape_of((count, width), jnp.bfloat16)] * 3 + [shape_of((count // 2, width), jnp.bfloat16)] * 2
    made = kernel_call(
        body, shapes, [in_smem()] + [in_vmem()] * len(arrays), scratch, 60, 7, "grad_parts"
    )(place, *arrays)
    return [made[5 * index : 5 * index + 5] for index in range(len(groups))]


def first_columns(values):
    rows = values.shape[0]

    def body(values_ref, *refs):
        turned = values_ref[...].astype(jnp.float32).T
        for index, ref in enumerate(refs):
            ref[...] = turned[index : index + 1]

    return kernel_call(
        body, [shape_of((1, rows), jnp.float32)] * 4, [in_vmem()], [], 16, 1, "first_columns"
    )(values)


def to_core(value):
    return lax.ppermute(value, "section", [(0, 1), (1, 0)])


def along_x(value):
    return lax.ppermute(value, "dp", [(i, i ^ 1) for i in range(4)])


def along_y(value):
    return lax.ppermute(value, "dp", [(i, i ^ 2) for i in range(4)])


def along_z(value):
    return lax.ppermute(value, "ctx", [(i, i ^ 1) for i in range(4)])


def near_blocks(value):
    pairs = [(i, i ^ 1) for i in range(4)] + [(4 + i, 4 + (i ^ 2)) for i in range(4)]
    return lax.ppermute(value, ("section", "ctx"), pairs)


def far_blocks(value):
    return lax.ppermute(value, ("section", "ctx"), [(4 + i, 4 + (i ^ 3)) for i in range(4)])


def same_role(value):
    return lax.ppermute(value, "ctx", [(i, i ^ 3) for i in range(4)])


def lowered(value):
    return value.astype(jnp.bfloat16)


def wide(value):
    return value.astype(jnp.float32)


def by_core(core, mine, theirs, axis):
    return jnp.where(
        core == 0,
        jnp.concatenate([mine, theirs], axis=axis),
        jnp.concatenate([theirs, mine], axis=axis),
    )


def half_of(array, which):
    width = array.shape[-1] // 2
    return lax.dynamic_slice_in_dim(array, which * width, width, array.ndim - 1)


def after(value, *others):
    return lax.optimization_barrier((value, *others))[0]


def gather_near(piece, *others):
    own = after(piece, *others)
    return [own, along_x(own), along_y(own)]


def gather_far(near, *others):
    rows = near[0].shape[0] // 2
    return [along_x(after(near[2][:rows], *others)), along_y(after(near[1][rows:], *others))]


def both_cores(near, far, other):
    return [
        *near,
        *far,
        other,
        to_core(jnp.concatenate(near[1:3], axis=0)),
        to_core(jnp.concatenate(far, axis=0)),
    ]


def reduce_first(parts, *others):
    return along_x(after(parts[1], *others)), along_y(after(parts[2], *others))


def reduce_second(parts, first, *others):
    _, _, _, x_lower, y_upper = after(tuple(parts), *others)
    from_x, from_y = first
    rows = x_lower.shape[0]
    return (
        along_x(lowered(wide(x_lower) + wide(from_y[rows:]))),
        along_y(lowered(wide(y_upper) + wide(from_x[rows:]))),
    )


def reduce_last(parts, first, second):
    from_x, from_y = first
    rows = second[0].shape[0]
    return lowered(
        wide(parts[0])
        + jnp.concatenate(
            [wide(from_x[:rows]) + wide(second[1]), wide(from_y[:rows]) + wide(second[0])], axis=0
        )
    )


def reduce_ctx(pieces, middle, last):
    received = [same_role(pieces[0]), same_role(pieces[1])]
    mine, others = [], []
    for index, piece in enumerate(pieces):
        mine.append(lowered(wide(piece) + wide(after(received[index], *last))))
        last = (mine[index],)
        others.append(along_z(mine[index]))
        if index + 2 < len(pieces):
            received.append(same_role(after(pieces[index + 2], received[index])))
    sums = [(jnp.where(middle, theirs, own), jnp.where(middle, own, theirs)) for own, theirs in zip(mine, others)]
    return sums, mine[-2]


def paired_on_device(
    tokens,
    seg_ids,
    query_key_value_weight,
    output_weight,
    gate_weight,
    up_weight,
    down_weight,
    norm1_gain,
    norm1_bias,
    norm2_gain,
    norm2_bias,
    cotangent,
):
    core, ctx_rank, dp_rank = (lax.axis_index(a) for a in ("section", "ctx", "dp"))
    span, width = tokens.shape[1], tokens.shape[2]
    sequence = ctx_rank // 2
    middle = (ctx_rank == 1) | (ctx_rank == 2)
    role = jnp.where(middle, 1, 0)
    even = ctx_rank % 2 == 0
    place = jnp.stack([dp_rank, core, role]).astype(jnp.int32)
    pick = lambda array, index: lax.dynamic_index_in_dim(array, index, 0, keepdims=False)

    def in_order(left, right):
        return jnp.where(even, jnp.concatenate([left, right]), jnp.concatenate([right, left]))

    def to_rows(tokens, cotangent, others):
        mine, theirs = jnp.where(middle, cotangent, tokens), jnp.where(middle, tokens, cotangent)
        first = near_blocks(jnp.where(core == 0, pick(theirs, sequence), pick(theirs, 1 - sequence)))
        second = far_blocks(pick(mine, 1 - sequence))
        first, second = after((first, second), *others)
        return in_order(
            jnp.where(core == 0, pick(mine, sequence), first), jnp.where(core == 0, first, second)
        )

    def send_rows(rows):
        halves = rows.reshape(2, span, width)
        left, right = pick(halves, jnp.where(even, 0, 1)), pick(halves, jnp.where(even, 1, 0))
        return left, near_blocks(jnp.where(core == 0, right, left)), far_blocks(right)

    def placed_rows(left, first, second):
        same = jnp.where(core == 0, left, second)
        first_layer, second_layer = jnp.where(middle, first, same), jnp.where(middle, same, first)
        other = to_core(jnp.where(core == 0, second_layer, first_layer))
        mine = jnp.where(core == 0, first_layer, second_layer)
        return jnp.where(
            sequence == core, jnp.stack([mine, other]), jnp.stack([other, mine])
        )[None]

    norm_columns = jnp.concatenate([norm1_gain, norm1_bias, norm2_gain, norm2_bias], axis=0).T
    norm_columns = jnp.pad(norm_columns, ((0, 0), (0, 124)))

    def first_pack(which):
        return jnp.concatenate(
            [half_of(query_key_value_weight[0], which), half_of(output_weight[0], which), norm_columns], axis=1
        )

    def rest_pack(which, *others):
        gate, up, down = after((gate_weight[0], up_weight[0], down_weight[0]), *others)
        return jnp.concatenate(
            [half_of(gate, which), half_of(up, which)]
            + jnp.split(half_of(down, which), down.shape[0] // gate.shape[0]),
            axis=1,
        )

    def halves(own, other, other_sent):
        return jnp.where(core == role, own, other_sent), lambda near: jnp.where(
            core == role, other, to_core(after(own, *near[1:3]))
        )

    own, other = first_pack(core), first_pack(1 - core)
    other_sent = to_core(other)
    first_piece, first_other = halves(own, other, other_sent)
    near = gather_near(first_piece)
    far = gather_far(near)
    own, other = rest_pack(core, other_sent), rest_pack(1 - core, other_sent)
    rest_piece, rest_other = halves(own, other, to_core(other))
    near_mlp = gather_near(rest_piece, *near[1:3])
    given = to_rows(*after((tokens, cotangent), first_piece), far)

    seg = pick(seg_ids, sequence)
    rows = 2 * span
    begin = (sequence ^ core) * rows
    seg_rows = lax.dynamic_slice_in_dim(seg, begin, rows, 0)
    seg_keys = jnp.concatenate([seg_rows, lax.dynamic_slice_in_dim(seg, rows - begin, rows, 0)])
    begins = jnp.sum((seg[None, :] < seg_rows[:, None]).astype(jnp.int32), axis=1)
    places = begin + jnp.arange(rows, dtype=jnp.int32) - begins
    lanes = jnp.arange(128, dtype=jnp.int32) % HEAD
    half = HEAD // 2
    spread = 1000.0 ** (-2.0 * (lanes % half).astype(jnp.float32) / HEAD)
    angles = places.astype(jnp.float32)[:, None] * spread[None, :]
    cosine, sine = jnp.cos(angles), jnp.where(lanes < half, -1.0, 1.0) * jnp.sin(angles)

    def attention(*hidden):
        queries, own, *chosen = project_rows(place, hidden, cosine, sine, first)
        blocks = [own, to_core(own)]
        return *chosen, queries, blocks, *attend_rows(queries, blocks, seg_rows[:, None], seg_keys[None, :])

    first = both_cores(near, far, first_other(near))
    queries, blocks, attended, sums = attention(given)
    near_mlp = [after(part, attended) for part in near_mlp]
    rest = both_cores(near_mlp, gather_far(near_mlp), rest_other(near_mlp))
    output = mlp_rows(place, given, attended, first, rest, False)[0]

    hidden, queries, blocks, attended, sums = attention(given, along_z(output))
    output, one, two, normed, mids, gate, up = mlp_rows(place, hidden, attended, first, rest, True)

    dresid_one, dattended = mlp_rows_back(place, (given,), one, two, gate, up, first, rest, False)
    sent_outputs = send_rows(output)
    dqueries, own, across = attend_rows_back(
        queries, blocks, seg_rows[None, :], seg_keys[:, None], attended, sums, after(dattended, *sent_outputs)
    )
    dhidden = project_rows_back(
        place, dqueries, (own, to_core(across)), dresid_one, cosine, sine, first
    )[2]
    relayed = along_z(dhidden)

    both = lambda value: (value, to_core(value))
    mids, normed, attended, hidden = both(mids), both(normed), both(attended), both(hidden)
    relayed = after(relayed, mids[1], normed[1], attended[1], hidden[1])
    dresid_one, dattended, keep, send, keep_gate, keep_up, send_gate, send_up = mlp_rows_back(
        place, (relayed, given), one, two, gate, up, first, rest, True
    )
    ff = mids[0].shape[1]
    right, right_gate, right_up = (keep, to_core(send)), (keep_gate, to_core(send_gate)), (keep_up, to_core(send_up))
    parts = grad_parts(place, [[(normed, (0, width), right_gate, (0, ff // 2), 1)]])
    near = [reduce_first(parts[0])]
    normed = (after(normed[0], *parts[0]), normed[1])
    parts += grad_parts(place, [[(normed, (0, width), right_up, (0, ff // 2), 1)]])
    near.append(reduce_first(parts[1]))
    dqueries, own, across = attend_rows_back(
        queries, blocks, seg_rows[None, :], seg_keys[:, None], attended[0], sums, after(dattended, *parts[1])
    )
    across = to_core(after(across, *near[0], *near[1]))
    far = [reduce_second(parts[0], near[0], dqueries), reduce_second(parts[1], near[1], dqueries)]
    mids = (after(mids[0], dqueries), mids[1])
    parts += grad_parts(
        place,
        [
            [
                (mids, (0, ff), right, (0, width // 2), ff // width),
                (attended, (0, width), right, (width // 2, width), 1),
            ]
        ],
        1,
    )
    keep, send, dhidden = project_rows_back(
        place, dqueries, (own, across), after(dresid_one, *parts[2], *far[0], *far[1]), cosine, sine, first
    )
    near.append(reduce_first(parts[2], *far[0], *far[1]))
    parts += grad_parts(place, [[(hidden, (0, width), (keep, to_core(send)), (0, 3 * width // 2), 1)]])
    near.append(reduce_first(parts[3]))
    far.append(reduce_second(parts[2], near[2], *parts[3]))
    far.append(reduce_second(parts[3], near[3]))
    pieces = [reduce_last(*group) for group in zip(parts, near, far)]
    totals, nearly = reduce_ctx(pieces, middle, parts[3])
    sent_grads = send_rows(after(dhidden, nearly))

    pairs = []
    for first_layer, second_layer in totals:
        pairs.append(
            (
                jnp.where(core == 0, first_layer, second_layer),
                to_core(jnp.where(core == 0, second_layer, first_layer)),
            )
        )
    joined = lambda index, begin, end: wide(
        by_core(core, pairs[index][0][:, begin:end], pairs[index][1][:, begin:end], 1)
    )[None]
    norm_grads = first_columns(pairs[2][0][:, 5 * width // 2 :])
    pick_down = lambda which: jnp.concatenate(
        [pairs[2][which][:, i * width // 2 : (i + 1) * width // 2] for i in range(ff // width)]
    )
    grad_down = wide(by_core(core, pick_down(0), pick_down(1), 1))[None]

    return (
        placed_rows(*after(sent_outputs, *far[3])),
        wide(placed_rows(*sent_grads)),
        joined(3, 0, 3 * width // 2),
        joined(2, 2 * width, 5 * width // 2),
        joined(0, 0, ff // 2),
        joined(1, 0, ff // 2),
        grad_down,
        *norm_grads,
    )


def solution(mesh):
    placed = (
        P("dp", "ctx", None),
        P("dp", None),
        P("section", "dp", None),
        P("section", "dp", None),
        P("section", "dp", None),
        P("section", "dp", None),
        P("section", "dp", None),
        P("section", "dp"),
        P("section", "dp"),
        P("section", "dp"),
        P("section", "dp"),
        P("dp", "ctx", None),
    )
    paired = mesh.shape["section"] == 2 and mesh.shape["ctx"] == 4 and mesh.shape["dp"] == 4
    return jax.shard_map(
        paired_on_device if paired else relay_on_device,
        mesh=mesh,
        in_specs=placed,
        out_specs=(
            P("section", "dp", "ctx", None),
            P("section", "dp", "ctx", None),
            P("section", "dp", None),
            P("section", "dp", None),
            P("section", "dp", None),
            P("section", "dp", None),
            P("section", "dp", None),
            P("section", "dp"),
            P("section", "dp"),
            P("section", "dp"),
            P("section", "dp"),
        ),
        check_vma=False,
    )
```

```python
import jax
import jax.numpy as jnp
from jax import lax
from jax.experimental import pallas as pl
from jax.experimental.pallas import tpu as pltpu
from jax.sharding import PartitionSpec as P

HEAD = 64
MICRO = 2


EPS = 1e-05
NEG = -1e30


def passed_along(value, axis, steps):
    count = lax.axis_size(axis)
    first, last = (max(0, -steps), min(count, count - steps))
    return lax.ppermute(value, axis, [(source, source + steps) for source in range(first, last)])


def for_sending(array):
    return jax.tree.map(lambda a: a.astype(jnp.bfloat16) if a.dtype == jnp.float32 else a, array)


def positions(seg_ids):
    places = lax.broadcasted_iota(jnp.int32, seg_ids.shape, 1)
    begins = jnp.concatenate(
        [jnp.ones_like(seg_ids[:, :1]), (seg_ids[:, 1:] != seg_ids[:, :-1]).astype(jnp.int32)],
        axis=1,
    )
    return places - lax.cummax(places * begins, axis=1)


def rope_tables(places, half_dim):
    spread = 1000.0 ** (-2.0 * jnp.arange(half_dim, dtype=jnp.float32) / (2 * half_dim))
    angles = places.astype(jnp.float32)[..., None] * spread
    return (jnp.cos(angles), jnp.sin(angles))


def rotate(values, cosine, sine_table):
    half_dim = values.shape[-1] // 2
    former, latter = (values[..., :half_dim], values[..., half_dim:])
    cosine, sine_table = (cosine[..., None, :], sine_table[..., None, :])
    return jnp.concatenate(
        [former * cosine - latter * sine_table, latter * cosine + former * sine_table], axis=-1
    )


def unrotate(values, cosine, sine_table):
    half_dim = values.shape[-1] // 2
    former, latter = (values[..., :half_dim], values[..., half_dim:])
    cosine, sine_table = (cosine[..., None, :], sine_table[..., None, :])
    return jnp.concatenate(
        [former * cosine + latter * sine_table, latter * cosine - former * sine_table], axis=-1
    )


def norm_parts(resid, gain, bias):
    centred = resid - jnp.mean(resid, axis=-1, keepdims=True)
    scaling = lax.rsqrt(jnp.mean(centred * centred, axis=-1, keepdims=True) + EPS)
    unit_rows = centred * scaling
    return (unit_rows * gain + bias, unit_rows, scaling)


def norm_back(incoming, unit_rows, scaling, gain):
    scaled = incoming * gain
    inner = (
        scaled
        - jnp.mean(scaled, axis=-1, keepdims=True)
        - unit_rows * jnp.mean(scaled * unit_rows, axis=-1, keepdims=True)
    )
    return (
        scaling * inner,
        jnp.sum(incoming * unit_rows, axis=(0, 1)),
        jnp.sum(incoming, axis=(0, 1)),
    )


def masked_scores(queries, all_keys, seg_rows, seg_keys):
    row_count, model_width = queries.shape
    head_count = model_width // HEAD
    scores = jnp.einsum(
        "qhd,khd->hqk",
        queries.reshape(row_count, head_count, HEAD),
        all_keys.reshape(all_keys.shape[0], head_count, HEAD),
        preferred_element_type=jnp.float32,
    ) * HEAD ** (-0.5)
    return jnp.where((seg_rows[:, None] == seg_keys[None, :])[None], scores, NEG)


def attend(operands):
    queries, all_keys, all_values, seg_rows, seg_keys = operands
    row_count, model_width = queries.shape
    head_count = model_width // HEAD
    scores = masked_scores(queries, all_keys, seg_rows, seg_keys)
    row_max = jnp.max(scores, axis=-1, keepdims=True)
    exponent = jnp.exp(scores - row_max)
    row_sum = jnp.sum(exponent, axis=-1, keepdims=True)
    probs_low = (exponent / row_sum).astype(jnp.bfloat16)
    result = jnp.einsum(
        "hqk,khd->qhd",
        probs_low,
        all_values.reshape(all_values.shape[0], head_count, HEAD),
        preferred_element_type=jnp.float32,
    )
    return (result.reshape(row_count, model_width), (row_max + jnp.log(row_sum))[..., 0])


def attend_back(operands):
    queries, all_keys, all_values, seg_rows, seg_keys, log_sum, incoming = operands
    row_count, model_width = queries.shape
    head_count = model_width // HEAD
    key_count = all_keys.shape[0]
    probs = jnp.exp(masked_scores(queries, all_keys, seg_rows, seg_keys) - log_sum[..., None])
    heads_in = incoming.reshape(row_count, head_count, HEAD)
    dprobs = jnp.einsum(
        "qhd,khd->hqk",
        heads_in,
        all_values.reshape(key_count, head_count, HEAD),
        preferred_element_type=jnp.float32,
    )
    dscores = (probs * (dprobs - jnp.sum(probs * dprobs, axis=-1, keepdims=True))).astype(
        jnp.bfloat16
    )
    dquery = jnp.einsum(
        "hqk,khd->qhd",
        dscores,
        all_keys.reshape(key_count, head_count, HEAD),
        preferred_element_type=jnp.float32,
    ) * HEAD ** (-0.5)
    dkeys_part = jnp.einsum(
        "hqk,qhd->khd",
        dscores,
        queries.reshape(row_count, head_count, HEAD),
        preferred_element_type=jnp.float32,
    ) * HEAD ** (-0.5)
    dvalue = jnp.einsum(
        "hqk,qhd->khd", probs.astype(jnp.bfloat16), heads_in, preferred_element_type=jnp.float32
    )
    return (
        dquery.reshape(row_count, model_width),
        dkeys_part.reshape(key_count, model_width),
        dvalue.reshape(key_count, model_width),
    )


def layer_forward(hidden_state, weights_full, seg_rows, seg_keys, cosine, sine_table):
    query_key_value_weight, output_weight, gate_weight, up_weight, down_weight, norm_params = (
        weights_full
    )
    model_width = hidden_state.shape[-1]
    shaped = hidden_state.shape[:2] + (model_width // HEAD, HEAD)
    mixed_query_key_value = jnp.einsum(
        "bld,de->ble", hidden_state, query_key_value_weight, preferred_element_type=jnp.float32
    )
    queries = (
        rotate(mixed_query_key_value[..., :model_width].reshape(shaped), cosine, sine_table)
        .reshape(hidden_state.shape)
        .astype(jnp.bfloat16)
    )
    key_rows = (
        rotate(
            mixed_query_key_value[..., model_width : 2 * model_width].reshape(shaped),
            cosine,
            sine_table,
        )
        .reshape(hidden_state.shape)
        .astype(jnp.bfloat16)
    )
    value_rows = mixed_query_key_value[..., 2 * model_width :].astype(jnp.bfloat16)
    all_keys, all_values = (
        lax.all_gather(key_rows, "ctx", axis=1, tiled=True),
        lax.all_gather(value_rows, "ctx", axis=1, tiled=True),
    )
    attention_output, log_sum = lax.map(attend, (queries, all_keys, all_values, seg_rows, seg_keys))
    attention_output = attention_output.astype(jnp.bfloat16)
    residual_first = hidden_state.astype(jnp.float32) + jnp.einsum(
        "bld,de->ble", attention_output, output_weight, preferred_element_type=jnp.float32
    )
    normalized_rows, unit_one, scale_one = norm_parts(
        residual_first, norm_params[0], norm_params[1]
    )
    normalized_lowered = normalized_rows.astype(jnp.bfloat16)
    gate_projected = jnp.einsum(
        "bld,df->blf", normalized_lowered, gate_weight, preferred_element_type=jnp.float32
    )
    up_projected = jnp.einsum(
        "bld,df->blf", normalized_lowered, up_weight, preferred_element_type=jnp.float32
    )
    middle_state = (gate_projected * jax.nn.sigmoid(gate_projected) * up_projected).astype(
        jnp.bfloat16
    )
    residual_second = normalized_rows + jnp.einsum(
        "blf,fd->bld", middle_state, down_weight, preferred_element_type=jnp.float32
    )
    output, unit_two, scale_two = norm_parts(residual_second, norm_params[2], norm_params[3])
    extra = (all_keys, all_values)
    kept = (
        hidden_state,
        queries,
        key_rows,
        value_rows,
        log_sum,
        attention_output,
        unit_one,
        scale_one,
        gate_projected,
        up_projected,
        unit_two,
        scale_two,
    ) + extra
    return (output, kept)


def layer_backward(incoming, kept, weights_full, seg_rows, seg_keys, cosine, sine_table):
    query_key_value_weight, output_weight, gate_weight, up_weight, down_weight, norm_params = (
        weights_full
    )
    (
        hidden_state,
        queries,
        key_rows,
        value_rows,
        log_sum,
        attention_output,
        unit_one,
        scale_one,
        gate_projected,
        up_projected,
        unit_two,
        scale_two,
    ) = kept[:12]
    all_keys, all_values = (kept[12], kept[13])
    dresid_two, dgain_two, dbias_two = norm_back(incoming, unit_two, scale_two, norm_params[2])
    normalized_lowered = (unit_one * norm_params[0] + norm_params[1]).astype(jnp.bfloat16)
    sigmoid_gate = jax.nn.sigmoid(gate_projected)
    swish_gate = gate_projected * sigmoid_gate
    middle_state = (swish_gate * up_projected).astype(jnp.bfloat16)
    dout_two = dresid_two.astype(jnp.bfloat16)
    grad_down = jnp.einsum(
        "blf,bld->fd", middle_state, dout_two, preferred_element_type=jnp.float32
    )
    dmiddle = jnp.einsum("bld,fd->blf", dout_two, down_weight, preferred_element_type=jnp.float32)
    dgate_proj = (
        dmiddle * up_projected * sigmoid_gate * (1.0 + gate_projected * (1.0 - sigmoid_gate))
    ).astype(jnp.bfloat16)
    dup_proj = (dmiddle * swish_gate).astype(jnp.bfloat16)
    grad_gate = jnp.einsum(
        "bld,blf->df", normalized_lowered, dgate_proj, preferred_element_type=jnp.float32
    )
    grad_up = jnp.einsum(
        "bld,blf->df", normalized_lowered, dup_proj, preferred_element_type=jnp.float32
    )
    dnormed = (
        dresid_two
        + jnp.einsum("blf,df->bld", dgate_proj, gate_weight, preferred_element_type=jnp.float32)
        + jnp.einsum("blf,df->bld", dup_proj, up_weight, preferred_element_type=jnp.float32)
    )
    dresid_one, dgain_one, dbias_one = norm_back(dnormed, unit_one, scale_one, norm_params[0])
    dattn_out = dresid_one.astype(jnp.bfloat16)
    grad_out = jnp.einsum(
        "ble,bld->ed", attention_output, dattn_out, preferred_element_type=jnp.float32
    )
    dattended = jnp.einsum(
        "bld,ed->ble", dattn_out, output_weight, preferred_element_type=jnp.float32
    ).astype(jnp.bfloat16)
    dqueries, dkeys_all, dvalues_all = lax.map(
        attend_back, (queries, all_keys, all_values, seg_rows, seg_keys, log_sum, dattended)
    )
    dkey_rows, dvalue_rows = (
        lax.psum_scatter(
            dkeys_all.astype(jnp.bfloat16), "ctx", scatter_dimension=1, tiled=True
        ).astype(jnp.float32),
        lax.psum_scatter(
            dvalues_all.astype(jnp.bfloat16), "ctx", scatter_dimension=1, tiled=True
        ).astype(jnp.float32),
    )
    shaped = dqueries.shape[:2] + (dqueries.shape[2] // HEAD, HEAD)
    dmixed = jnp.concatenate(
        [
            unrotate(dqueries.reshape(shaped), cosine, sine_table).reshape(dqueries.shape),
            unrotate(dkey_rows.reshape(shaped), cosine, sine_table).reshape(dqueries.shape),
            dvalue_rows,
        ],
        axis=-1,
    ).astype(jnp.bfloat16)
    grad_qkv = jnp.einsum("bld,ble->de", hidden_state, dmixed, preferred_element_type=jnp.float32)
    dhidden = dresid_one + jnp.einsum(
        "ble,de->bld", dmixed, query_key_value_weight, preferred_element_type=jnp.float32
    )
    return (
        dhidden,
        (
            grad_qkv,
            grad_out,
            grad_gate,
            grad_up,
            grad_down,
            jnp.stack([dgain_one, dbias_one, dgain_two, dbias_two]),
        ),
    )


def relay_on_device(
    tokens,
    seg_ids,
    query_key_value_weight,
    output_weight,
    gate_weight,
    up_weight,
    down_weight,
    norm1_gain,
    norm1_bias,
    norm2_gain,
    norm2_bias,
    cotangent,
):
    leading = lax.axis_index("section") == 0
    ctx_rank = lax.axis_index("ctx")
    span_len = tokens.shape[1]
    per_micro = tokens.shape[0] // MICRO
    seg_near = lax.dynamic_slice_in_dim(seg_ids, ctx_rank * span_len, span_len, 1)
    cosine_rows, sine_rows = rope_tables(
        lax.dynamic_slice_in_dim(positions(seg_ids), ctx_rank * span_len, span_len, 1), HEAD // 2
    )
    shards = (
        query_key_value_weight[0],
        output_weight[0],
        gate_weight[0],
        up_weight[0],
        down_weight[0],
        jnp.stack([norm1_gain[0], norm1_bias[0], norm2_gain[0], norm2_bias[0]]),
    )
    gathered = (
        lax.all_gather(shards[0], "dp", axis=0, tiled=True),
        lax.all_gather(shards[1], "dp", axis=0, tiled=True),
        lax.all_gather(shards[2], "dp", axis=0, tiled=True),
        lax.all_gather(shards[3], "dp", axis=0, tiled=True),
        lax.all_gather(shards[4], "dp", axis=0, tiled=True),
        lax.all_gather(shards[5], "dp", axis=1, tiled=True),
    )
    weights_full = gathered[:5] + (gathered[5].astype(jnp.float32),)

    def select(array, micro_idx):
        return lax.dynamic_slice_in_dim(array, micro_idx * per_micro, per_micro, 0)

    delay_fwd = jnp.where(leading, 0, 1)
    received = jnp.zeros((per_micro,) + tokens.shape[1:], jnp.bfloat16)
    outputs = []
    stored = []
    for tick_no in range(MICRO + 1):
        micro_idx = jnp.clip(tick_no - delay_fwd, 0, MICRO - 1)
        hidden_state = jnp.where(leading, select(tokens, micro_idx), received)
        output, kept = layer_forward(
            hidden_state,
            weights_full,
            select(seg_near, micro_idx),
            select(seg_ids, micro_idx),
            select(cosine_rows, micro_idx),
            select(sine_rows, micro_idx),
        )
        sent_rows = output.astype(jnp.bfloat16)
        outputs.append(sent_rows)
        stored.append(kept)
        if tick_no < MICRO:
            received = passed_along(sent_rows, "section", 1)
    gathered = (
        lax.all_gather(shards[0], "dp", axis=0, tiled=True),
        lax.all_gather(shards[1], "dp", axis=0, tiled=True),
        lax.all_gather(shards[2], "dp", axis=0, tiled=True),
        lax.all_gather(shards[3], "dp", axis=0, tiled=True),
        lax.all_gather(shards[4], "dp", axis=0, tiled=True),
        lax.all_gather(shards[5], "dp", axis=1, tiled=True),
    )
    weights_full = gathered[:5] + (gathered[5].astype(jnp.float32),)
    returned = jnp.zeros_like(received)
    totals = None
    input_parts = []
    for tick_no in range(MICRO + 1):
        micro_idx = jnp.clip(tick_no - 1 + delay_fwd, 0, MICRO - 1)
        active = jnp.where(leading, tick_no >= 1, tick_no < MICRO)
        incoming = jnp.where(
            leading, returned.astype(jnp.float32), select(cotangent, micro_idx).astype(jnp.float32)
        )
        incoming = jnp.where(active, incoming, 0.0)
        kept = jax.tree.map(
            lambda early, later: jnp.where(leading, early, later),
            stored[max(tick_no - 1, 0)],
            stored[min(tick_no + 1, MICRO)],
        )
        dhidden, grad_terms = layer_backward(
            incoming,
            kept,
            weights_full,
            select(seg_near, micro_idx),
            select(seg_ids, micro_idx),
            select(cosine_rows, micro_idx),
            select(sine_rows, micro_idx),
        )
        totals = (
            grad_terms
            if totals is None
            else tuple((early + later for early, later in zip(totals, grad_terms)))
        )
        input_parts.append(dhidden)
        if tick_no < MICRO:
            returned = passed_along(dhidden.astype(jnp.bfloat16), "section", -1)
    summed = (
        lax.psum_scatter(
            totals[0].astype(jnp.bfloat16), "dp", scatter_dimension=0, tiled=True
        ).astype(jnp.float32),
        lax.psum_scatter(
            totals[1].astype(jnp.bfloat16), "dp", scatter_dimension=0, tiled=True
        ).astype(jnp.float32),
        lax.psum_scatter(
            totals[2].astype(jnp.bfloat16), "dp", scatter_dimension=0, tiled=True
        ).astype(jnp.float32),
        lax.psum_scatter(
            totals[3].astype(jnp.bfloat16), "dp", scatter_dimension=0, tiled=True
        ).astype(jnp.float32),
        lax.psum_scatter(
            totals[4].astype(jnp.bfloat16), "dp", scatter_dimension=0, tiled=True
        ).astype(jnp.float32),
        lax.psum_scatter(
            totals[5].astype(jnp.bfloat16), "dp", scatter_dimension=1, tiled=True
        ).astype(jnp.float32),
    )
    summed = jax.tree.map(
        lambda part: part.astype(jnp.float32), lax.psum(for_sending(summed), "ctx")
    )
    last_rows = jnp.concatenate(
        [jnp.where(leading, outputs[micro_no], outputs[micro_no + 1]) for micro_no in range(MICRO)],
        axis=0,
    )
    input_grads = jnp.concatenate(
        [
            jnp.where(leading, input_parts[micro_no + 1], input_parts[micro_no])
            for micro_no in range(MICRO)
        ],
        axis=0,
    )
    norm_grads = summed[5]
    return (
        last_rows[None],
        input_grads[None],
        summed[0][None],
        summed[1][None],
        summed[2][None],
        summed[3][None],
        summed[4][None],
        norm_grads[0][None],
        norm_grads[1][None],
        norm_grads[2][None],
        norm_grads[3][None],
    )


NT = (((1,), (1,)), ((), ()))
TN = (((0,), (0,)), ((), ()))


def mm(left, right, dims=(((1,), (0,)), ((), ()))):
    return lax.dot_general(left, right, dims, preferred_element_type=jnp.float32)


def in_vmem():
    return pl.BlockSpec(memory_space=pltpu.VMEM)


def anywhere():
    return pl.BlockSpec(memory_space=pl.ANY)


def in_smem():
    return pl.BlockSpec(memory_space=pltpu.SMEM)


def kernel_call(
    body, out_shapes, in_specs, scratch, mbytes, cost, name, out_specs=None, grid=None, prefetch=False
):
    out_specs = [in_vmem()] * len(out_shapes) if out_specs is None else out_specs
    if prefetch:
        spec = {
            "grid_spec": pltpu.PrefetchScalarGridSpec(
                num_scalar_prefetch=1, grid=grid, in_specs=in_specs, out_specs=out_specs, scratch_shapes=scratch
            )
        }
    else:
        spec = {"in_specs": in_specs, "out_specs": out_specs, "scratch_shapes": scratch}
        if grid is not None:
            spec["grid"] = grid
    return pl.pallas_call(
        body,
        out_shape=out_shapes,
        **spec,
        compiler_params=pltpu.CompilerParams(vmem_limit_bytes=mbytes * 2**20),
        cost_estimate=pl.CostEstimate(flops=0, bytes_accessed=3 * 10**6 * cost, transcendentals=0),
        name=name,
    )


def shape_of(shape, dtype):
    return jax.ShapeDtypeStruct(shape, dtype)


def loads_of(place, pieces, first, width, scratch, sems, begin, blocks=1):
    dp_rank, core = place[0], place[1]
    count = pieces[0].shape[0]
    copies = []
    cuts = ((0, 0, 2, 0, 0, 0), (1, 0, 2, 1, 0, 0), (2, 0, 2, 2, 0, 0), (3, 0, 1, 3, 0, 0), (4, 0, 1, 3, 1, 0))
    cuts += ((5, 0, 2, 0, 0, 1), (6, 0, 2, 1, 0, 1), (6, 2, 2, 2, 0, 1), (7, 0, 2, 3, 0, 1))
    unit = count // 2
    for piece, source, size, flip, target, other in cuts:
        half = 1 - core if other else core
        for block in range(blocks):
            row = ((dp_rank ^ flip) * blocks + block) * count + target * unit
            copies.append(
                pltpu.make_async_copy(
                    pieces[piece].at[pl.ds(source * unit, size * unit), pl.ds(first + block * width, width)],
                    scratch.at[
                        pl.ds(pl.multiple_of(row, unit), size * unit),
                        pl.ds(pl.multiple_of(half * width, 128), width),
                    ],
                    sems.at[begin + len(copies)],
                )
            )
    return copies


def start_loads(*arguments):
    copies = loads_of(*arguments)
    start_all(copies)
    return copies


def start_all(copies):
    for copy in copies:
        copy.start()


def wait_all(copies):
    for copy in copies:
        copy.wait()


def turn(values, cosine, sine):
    lane = lax.broadcasted_iota(jnp.int32, values.shape, 1)
    swapped = jnp.where(
        lane % 64 < 32, pltpu.roll(values, 96, 1), pltpu.roll(values, 32, 1)
    )
    return values * cosine + swapped * sine


def project_rows(place, hidden, cosine, sine, pieces):
    rows, width = hidden[0].shape
    half = 3 * width // 2
    count = len(hidden)

    def body(place_ref, *refs):
        hidden_refs, (cos_ref, sin_ref), refs = refs[:count], refs[count : count + 2], refs[count + 2 :]
        parts, (q_ref, kv_ref, *chosen, weight, sems) = refs[:8], refs[8:]
        loads = start_loads(place_ref, parts, 0, half, weight, sems, 0)
        rows_ref = hidden_refs[0]
        if count == 2:
            rows_ref = chosen[0]
            for index in range(2):
                @pl.when(place_ref[2] == index)
                def _():
                    rows_ref[...] = hidden_refs[index][...]

        wait_all(loads)
        for step in range(3 * width // 256):
            mixed = mm(rows_ref[...], weight[:, step * 256 : step * 256 + 256])
            for pair in range(2):
                column = step * 256 + pair * 128
                part = mixed[:, pair * 128 : pair * 128 + 128]
                which, lane = column // width, column % width
                if which < 2:
                    part = turn(part, cos_ref[...], sin_ref[...])
                if which == 0:
                    q_ref[:, lane : lane + 128] = (
                        part.astype(jnp.bfloat16).astype(jnp.float32) * HEAD**-0.5
                    ).astype(jnp.bfloat16)
                else:
                    kv_ref[which - 1, :, lane : lane + 128] = part.astype(jnp.bfloat16)

    shapes = [shape_of((rows, width), jnp.bfloat16), shape_of((2, rows, width), jnp.bfloat16)]
    return kernel_call(
        body,
        shapes + [shape_of((rows, width), jnp.bfloat16)] * (count - 1),
        [in_smem()] + [in_vmem()] * (count + 2) + [anywhere()] * 8,
        [pltpu.VMEM((width, 3 * width), jnp.bfloat16), pltpu.SemaphoreType.DMA((10,))],
        60,
        3,
        "project_rows",
    )(place, *hidden, cosine, sine, *pieces)


def attend_rows(queries, blocks, seg_column, seg_row):
    rows, width = queries.shape
    keys = 2 * rows

    def body(col_ref, row_ref, q_ref, b0, b1, out_ref, sum_ref, bias, sums):
        step = pl.program_id(0)

        @pl.when(step == 0)
        def _():
            bias[...] = jnp.where(col_ref[...] == row_ref[...], 0.0, NEG)
            sums[...] = jnp.zeros_like(sums)

        lane = lax.broadcasted_iota(jnp.int32, (rows, 128), 1)
        query = q_ref[...]
        key = jnp.concatenate([b[0] for b in (b0, b1)], axis=0)
        value = jnp.concatenate([b[1] for b in (b0, b1)], axis=0)
        results = []
        for head in range(2):
            own = (lane < 64) if head == 0 else (lane >= 64)
            scores = mm(jnp.where(own, query, jnp.zeros_like(query)), key, NT) + bias[...]
            top = jnp.max(scores, axis=1, keepdims=True)
            exponent = jnp.exp(scores - top)
            total = jnp.sum(exponent, axis=1, keepdims=True)
            results.append(mm(exponent.astype(jnp.bfloat16), value) / total)
            sums[...] = jnp.where(lane == 2 * step + head, top + jnp.log(total), sums[...])
        out_ref[...] = jnp.where(lane < 64, results[0], results[1]).astype(jnp.bfloat16)

        @pl.when(step == width // 128 - 1)
        def _():
            sum_ref[...] = sums[...].T

    block = pl.BlockSpec((2, rows, 128), lambda j: (0, 0, j))
    return kernel_call(
        body,
        [shape_of((rows, width), jnp.bfloat16), shape_of((128, rows), jnp.float32)],
        [
            pl.BlockSpec((rows, 1), lambda j: (0, 0)),
            pl.BlockSpec((1, keys), lambda j: (0, 0)),
            pl.BlockSpec((rows, 128), lambda j: (0, j)),
            block, block,
        ],
        [pltpu.VMEM((rows, keys), jnp.float32), pltpu.VMEM((rows, 128), jnp.float32)],
        60,
        8,
        "attend_rows",
        [pl.BlockSpec((rows, 128), lambda j: (0, j)), pl.BlockSpec((128, rows), lambda j: (0, 0))],
        (width // 128,),
    )(seg_column, seg_row, queries, *blocks)


def attend_rows_back(queries, blocks, seg_row, seg_column, attended, sums, incoming):
    rows, width = queries.shape
    keys = 2 * rows

    def body(row_ref, col_ref, sum_ref, q_ref, att_ref, in_ref, b0, b1, dq_ref, own_ref, core_ref, bias):
        step = pl.program_id(0)

        @pl.when(step == 0)
        def _():
            bias[...] = jnp.where(col_ref[...] == row_ref[...], 0.0, NEG)

        lane = lax.broadcasted_iota(jnp.int32, (rows, 128), 1)
        query, given = q_ref[...], in_ref[...]
        key = jnp.concatenate([b[0] for b in (b0, b1)], axis=0)
        value = jnp.concatenate([b[1] for b in (b0, b1)], axis=0)
        key_t = key.T
        inner = (given.astype(jnp.float32) * att_ref[...].astype(jnp.float32)).T
        dkeys, dvalues, dqueries = [], [], []
        for head in range(2):
            own = (lane < 64) if head == 0 else (lane >= 64)
            scores = mm(key, jnp.where(own, query, jnp.zeros_like(query)), NT) + bias[...]
            probs = jnp.exp(scores - sum_ref[pl.ds(2 * step + head, 1), :])
            dvalues.append(mm(probs.astype(jnp.bfloat16), given))
            dprobs = mm(value, jnp.where(own, given, jnp.zeros_like(given)), NT)
            inner_row = jnp.sum(inner[64 * head : 64 * head + 64], axis=0, keepdims=True)
            dscores = (probs * (dprobs - inner_row)).astype(jnp.bfloat16)
            dkeys.append(mm(dscores, query))
            dqueries.append(mm(key_t[64 * head : 64 * head + 64], dscores))
        dq_ref[...] = jnp.concatenate(dqueries, axis=0).T * HEAD**-0.5
        wide = lax.broadcasted_iota(jnp.int32, (keys, 128), 1) < 64
        for which, pair in enumerate((dkeys, dvalues)):
            both = jnp.where(wide, pair[0], pair[1]).astype(jnp.bfloat16)
            own_ref[which] = both[:rows]
            core_ref[which] = both[rows:]

    block = pl.BlockSpec((2, rows, 128), lambda j: (0, 0, j))
    columns = pl.BlockSpec((rows, 128), lambda j: (0, j))
    pair_shape = shape_of((2, rows, width), jnp.bfloat16)
    return kernel_call(
        body,
        [
            shape_of((rows, width), jnp.float32),
            pair_shape,
            pair_shape,
        ],
        [
            pl.BlockSpec((1, rows), lambda j: (0, 0)),
            pl.BlockSpec((keys, 1), lambda j: (0, 0)),
            pl.BlockSpec((128, rows), lambda j: (0, 0)),
            columns, columns, columns, block, block,
        ],
        [pltpu.VMEM((keys, rows), jnp.float32)],
        60,
        18,
        "attend_rows_back",
        [columns, block, block],
        (width // 128,),
    )(seg_row, seg_column, sums, queries, attended, incoming, *blocks)


def unit_of(resid):
    centred = resid - jnp.mean(resid, axis=1, keepdims=True)
    scaling = lax.rsqrt(jnp.mean(centred * centred, axis=1, keepdims=True) + EPS)
    return centred * scaling, scaling


def norm_rows_back(incoming, unit, scaling, gain):
    scaled = incoming * gain
    return scaling * (
        scaled
        - jnp.mean(scaled, axis=1, keepdims=True)
        - unit * jnp.mean(scaled * unit, axis=1, keepdims=True)
    )


FF_STEP = 768


def mlp_scratch(width, hidden_width):
    return [
        pltpu.VMEM((width, width), jnp.bfloat16),
        pltpu.VMEM((width, hidden_width), jnp.bfloat16),
        pltpu.VMEM((width, hidden_width), jnp.bfloat16),
        pltpu.VMEM((hidden_width, width), jnp.bfloat16),
        pltpu.VMEM((width, 256), jnp.bfloat16),
        pltpu.VMEM((128, width), jnp.float32),
        pltpu.SemaphoreType.DMA((80,)),
    ]


def mlp_loads(place_ref, parts, scratch, width, ff_half):
    w_out, w_gate, w_up, w_down, w_norm, _, sems = scratch
    return (
        loads_of(place_ref, parts[:8], 2 * width, 128, w_norm, sems, 70),
        loads_of(place_ref, parts[:8], 3 * width // 2, width // 2, w_out, sems, 0),
        loads_of(place_ref, parts[8:], 0, ff_half, w_gate, sems, 10),
        loads_of(place_ref, parts[8:], ff_half, ff_half, w_up, sems, 20),
        loads_of(place_ref, parts[8:], 2 * ff_half, width // 2, w_down, sems, 30, 4),
    )


MINE = 5


def mlp_blocks(ff):
    steps = ff // FF_STEP
    return steps, lambda j, place: (place[1] ^ (j // (steps // 2))) * (steps // 2) + j % (steps // 2)


def mlp_rows(place, hidden, attended, first_parts, rest_parts, keep_all):
    rows, width = hidden.shape
    ff_half = (rest_parts[0].shape[1] - 2 * width) // 2
    ff = 2 * ff_half
    steps, block_of = mlp_blocks(ff)

    def body(place_ref, hidden_ref, att_ref, *refs):
        parts, rest = refs[:16], refs[16:]
        if keep_all:
            (out_ref, one_ref, two_ref, normed_ref, mid_ref, gate_ref, up_ref), rest = rest[:7], rest[7:]
        else:
            out_ref, rest, (two_ref, normed_ref) = rest[0], rest[1:-2], rest[-2:]
        w_out, w_gate, w_up, w_down, w_norm, norm_ref, _ = rest
        step = pl.program_id(0)
        norm, out, gates, ups, downs = mlp_loads(place_ref, parts, rest, width, ff_half)

        @pl.when(step == 0)
        def _():
            for copies in (norm, out, gates[:MINE], ups[:MINE], downs, gates[MINE:], ups[MINE:]):
                start_all(copies)
            wait_all(norm)
            norm_ref[...] = w_norm[:, :128].astype(jnp.float32).T
            wait_all(out)
            resid = hidden_ref[...].astype(jnp.float32) + mm(att_ref[...], w_out[...])
            if keep_all:
                one_ref[...] = resid
            normed = unit_of(resid)[0] * norm_ref[0:1] + norm_ref[1:2]
            normed_ref[...] = normed.astype(jnp.bfloat16)
            two_ref[...] = normed
            wait_all(gates[:MINE])
            wait_all(ups[:MINE])

        @pl.when(step == steps // 2)
        def _():
            wait_all(gates[MINE:])
            wait_all(ups[MINE:])

        span = pl.ds(pl.multiple_of(block_of(step, place_ref) * FF_STEP, FF_STEP), FF_STEP)
        gate = mm(normed_ref[...], w_gate[:, span])
        up = mm(normed_ref[...], w_up[:, span])
        middle = (gate * jax.nn.sigmoid(gate) * up).astype(jnp.bfloat16)
        if keep_all:
            gate_ref[...], up_ref[...], mid_ref[...] = gate.astype(jnp.bfloat16), up.astype(jnp.bfloat16), middle

        @pl.when(step == 0)
        def _():
            wait_all(downs)

        two_ref[...] += mm(middle, w_down[span, :])

        @pl.when(step == steps - 1)
        def _():
            out_ref[...] = (unit_of(two_ref[...])[0] * norm_ref[2:3] + norm_ref[3:4]).astype(jnp.bfloat16)

    whole = pl.BlockSpec((rows, width), lambda j, place: (0, 0))
    part = pl.BlockSpec((rows, FF_STEP), lambda j, place: (0, block_of(j, place)))
    shapes, scratch = [shape_of((rows, width), jnp.bfloat16)], mlp_scratch(width, ff)
    if keep_all:
        shapes += [shape_of((rows, width), jnp.float32)] * 2 + [shape_of((rows, width), jnp.bfloat16)]
        shapes += [shape_of((rows, ff), jnp.bfloat16)] * 3
    else:
        scratch += [pltpu.VMEM((rows, width), jnp.float32), pltpu.VMEM((rows, width), jnp.bfloat16)]
    return kernel_call(
        body,
        shapes,
        [whole, whole] + [anywhere()] * 16,
        scratch,
        60,
        16,
        "mlp_rows",
        [whole] * 4 + [part] * 3 if keep_all else [whole],
        (steps,),
        True,
    )(place, hidden, attended, *first_parts, *rest_parts)


def mlp_rows_back(place, incoming, one, two, gate, up, first_parts, rest_parts, for_weights):
    rows, width = incoming[0].shape
    ff_half = (rest_parts[0].shape[1] - 2 * width) // 2
    ff = 2 * ff_half
    steps, block_of = mlp_blocks(ff)
    extra = 6 if for_weights else 0

    def body(place_ref, *refs):
        in_refs, refs = refs[: len(incoming)], refs[len(incoming) :]
        (one_ref, two_ref, gate_ref, up_ref), refs = refs[:4], refs[4:]
        parts, outs, rest = refs[:16], refs[16 : 18 + extra], refs[18 + extra :]
        dresid_ref, datt_ref = outs[:2]
        w_out, w_gate, w_up, w_down, w_norm, norm_ref, _, low_ref, sums_ref = rest
        step = pl.program_id(0)
        norm, out, gates, ups, downs = mlp_loads(place_ref, parts, rest[:7], width, ff_half)

        def share(column):
            half = width // 2
            low, first = low_ref[...], place_ref[1] == 0
            for ref, mine in ((outs[2], True), (outs[3], False)):
                ref[:rows, column : column + half] = jnp.where(
                    first == mine, low[:, :half], low[:, half:]
                )

        @pl.when(step == 0)
        def _():
            for copies in (norm, downs, gates[:MINE], ups[:MINE], gates[MINE:], ups[MINE:], out):
                start_all(copies)
            wait_all(norm)
            norm_ref[...] = w_norm[:, :128].astype(jnp.float32).T
            given = in_refs[0][...]
            if len(in_refs) == 2:
                given = jnp.where(place_ref[2] == 0, given, in_refs[1][...])
            given = given.astype(jnp.float32)
            unit, scaling = unit_of(two_ref[...])
            dresid_two = norm_rows_back(given, unit, scaling, norm_ref[2:3])
            dresid_ref[...] = dresid_two
            low_ref[...] = dresid_two.astype(jnp.bfloat16)
            if for_weights:
                sums_ref[...] = jnp.zeros_like(sums_ref)
                sums_ref[2:3] = jnp.sum(given * unit, axis=0, keepdims=True)
                sums_ref[3:4] = jnp.sum(given, axis=0, keepdims=True)
                share(0)
            wait_all(downs)
            wait_all(gates[:MINE])
            wait_all(ups[:MINE])

        @pl.when(step == steps // 2)
        def _():
            wait_all(gates[MINE:])
            wait_all(ups[MINE:])

        span = pl.ds(pl.multiple_of(block_of(step, place_ref) * FF_STEP, FF_STEP), FF_STEP)
        dmiddle = mm(low_ref[...], w_down[span, :], NT)
        gate_block = gate_ref[...].astype(jnp.float32)
        sig = jax.nn.sigmoid(gate_block)
        swish = gate_block * sig
        dup = (dmiddle * swish).astype(jnp.bfloat16)
        dgate = (dmiddle * up_ref[...].astype(jnp.float32) * (sig + swish * (1.0 - sig))).astype(jnp.bfloat16)
        if for_weights:
            @pl.when(step < steps // 2)
            def _():
                outs[4][...], outs[5][...] = dgate, dup

            @pl.when(step >= steps // 2)
            def _():
                outs[6][...], outs[7][...] = dgate, dup

        dresid_ref[...] += mm(dgate, w_gate[:, span], NT) + mm(dup, w_up[:, span], NT)

        @pl.when(step == steps - 1)
        def _():
            wait_all(out)
            dnormed = dresid_ref[...]
            unit, scaling = unit_of(one_ref[...])
            dresid_one = norm_rows_back(dnormed, unit, scaling, norm_ref[0:1])
            dresid_ref[...] = dresid_one
            low_ref[...] = dresid_one.astype(jnp.bfloat16)
            if for_weights:
                sums_ref[0:1] = jnp.sum(dnormed * unit, axis=0, keepdims=True)
                sums_ref[1:2] = jnp.sum(dnormed, axis=0, keepdims=True)
                share(width // 2)
                for ref in outs[2:4]:
                    ref[rows:] = sums_ref[...].astype(jnp.bfloat16)
            datt_ref[...] = mm(low_ref[...], w_out[...], NT).astype(jnp.bfloat16)

    half_steps = steps // 2
    whole = pl.BlockSpec((rows, width), lambda j, place: (0, 0))
    longer = pl.BlockSpec((rows + 16, width), lambda j, place: (0, 0))
    part = pl.BlockSpec((rows, FF_STEP), lambda j, place: (0, block_of(j, place)))
    mine = pl.BlockSpec((rows, FF_STEP), lambda j, place: (0, jnp.minimum(j, half_steps - 1)))
    theirs = pl.BlockSpec((rows, FF_STEP), lambda j, place: (0, jnp.maximum(j - half_steps, 0)))
    shapes = [shape_of((rows, width), jnp.float32), shape_of((rows, width), jnp.bfloat16)]
    specs = [whole, whole]
    if for_weights:
        shapes += [shape_of((rows + 16, width), jnp.bfloat16)] * 2 + [shape_of((rows, ff_half), jnp.bfloat16)] * 4
        specs += [longer] * 2 + [mine] * 2 + [theirs] * 2
    return kernel_call(
        body,
        shapes,
        [whole] * (len(incoming) + 2) + [part, part] + [anywhere()] * 16,
        mlp_scratch(width, ff) + [pltpu.VMEM((rows, width), jnp.bfloat16), pltpu.VMEM((16, width), jnp.float32)],
        60,
        21,
        "mlp_rows_back",
        specs,
        (steps,),
        True,
    )(place, *incoming, one, two, gate, up, *first_parts, *rest_parts)


def project_rows_back(place, dqueries, sums, dresid_one, cosine, sine, pieces):
    rows, width = dqueries.shape
    half = 3 * width // 2
    count = len(sums)

    def body(place_ref, dq_ref, resid_ref, cos_ref, sin_ref, *refs):
        parts, rest = refs[:8], refs[8:]
        sum_refs, (keep_ref, send_ref, dhidden_ref, weight, sems, dmixed_ref) = rest[:count], rest[count:]
        core = place_ref[1]
        loads = start_loads(place_ref, parts, 0, half, weight, sems, 0)
        for column in range(0, 3 * width, 128):
            which, lane = column // width, column % width
            span = slice(lane, lane + 128)
            if which == 0:
                part = dq_ref[:, span]
            else:
                part = sum(ref[which - 1, :, span].astype(jnp.float32) for ref in sum_refs)
            if which < 2:
                part = turn(part, cos_ref[...], -sin_ref[...])
            dmixed_ref[:, column : column + 128] = part.astype(jnp.bfloat16)
        for index in range(2):
            @pl.when(core == index)
            def _():
                keep_ref[...] = dmixed_ref[:, index * half : (index + 1) * half]
                send_ref[...] = dmixed_ref[:, (1 - index) * half : (2 - index) * half]

        wait_all(loads)
        dhidden_ref[...] = (resid_ref[...] + mm(dmixed_ref[...], weight[...], NT)).astype(jnp.bfloat16)

    return kernel_call(
        body,
        [
            shape_of((rows, half), jnp.bfloat16),
            shape_of((rows, half), jnp.bfloat16),
            shape_of((rows, width), jnp.bfloat16),
        ],
        [in_smem()] + [in_vmem()] * 4 + [anywhere()] * 8 + [in_vmem()] * count,
        [
            pltpu.VMEM((width, 3 * width), jnp.bfloat16),
            pltpu.SemaphoreType.DMA((10,)),
            pltpu.VMEM((rows, 3 * width), jnp.bfloat16),
        ],
        60,
        6,
        "project_rows_back",
    )(place, dqueries, dresid_one, cosine, sine, *pieces, *sums)


def grad_parts(place, groups, sums=None):
    jobs = [job for group in groups for job in group]
    rows = jobs[0][0][0].shape[0]
    lefts, rights, arrays = [], [], []
    for left, left_span, right, right_span, blocks in jobs:
        for known, entry in ((lefts, (left, left_span)), (rights, (right, right_span))):
            if not any(entry[0] is other[0] and entry[1] == other[1] for other in known):
                known.append(entry)
        for array in (*left, *right):
            if not any(array is other for other in arrays):
                arrays.append(array)
    where = lambda array: next(i for i, other in enumerate(arrays) if other is array)
    slot = lambda known, pair, span: next(
        i for i, other in enumerate(known) if other[0] is pair and other[1] == span
    )
    count = (jobs[0][1][1] - jobs[0][1][0]) // 4 // jobs[0][4]
    totals = [sum((job[3][1] - job[3][0]) * job[4] for job in group) for group in groups]
    widths = list(totals)
    if sums is not None:
        widths[0] += 128

    def body(place_ref, *refs):
        inputs, refs = refs[: len(arrays)], refs[len(arrays) :]
        outs, refs = refs[: 5 * len(groups)], refs[5 * len(groups) :]
        block, left_refs, right_refs = refs[0], refs[1 : 1 + len(lefts)], refs[1 + len(lefts) :]
        for ref, (pair, span) in zip(left_refs, lefts):
            for core in range(2):
                ref[:, core * rows : (core + 1) * rows] = inputs[where(pair[core])][:rows, span[0] : span[1]].T
        for ref, (pair, span) in zip(right_refs, rights):
            for core in range(2):
                ref[core * rows : (core + 1) * rows] = inputs[where(pair[core])][:rows, span[0] : span[1]]
        if sums is not None:
            padded, turned = refs[-2:]
            padded[...] = jnp.zeros_like(padded)
            padded[:16] = sum(
                inputs[where(array)][rows:, : 4 * count].astype(jnp.float32) for array in jobs[sums][2]
            )
            turned[...] = padded[...].T
        upper, lower = slice(0, count // 2), slice(count // 2, count)
        for index, group in enumerate(groups):
            own_ref, x_ref, y_ref, xl_ref, yu_ref = outs[5 * index : 5 * index + 5]
            end = widths[index]
            for flip in range(4):
                target = 0
                for left, left_span, right, right_span, blocks in group:
                    left_t, right_all = left_refs[slot(lefts, left, left_span)], right_refs[slot(rights, right, right_span)]
                    width = right_span[1] - right_span[0]
                    tile = 512 if width % 512 == 0 else 384
                    for part in range(blocks):
                        begin = ((place_ref[0] ^ flip) * blocks + part) * count
                        rows_t = left_t[pl.ds(pl.multiple_of(begin, count), count), :]
                        for column in range(0, width, tile):
                            block[:, target : target + tile] = mm(
                                rows_t, right_all[:, column : column + tile]
                            ).astype(jnp.bfloat16)
                            target += tile
                if target < end:
                    begin = pl.multiple_of((place_ref[0] ^ flip) * count, count)
                    block[:, target:end] = turned[pl.ds(begin, count), :].astype(jnp.bfloat16)
                if flip == 0:
                    own_ref[...] = block[:, :end]
                elif flip == 1:
                    x_ref[upper] = block[upper, :end]
                    xl_ref[...] = block[lower, :end]
                elif flip == 2:
                    y_ref[upper] = block[lower, :end]
                    yu_ref[...] = block[upper, :end]
                else:
                    x_ref[lower] = block[upper, :end]
                    y_ref[lower] = block[lower, :end]

    scratch = [pltpu.VMEM((count, max(widths)), jnp.bfloat16)]
    scratch += [pltpu.VMEM((span[1] - span[0], 2 * rows), jnp.bfloat16) for _, span in lefts]
    scratch += [pltpu.VMEM((2 * rows, span[1] - span[0]), jnp.bfloat16) for _, span in rights]
    if sums is not None:
        scratch += [pltpu.VMEM((128, 4 * count), jnp.float32), pltpu.VMEM((4 * count, 128), jnp.float32)]
    shapes = []
    for width in widths:
        shapes += [shape_of((count, width), jnp.bfloat16)] * 3 + [shape_of((count // 2, width), jnp.bfloat16)] * 2
    made = kernel_call(
        body, shapes, [in_smem()] + [in_vmem()] * len(arrays), scratch, 60, 7, "grad_parts"
    )(place, *arrays)
    return [made[5 * index : 5 * index + 5] for index in range(len(groups))]


def first_columns(values):
    rows = values.shape[0]

    def body(values_ref, *refs):
        turned = values_ref[...].astype(jnp.float32).T
        for index, ref in enumerate(refs):
            ref[...] = turned[index : index + 1]

    return kernel_call(
        body, [shape_of((1, rows), jnp.float32)] * 4, [in_vmem()], [], 16, 1, "first_columns"
    )(values)


def to_core(value):
    return lax.ppermute(value, "section", [(0, 1), (1, 0)])


def along_x(value):
    return lax.ppermute(value, "dp", [(i, i ^ 1) for i in range(4)])


def along_y(value):
    return lax.ppermute(value, "dp", [(i, i ^ 2) for i in range(4)])


def along_z(value):
    return lax.ppermute(value, "ctx", [(i, i ^ 1) for i in range(4)])


def near_blocks(value):
    pairs = [(i, i ^ 1) for i in range(4)] + [(4 + i, 4 + (i ^ 2)) for i in range(4)]
    return lax.ppermute(value, ("section", "ctx"), pairs)


def far_blocks(value):
    return lax.ppermute(value, ("section", "ctx"), [(4 + i, 4 + (i ^ 3)) for i in range(4)])


def same_role(value):
    return lax.ppermute(value, "ctx", [(i, i ^ 3) for i in range(4)])


def lowered(value):
    return value.astype(jnp.bfloat16)


def wide(value):
    return value.astype(jnp.float32)


def by_core(core, mine, theirs, axis):
    return jnp.where(
        core == 0,
        jnp.concatenate([mine, theirs], axis=axis),
        jnp.concatenate([theirs, mine], axis=axis),
    )


def half_of(array, which):
    width = array.shape[-1] // 2
    return lax.dynamic_slice_in_dim(array, which * width, width, array.ndim - 1)


def after(value, *others):
    return lax.optimization_barrier((value, *others))[0]


def gather_near(piece, *others):
    own = after(piece, *others)
    return [own, along_x(own), along_y(own)]


def gather_far(near, *others):
    rows = near[0].shape[0] // 2
    return [along_x(after(near[2][:rows], *others)), along_y(after(near[1][rows:], *others))]


def both_cores(near, far, other):
    return [
        *near,
        *far,
        other,
        to_core(jnp.concatenate(near[1:3], axis=0)),
        to_core(jnp.concatenate(far, axis=0)),
    ]


def reduce_first(parts, *others):
    return along_x(after(parts[1], *others)), along_y(after(parts[2], *others))


def reduce_second(parts, first, *others):
    _, _, _, x_lower, y_upper = after(tuple(parts), *others)
    from_x, from_y = first
    rows = x_lower.shape[0]
    return (
        along_x(lowered(wide(x_lower) + wide(from_y[rows:]))),
        along_y(lowered(wide(y_upper) + wide(from_x[rows:]))),
    )


def reduce_last(parts, first, second):
    from_x, from_y = first
    rows = second[0].shape[0]
    return lowered(
        wide(parts[0])
        + jnp.concatenate(
            [wide(from_x[:rows]) + wide(second[1]), wide(from_y[:rows]) + wide(second[0])], axis=0
        )
    )


def reduce_ctx(pieces, middle, last):
    received = [same_role(pieces[0]), same_role(pieces[1])]
    mine, others = [], []
    for index, piece in enumerate(pieces):
        mine.append(lowered(wide(piece) + wide(after(received[index], *last))))
        last = (mine[index],)
        others.append(along_z(mine[index]))
        if index + 2 < len(pieces):
            received.append(same_role(after(pieces[index + 2], received[index])))
    sums = [(jnp.where(middle, theirs, own), jnp.where(middle, own, theirs)) for own, theirs in zip(mine, others)]
    return sums, mine[-2]


def paired_on_device(
    tokens,
    seg_ids,
    query_key_value_weight,
    output_weight,
    gate_weight,
    up_weight,
    down_weight,
    norm1_gain,
    norm1_bias,
    norm2_gain,
    norm2_bias,
    cotangent,
):
    core, ctx_rank, dp_rank = (lax.axis_index(a) for a in ("section", "ctx", "dp"))
    span, width = tokens.shape[1], tokens.shape[2]
    sequence = ctx_rank // 2
    middle = (ctx_rank == 1) | (ctx_rank == 2)
    role = jnp.where(middle, 1, 0)
    even = ctx_rank % 2 == 0
    place = jnp.stack([dp_rank, core, role]).astype(jnp.int32)
    pick = lambda array, index: lax.dynamic_index_in_dim(array, index, 0, keepdims=False)

    def in_order(left, right):
        return jnp.where(even, jnp.concatenate([left, right]), jnp.concatenate([right, left]))

    def to_rows(tokens, cotangent, others):
        mine, theirs = jnp.where(middle, cotangent, tokens), jnp.where(middle, tokens, cotangent)
        first = near_blocks(jnp.where(core == 0, pick(theirs, sequence), pick(theirs, 1 - sequence)))
        second = far_blocks(pick(mine, 1 - sequence))
        first, second = after((first, second), *others)
        return in_order(
            jnp.where(core == 0, pick(mine, sequence), first), jnp.where(core == 0, first, second)
        )

    def send_rows(rows):
        halves = rows.reshape(2, span, width)
        left, right = pick(halves, jnp.where(even, 0, 1)), pick(halves, jnp.where(even, 1, 0))
        return left, near_blocks(jnp.where(core == 0, right, left)), far_blocks(right)

    def placed_rows(left, first, second):
        same = jnp.where(core == 0, left, second)
        first_layer, second_layer = jnp.where(middle, first, same), jnp.where(middle, same, first)
        other = to_core(jnp.where(core == 0, second_layer, first_layer))
        mine = jnp.where(core == 0, first_layer, second_layer)
        return jnp.where(
            sequence == core, jnp.stack([mine, other]), jnp.stack([other, mine])
        )[None]

    norm_columns = jnp.concatenate([norm1_gain, norm1_bias, norm2_gain, norm2_bias], axis=0).T
    norm_columns = jnp.pad(norm_columns, ((0, 0), (0, 124)))

    def first_pack(which):
        return jnp.concatenate(
            [half_of(query_key_value_weight[0], which), half_of(output_weight[0], which), norm_columns], axis=1
        )

    def rest_pack(which, *others):
        gate, up, down = after((gate_weight[0], up_weight[0], down_weight[0]), *others)
        return jnp.concatenate(
            [half_of(gate, which), half_of(up, which)]
            + jnp.split(half_of(down, which), down.shape[0] // gate.shape[0]),
            axis=1,
        )

    def halves(own, other, other_sent):
        return jnp.where(core == role, own, other_sent), lambda near: jnp.where(
            core == role, other, to_core(after(own, *near[1:3]))
        )

    own, other = first_pack(core), first_pack(1 - core)
    other_sent = to_core(other)
    first_piece, first_other = halves(own, other, other_sent)
    near = gather_near(first_piece)
    far = gather_far(near)
    own, other = rest_pack(core, other_sent), rest_pack(1 - core, other_sent)
    rest_piece, rest_other = halves(own, other, to_core(other))
    near_mlp = gather_near(rest_piece, *near[1:3])
    given = to_rows(*after((tokens, cotangent), first_piece), far)

    seg = pick(seg_ids, sequence)
    rows = 2 * span
    begin = (sequence ^ core) * rows
    seg_rows = lax.dynamic_slice_in_dim(seg, begin, rows, 0)
    seg_keys = jnp.concatenate([seg_rows, lax.dynamic_slice_in_dim(seg, rows - begin, rows, 0)])
    begins = jnp.sum((seg[None, :] < seg_rows[:, None]).astype(jnp.int32), axis=1)
    places = begin + jnp.arange(rows, dtype=jnp.int32) - begins
    lanes = jnp.arange(128, dtype=jnp.int32) % HEAD
    half = HEAD // 2
    spread = 1000.0 ** (-2.0 * (lanes % half).astype(jnp.float32) / HEAD)
    angles = places.astype(jnp.float32)[:, None] * spread[None, :]
    cosine, sine = jnp.cos(angles), jnp.where(lanes < half, -1.0, 1.0) * jnp.sin(angles)

    key_column = seg_keys[:, None]

    def attention(*hidden):
        queries, own, *chosen = project_rows(place, hidden, cosine, sine, first)
        blocks = [own, to_core(own)]
        return *chosen, queries, blocks, *attend_rows(queries, blocks, seg_rows[:, None], seg_keys[None, :])

    first = both_cores(near, far, first_other(near))
    key_column, given = lax.optimization_barrier((key_column, given))
    queries, blocks, attended, sums = attention(given)
    near_mlp = [after(part, attended) for part in near_mlp]
    rest = both_cores(near_mlp, gather_far(near_mlp), rest_other(near_mlp))
    output = mlp_rows(place, given, attended, first, rest, False)[0]

    hidden, queries, blocks, attended, sums = attention(given, along_z(output))
    output, one, two, normed, mids, gate, up = mlp_rows(place, hidden, attended, first, rest, True)

    dresid_one, dattended = mlp_rows_back(place, (given,), one, two, gate, up, first, rest, False)
    sent_outputs = send_rows(output)
    dqueries, own, across = attend_rows_back(
        queries, blocks, seg_rows[None, :], key_column, attended, sums, dattended
    )
    dhidden = project_rows_back(
        place, dqueries, (own, to_core(across)), after(dresid_one, *sent_outputs), cosine, sine, first
    )[2]
    relayed = along_z(dhidden)

    both = lambda value: (value, to_core(value))
    mids, normed, attended, hidden = both(mids), both(normed), both(attended), both(hidden)
    relayed = after(relayed, mids[1], normed[1], attended[1], hidden[1])
    dresid_one, dattended, keep, send, keep_gate, keep_up, send_gate, send_up = mlp_rows_back(
        place, (relayed, given), one, two, gate, up, first, rest, True
    )
    ff = mids[0].shape[1]
    right, right_gate, right_up = (keep, to_core(send)), (keep_gate, to_core(send_gate)), (keep_up, to_core(send_up))
    parts = grad_parts(place, [[(normed, (0, width), right_gate, (0, ff // 2), 1)]])
    near = [reduce_first(parts[0])]
    normed = (after(normed[0], *parts[0]), normed[1])
    parts += grad_parts(place, [[(normed, (0, width), right_up, (0, ff // 2), 1)]])
    near.append(reduce_first(parts[1]))
    dqueries, own, across = attend_rows_back(
        queries, blocks, seg_rows[None, :], key_column, attended[0], sums, after(dattended, *parts[1])
    )
    across = to_core(after(across, *near[0], *near[1]))
    far = [reduce_second(parts[0], near[0], dqueries), reduce_second(parts[1], near[1], dqueries)]
    mids = (after(mids[0], dqueries), mids[1])
    parts += grad_parts(
        place,
        [
            [
                (mids, (0, ff), right, (0, width // 2), ff // width),
                (attended, (0, width), right, (width // 2, width), 1),
            ]
        ],
        1,
    )
    keep, send, dhidden = project_rows_back(
        place, dqueries, (own, across), after(dresid_one, *parts[2], *far[0], *far[1]), cosine, sine, first
    )
    near.append(reduce_first(parts[2], *far[0], *far[1]))
    parts += grad_parts(place, [[(hidden, (0, width), (keep, to_core(send)), (0, 3 * width // 2), 1)]])
    near.append(reduce_first(parts[3]))
    far.append(reduce_second(parts[2], near[2], *parts[3]))
    far.append(reduce_second(parts[3], near[3]))
    pieces = [reduce_last(*group) for group in zip(parts, near, far)]
    totals, nearly = reduce_ctx(pieces, middle, parts[3])
    sent_grads = send_rows(after(dhidden, nearly))

    pairs = []
    for first_layer, second_layer in totals:
        pairs.append(
            (
                jnp.where(core == 0, first_layer, second_layer),
                to_core(jnp.where(core == 0, second_layer, first_layer)),
            )
        )
    joined = lambda index, begin, end: wide(
        by_core(core, pairs[index][0][:, begin:end], pairs[index][1][:, begin:end], 1)
    )[None]
    norm_grads = first_columns(pairs[2][0][:, 5 * width // 2 :])
    pick_down = lambda which: jnp.concatenate(
        [pairs[2][which][:, i * width // 2 : (i + 1) * width // 2] for i in range(ff // width)]
    )
    grad_down = wide(by_core(core, pick_down(0), pick_down(1), 1))[None]

    return (
        placed_rows(*after(sent_outputs, *far[3])),
        wide(placed_rows(*sent_grads)),
        joined(3, 0, 3 * width // 2),
        joined(2, 2 * width, 5 * width // 2),
        joined(0, 0, ff // 2),
        joined(1, 0, ff // 2),
        grad_down,
        *norm_grads,
    )


def solution(mesh):
    placed = (
        P("dp", "ctx", None),
        P("dp", None),
        P("section", "dp", None),
        P("section", "dp", None),
        P("section", "dp", None),
        P("section", "dp", None),
        P("section", "dp", None),
        P("section", "dp"),
        P("section", "dp"),
        P("section", "dp"),
        P("section", "dp"),
        P("dp", "ctx", None),
    )
    paired = mesh.shape["section"] == 2 and mesh.shape["ctx"] == 4 and mesh.shape["dp"] == 4
    return jax.shard_map(
        paired_on_device if paired else relay_on_device,
        mesh=mesh,
        in_specs=placed,
        out_specs=(
            P("section", "dp", "ctx", None),
            P("section", "dp", "ctx", None),
            P("section", "dp", None),
            P("section", "dp", None),
            P("section", "dp", None),
            P("section", "dp", None),
            P("section", "dp", None),
            P("section", "dp"),
            P("section", "dp"),
            P("section", "dp"),
            P("section", "dp"),
        ),
        check_vma=False,
    )
```
